32 devices in a mesh: section: 2 (over core), fsdp: 4 (over z), rep: 4 (over y, x).
Axes of the slice: x: 2, y: 2, z: 4, core: 2. Of those that a mesh axis runs over, the one named last changes fastest.
Arguments:
- tokens: bfloat16 [2, 4, 512, 768], P('section', 'rep', 'fsdp'), may hold values from -6 to 6
- lengths: int32 [2, 4], P(None, 'rep'), may hold values from 256 to 512, as said below
- cotangent: bfloat16 [2, 4, 512, 768], P('section', 'rep', 'fsdp'), may hold values from -6 to 6
- w_qkv: bfloat16 [2, 768, 2304], P('section', 'fsdp'), may hold values from -0.21875 to 0.21875
- w_out: bfloat16 [2, 768, 768], P('section', 'fsdp'), may hold values from -0.875 to 0.875
- norm1_gain: bfloat16 [2, 768], P('section', 'fsdp'), may hold values from 0.5 to 1.5
- norm1_bias: bfloat16 [2, 768], P('section', 'fsdp'), may hold values from -1.75 to 1.75
- w_gate: bfloat16 [2, 768, 3072], P('section', 'fsdp'), may hold values from -0.21875 to 0.21875
- w_up: bfloat16 [2, 768, 3072], P('section', 'fsdp'), may hold values from -0.21875 to 0.21875
- w_down: bfloat16 [2, 3072, 768], P('section', 'fsdp'), may hold values from -0.109375 to 0.109375
- norm2_gain: bfloat16 [2, 768], P('section', 'fsdp'), may hold values from 0.5 to 1.5
- norm2_bias: bfloat16 [2, 768], P('section', 'fsdp'), may hold values from -1.75 to 1.75
Outputs:
- output: bfloat16 [2, 4, 512, 768], P('section', 'rep', 'fsdp')
- token_grad: bfloat16 [2, 4, 512, 768], P('section', 'rep', 'fsdp')
- grad_w_qkv: float32 [2, 768, 2304], P('section', 'fsdp')
- grad_w_out: float32 [2, 768, 768], P('section', 'fsdp')
- grad_norm1_gain: float32 [2, 768], P('section', 'fsdp')
- grad_norm1_bias: float32 [2, 768], P('section', 'fsdp')
- grad_w_gate: float32 [2, 768, 3072], P('section', 'fsdp')
- grad_w_up: float32 [2, 768, 3072], P('section', 'fsdp')
- grad_w_down: float32 [2, 3072, 768], P('section', 'fsdp')
- grad_norm2_gain: float32 [2, 768], P('section', 'fsdp')
- grad_norm2_bias: float32 [2, 768], P('section', 'fsdp')
The draws below stay inside these ranges and needn't reach their ends.
Inputs may be any that keep to these rules, and one draw needn't show every extreme that they name: `lengths`: in every group one of the 2 sequences fills all 512 slots; the others fill half of them or more.
All inputs are finite; a program needn't handle non-finite values.
Results may differ from the reference program's by a relative error of at most 0.02.
Values may be sent and summed in bfloat16 or wider, within the bound.
A program may use at most 320 MiB of HBM per device.

```python
import jax
import jax.numpy as jnp
from jax import lax

D = 768
HEADS = 12
HEAD_DIM = 64
FF = 3072
MICRO = 2
LAYERS = 2
PACK = 512
GROUPS = 4


def draw_lengths(key, part):
    key = jax.random.fold_in(key, 11)
    first_key, second_key, third_key = jax.random.split(key, 3)
    full_batch = jax.random.randint(first_key, (GROUPS,), 0, MICRO)
    others = jax.random.randint(second_key, (MICRO, GROUPS), PACK // 2, PACK + 1)
    shortest_group = jax.random.randint(third_key, (), 0, GROUPS)
    batch_index = jnp.arange(MICRO)[:, None]
    group_index = jnp.arange(GROUPS)[None, :]
    others = jnp.where(group_index == shortest_group, PACK // 2, others)
    return jnp.where(batch_index == full_batch[None, :], PACK, others).astype(jnp.int32)


def levels(stream_key, shape, cuts, low, high):
    gain, own = 1.0, jax.random.fold_in(stream_key, 6)
    for dim, shards_of in cuts:
        steps = jnp.exp(jax.random.uniform(jax.random.fold_in(own, dim), (shards_of,), jnp.float32, low / len(cuts), high / len(cuts)))
        gain = gain * jnp.repeat(steps, shape[dim] // shards_of).reshape([-1 if axis == dim else 1 for axis in range(len(shape))])
    return gain


def scatter_about(stream_key, shape, scale, limit, shards=(), kind=jnp.bfloat16):
    entries = scale * jax.random.normal(stream_key, shape, jnp.float32)
    if shards:
        entries = entries * levels(stream_key, shape, shards, -0.22, 0.18)
    return jnp.clip(entries, -limit, limit).astype(kind)


def setup_inputs(seed: int = 0) -> dict:
    splits = jax.random.split(jax.random.key(seed), 13)
    tokens = scatter_about(splits[0], (MICRO, GROUPS, PACK, D), 1.0, 6.0, ((0, 2), (1, 4), (2, 4)))
    lengths = draw_lengths(jax.random.fold_in(splits[12], 71), 0)
    cotangent = scatter_about(splits[2], (MICRO, GROUPS, PACK, D), 1.0, 6.0, ((0, 2), (1, 4), (2, 4)))
    w_qkv = scatter_about(splits[3], (LAYERS, D, 3 * D), D ** -0.5, 0.21875, ((0, 2), (1, 4)))
    w_out = scatter_about(splits[4], (LAYERS, D, D), (D // 16) ** -0.5, 0.875, ((0, 2), (1, 4)))
    norm1_gain = jnp.clip(1.0 + 0.1 * jax.random.normal(splits[5], (LAYERS, D), jnp.float32), 0.5, 1.5).astype(jnp.bfloat16)
    norm1_bias = scatter_about(splits[6], (LAYERS, D), 0.3, 1.75, ((0, 2), (1, 4)))
    w_gate = scatter_about(splits[7], (LAYERS, D, FF), D ** -0.5, 0.21875, ((0, 2), (1, 4)))
    w_up = scatter_about(splits[8], (LAYERS, D, FF), D ** -0.5, 0.21875, ((0, 2), (1, 4)))
    w_down = scatter_about(splits[9], (LAYERS, FF, D), FF ** -0.5, 0.109375, ((0, 2), (1, 4)))
    norm2_gain = jnp.clip(1.0 + 0.1 * jax.random.normal(splits[10], (LAYERS, D), jnp.float32), 0.5, 1.5).astype(jnp.bfloat16)
    norm2_bias = scatter_about(splits[11], (LAYERS, D), 0.3, 1.75, ((0, 2), (1, 4)))
    return dict(tokens=tokens, lengths=lengths, cotangent=cotangent, w_qkv=w_qkv, w_out=w_out, norm1_gain=norm1_gain, norm1_bias=norm1_bias, w_gate=w_gate, w_up=w_up, w_down=w_down, norm2_gain=norm2_gain, norm2_bias=norm2_bias)


norm_eps = 1e-05
masked_score = -1000000000.0
top_precision = lax.Precision.HIGHEST

@jax.custom_vjp
def low(v):
    return lax.optimization_barrier(v.astype(jnp.bfloat16)).astype(jnp.float32)

@jax.custom_vjp
def low_back(v):
    return v

def low_keep(v):
    return (low(v), None)

def low_pass(kept, grad):
    return (grad,)

def back_keep(v):
    return (v, None)

def back_low(kept, grad):
    return (low(grad),)
low.defvjp(low_keep, low_pass)
low_back.defvjp(back_keep, back_low)

def norm_rows(values, norm_gain, offset):
    centre = values - lax.optimization_barrier(jnp.mean(values, axis=-1, keepdims=True))
    inverse = lax.rsqrt(lax.optimization_barrier(jnp.mean(centre * centre, axis=-1, keepdims=True)) + norm_eps)
    return centre * inverse * norm_gain + offset

def rotary_tables(row_count):
    half_dim = HEAD_DIM // 2
    inverse_freq = 1000.0 ** (-2.0 * jnp.arange(half_dim, dtype=jnp.float32) / HEAD_DIM)
    places = jnp.arange(row_count).astype(jnp.float32)
    angles = places[:, None] * inverse_freq[None, :]
    angles = jnp.concatenate([angles, angles], axis=-1)[:, None, :]
    return (jnp.cos(angles), jnp.sin(angles))

def turn_half(values):
    half_dim = values.shape[-1] // 2
    return jnp.concatenate([-values[..., half_dim:], values[..., :half_dim]], axis=-1)

def rotate(values, cosine_table, sine_table):
    return values * cosine_table + turn_half(values) * sine_table

def layer_apply(inputs, layer_params, live_keys, cosine_table, sine_table):
    w_qkv, w_out, gain_one, offset_one, w_gate, w_up, w_down, gain_two, offset_two = layer_params
    row_count = inputs.shape[0]
    head_shape = (row_count, HEADS, HEAD_DIM)
    joined = low_back(jnp.dot(inputs, w_qkv, precision=top_precision))
    query_part, key_part, value_part = jnp.split(joined, 3, axis=1)
    query_rot = low(rotate(query_part.reshape(head_shape), cosine_table, sine_table))
    key_rot = low(rotate(key_part.reshape(head_shape), cosine_table, sine_table))
    value_heads = low(value_part.reshape(head_shape))
    scores = low_back(jnp.einsum('qhd,khd->hqk', query_rot, key_rot, precision=top_precision) * HEAD_DIM ** (-0.5))
    scores = jnp.where(live_keys[None, None, :], scores, masked_score)
    softmax_weights = low(jax.nn.softmax(scores, axis=-1))
    mixed_heads = jnp.einsum('hqk,khd->qhd', softmax_weights, value_heads, precision=top_precision)
    mixed_heads = low_back(low(mixed_heads.reshape(row_count, HEADS * HEAD_DIM)))
    attended = low_back(jnp.dot(mixed_heads, w_out, precision=top_precision))
    hidden = norm_rows(inputs + attended, gain_one, offset_one)
    hidden_low = low(hidden)
    gate_proj = low_back(jnp.dot(hidden_low, w_gate, precision=top_precision))
    upward = low_back(jnp.dot(hidden_low, w_up, precision=top_precision))
    product = low(jax.nn.silu(gate_proj) * upward)
    mlp_out = low_back(jnp.dot(product, w_down, precision=top_precision))
    return norm_rows(hidden + mlp_out, gain_two, offset_two)

def sequence_out(inputs, length, params):
    slot_count = inputs.shape[0]
    live_keys = jnp.arange(slot_count) < length
    cosine_table, sine_table = rotary_tables(slot_count)
    current = inputs
    for layer_index in range(LAYERS):
        layer_params = tuple((weight_arr[layer_index] for weight_arr in params))
        current = layer_apply(current, layer_params, live_keys, cosine_table, sine_table)
        if layer_index + 1 < LAYERS:
            current = low_back(low(current))
    return low(current)

def model_apply(inputs, lengths, params):
    flat_tokens = inputs.reshape((-1,) + inputs.shape[2:])
    flat_lengths = lengths.reshape(-1)
    per_sequence = jax.checkpoint(lambda sequence_pair: sequence_out(sequence_pair[0], sequence_pair[1], params))
    results = lax.map(per_sequence, (flat_tokens, flat_lengths))
    return results.reshape(inputs.shape)

def reference(tokens, lengths, cotangent, w_qkv, w_out, norm1_gain, norm1_bias, w_gate, w_up, w_down, norm2_gain, norm2_bias):
    params = tuple((weight_arr.astype(jnp.float32) for weight_arr in (w_qkv, w_out, norm1_gain, norm1_bias, w_gate, w_up, w_down, norm2_gain, norm2_bias)))
    inputs = tokens.astype(jnp.float32)

    def forward(inputs_arg, *param_args):
        return model_apply(inputs_arg, lengths, param_args)
    output, pullback = jax.vjp(forward, inputs, *params)
    live = (jnp.arange(PACK)[None, None, :] < lengths[:, :, None]).astype(jnp.float32)
    seed_grad = cotangent.astype(jnp.float32) * live[..., None]
    grads = pullback(seed_grad)
    return (output.astype(jnp.bfloat16), grads[0].astype(jnp.bfloat16), grads[1].astype(jnp.float32), grads[2].astype(jnp.float32), grads[3].astype(jnp.float32), grads[4].astype(jnp.float32), grads[5].astype(jnp.float32), grads[6].astype(jnp.float32), grads[7].astype(jnp.float32), grads[8].astype(jnp.float32), grads[9].astype(jnp.float32))
```

```python
import jax
import jax.numpy as jnp
from jax import lax
from jax.sharding import PartitionSpec as P

HEADS = 12
HEAD_DIM = 64


norm_eps = 1e-05
masked_score = -1000000000.0


def partner(block, axis, distance):
    count = lax.axis_size(axis)
    route = []
    for low in range(count):
        high = low | 1 << distance
        if high != low and high < count:
            route += [(low, high), (high, low)]
    return lax.ppermute(block, axis, route)


def shifted(value, axis, steps):
    count = lax.axis_size(axis)
    initial, last = (max(0, -steps), min(count, count - steps))
    return lax.ppermute(value, axis, [(source, source + steps) for source in range(initial, last)])


def gather_spread(block):
    parts = lax.axis_size("rep")
    size = block.shape[0] // parts
    if block.ndim == 1 or block.shape[0] % parts or size % 16:
        return lax.all_gather(block, "fsdp", axis=0, tiled=True)
    part = lax.dynamic_slice_in_dim(block, lax.axis_index("rep") * size, size, 0)
    return lax.all_gather(part, ("fsdp", "rep"), axis=0, tiled=True)


def sum_spread(total):
    parts = lax.axis_size("rep") * lax.axis_size("fsdp")
    low = total.astype(jnp.bfloat16)
    if total.ndim == 1 or total.shape[0] % parts or total.shape[0] // parts % 16:
        share = lax.psum_scatter(low, "fsdp", scatter_dimension=0, tiled=True)
        return lax.psum(share, "rep").astype(jnp.float32)
    share = lax.psum_scatter(low, ("fsdp", "rep"), scatter_dimension=0, tiled=True)
    return lax.all_gather(share, "rep", axis=0, tiled=True).astype(jnp.float32)


def norm_rows(values, norm_gain, offset):
    centre = values - jnp.mean(values, axis=-1, keepdims=True)
    inverse = lax.rsqrt(jnp.mean(centre * centre, axis=-1, keepdims=True) + norm_eps)
    normed = centre * inverse
    return (normed * norm_gain + offset, normed, inverse)


def norm_back(grad_out, normed, inverse, norm_gain):
    scaled = grad_out * norm_gain
    return inverse * (
        scaled
        - jnp.mean(scaled, axis=-1, keepdims=True)
        - normed * jnp.mean(scaled * normed, axis=-1, keepdims=True)
    )


def rotary_tables(first_slot, row_count):
    half_dim = HEAD_DIM // 2
    inverse_freq = 1000.0 ** (-2.0 * jnp.arange(half_dim, dtype=jnp.float32) / HEAD_DIM)
    places = (first_slot + jnp.arange(row_count)).astype(jnp.float32)
    angles = places[:, None] * inverse_freq[None, :]
    angles = jnp.concatenate([angles, angles], axis=-1)[:, None, :]
    return (jnp.cos(angles), jnp.sin(angles))


def turn_half(values):
    half_dim = values.shape[-1] // 2
    return jnp.concatenate([-values[..., half_dim:], values[..., :half_dim]], axis=-1)


def rotate(values, cosine_table, sine_table):
    return values * cosine_table + turn_half(values) * sine_table


def rotate_back(values, cosine_table, sine_table):
    return values * cosine_table - turn_half(values) * sine_table


def masked_scores(query_rot, key_all, live_keys):
    key_heads = key_all.reshape(key_all.shape[0], HEADS, HEAD_DIM)
    scores = jnp.einsum(
        "qhd,khd->hqk", query_rot, key_heads, preferred_element_type=jnp.float32
    ) * HEAD_DIM ** (-0.5)
    return jnp.where(live_keys[None, None, :], scores, masked_score)


def batch_length(length_column, batch_now):
    picked = jnp.clip(batch_now, 0, length_column.shape[0] - 1)
    return lax.dynamic_index_in_dim(length_column, picked, 0, keepdims=False)


def layer_forward(inputs, weights, live_keys, cosine_table, sine_table):
    w_qkv, w_out, gain_one, offset_one, w_gate, w_up, w_down, gain_two, offset_two = weights
    row_count, model_width = inputs.shape
    head_shape = (row_count, HEADS, HEAD_DIM)
    inputs_low = inputs.astype(jnp.bfloat16)
    joined = jnp.dot(inputs_low, w_qkv, preferred_element_type=jnp.float32)
    query_rot = rotate(
        joined[:, :model_width].reshape(head_shape), cosine_table, sine_table
    ).astype(jnp.bfloat16)
    key_own = (
        rotate(
            joined[:, model_width : 2 * model_width].reshape(head_shape), cosine_table, sine_table
        )
        .reshape(row_count, model_width)
        .astype(jnp.bfloat16)
    )
    value_own = joined[:, 2 * model_width :].astype(jnp.bfloat16)
    key_all, value_all = (
        lax.all_gather(key_own, "fsdp", axis=0, tiled=True),
        lax.all_gather(value_own, "fsdp", axis=0, tiled=True),
    )
    scores = masked_scores(query_rot, key_all, live_keys)
    highest = jnp.max(scores, axis=-1, keepdims=True)
    log_total = highest + jnp.log(jnp.sum(jnp.exp(scores - highest), axis=-1, keepdims=True))
    softmax_weights = jnp.exp(scores - log_total).astype(jnp.bfloat16)
    value_heads = value_all.reshape(value_all.shape[0], HEADS, HEAD_DIM)
    mixed_heads = jnp.einsum(
        "hqk,khd->qhd", softmax_weights, value_heads, preferred_element_type=jnp.float32
    )
    mixed_heads = mixed_heads.reshape(row_count, model_width).astype(jnp.bfloat16)
    attended = jnp.dot(mixed_heads, w_out, preferred_element_type=jnp.float32)
    hidden, normed_one, inverse_one = norm_rows(inputs + attended, gain_one, offset_one)
    hidden_low = hidden.astype(jnp.bfloat16)
    gate_proj = jnp.dot(hidden_low, w_gate, preferred_element_type=jnp.float32)
    upward = jnp.dot(hidden_low, w_up, preferred_element_type=jnp.float32)
    product = (jax.nn.silu(gate_proj) * upward).astype(jnp.bfloat16)
    mlp_out = jnp.dot(product, w_down, preferred_element_type=jnp.float32)
    result, normed_two, inverse_two = norm_rows(hidden + mlp_out, gain_two, offset_two)
    key_saved, value_saved = (key_all, value_all)
    kept_state = (
        inputs_low,
        query_rot,
        key_saved,
        value_saved,
        log_total,
        mixed_heads,
        normed_one,
        inverse_one,
        hidden_low,
        gate_proj,
        upward,
        product,
        normed_two,
        inverse_two,
    )
    return (result, kept_state)


def layer_backward(grad_out, kept_state, weights, live_keys, cosine_table, sine_table):
    w_qkv, w_out, gain_one, offset_one, w_gate, w_up, w_down, gain_two, offset_two = weights
    (
        inputs_low,
        query_rot,
        key_saved,
        value_saved,
        log_total,
        mixed_heads,
        normed_one,
        inverse_one,
        hidden_low,
        gate_proj,
        upward,
        product,
        normed_two,
        inverse_two,
    ) = kept_state
    row_count, model_width = inputs_low.shape
    head_shape = (row_count, HEADS, HEAD_DIM)
    key_all, value_all = (key_saved, value_saved)
    grad_gain_two = jnp.sum(grad_out * normed_two, axis=0)
    grad_offset_two = jnp.sum(grad_out, axis=0)
    grad_second = norm_back(grad_out, normed_two, inverse_two, gain_two)
    grad_fed = grad_second.astype(jnp.bfloat16)
    grad_product = jnp.einsum("rd,fd->rf", grad_fed, w_down, preferred_element_type=jnp.float32)
    grad_w_down = jnp.einsum("rf,rd->fd", product, grad_fed, preferred_element_type=jnp.float32)
    sigmoid_gate = jax.nn.sigmoid(gate_proj)
    silu_gate = gate_proj * sigmoid_gate
    grad_gate = (
        grad_product * upward * sigmoid_gate * (1.0 + gate_proj * (1.0 - sigmoid_gate))
    ).astype(jnp.bfloat16)
    grad_upward = (grad_product * silu_gate).astype(jnp.bfloat16)
    grad_hidden = grad_second + jnp.einsum(
        "rf,df->rd", grad_gate, w_gate, preferred_element_type=jnp.float32
    )
    grad_hidden = grad_hidden + jnp.einsum(
        "rf,df->rd", grad_upward, w_up, preferred_element_type=jnp.float32
    )
    grad_w_gate = jnp.einsum("rd,rf->df", hidden_low, grad_gate, preferred_element_type=jnp.float32)
    grad_w_up = jnp.einsum("rd,rf->df", hidden_low, grad_upward, preferred_element_type=jnp.float32)
    grad_gain_one = jnp.sum(grad_hidden * normed_one, axis=0)
    grad_offset_one = jnp.sum(grad_hidden, axis=0)
    grad_first = norm_back(grad_hidden, normed_one, inverse_one, gain_one)
    grad_attended = grad_first.astype(jnp.bfloat16)
    grad_w_out = jnp.einsum(
        "rd,re->de", mixed_heads, grad_attended, preferred_element_type=jnp.float32
    )
    grad_mixed = (
        jnp.einsum("re,de->rd", grad_attended, w_out, preferred_element_type=jnp.float32)
        .astype(jnp.bfloat16)
        .reshape(head_shape)
    )
    scores = masked_scores(query_rot, key_all, live_keys)
    attention = jnp.exp(scores - log_total)
    key_count = key_all.shape[0]
    key_heads = key_all.reshape(key_count, HEADS, HEAD_DIM)
    value_heads = value_all.reshape(key_count, HEADS, HEAD_DIM)
    grad_attention = jnp.einsum(
        "qhd,khd->hqk", grad_mixed, value_heads, preferred_element_type=jnp.float32
    )
    centre_term = jnp.sum(grad_attention * attention, axis=-1, keepdims=True)
    grad_scores = (attention * (grad_attention - centre_term)).astype(jnp.bfloat16)
    score_scale = HEAD_DIM ** (-0.5)
    grad_query = (
        jnp.einsum("hqk,khd->qhd", grad_scores, key_heads, preferred_element_type=jnp.float32)
        * score_scale
    )
    attention_low = attention.astype(jnp.bfloat16)
    grad_value_all = jnp.einsum(
        "hqk,qhd->khd", attention_low, grad_mixed, preferred_element_type=jnp.float32
    )
    grad_key_all = (
        jnp.einsum("hqk,qhd->khd", grad_scores, query_rot, preferred_element_type=jnp.float32)
        * score_scale
    )
    grad_key, grad_value = (
        lax.psum_scatter(
            grad_key_all.reshape(key_count, model_width).astype(jnp.bfloat16),
            "fsdp",
            scatter_dimension=0,
            tiled=True,
        ).astype(jnp.float32),
        lax.psum_scatter(
            grad_value_all.reshape(key_count, model_width).astype(jnp.bfloat16),
            "fsdp",
            scatter_dimension=0,
            tiled=True,
        ).astype(jnp.float32),
    )
    grad_joined = jnp.concatenate(
        [
            rotate_back(grad_query, cosine_table, sine_table).reshape(row_count, model_width),
            rotate_back(grad_key.reshape(head_shape), cosine_table, sine_table).reshape(
                row_count, model_width
            ),
            grad_value,
        ],
        axis=1,
    ).astype(jnp.bfloat16)
    grad_w_qkv = jnp.einsum(
        "rd,re->de", inputs_low, grad_joined, preferred_element_type=jnp.float32
    )
    grad_inputs = grad_first + jnp.einsum(
        "re,de->rd", grad_joined, w_qkv, preferred_element_type=jnp.float32
    )
    weight_grads = (
        grad_w_qkv,
        grad_w_out,
        grad_gain_one,
        grad_offset_one,
        grad_w_gate,
        grad_w_up,
        grad_w_down,
        grad_gain_two,
        grad_offset_two,
    )
    return (grad_inputs, weight_grads)


def shards(
    tokens,
    lengths,
    cotangent,
    w_qkv,
    w_out,
    norm1_gain,
    norm1_bias,
    w_gate,
    w_up,
    w_down,
    norm2_gain,
    norm2_bias,
):
    section_index = lax.axis_index("section")
    fsdp_index = lax.axis_index("fsdp")
    is_first = section_index == 0
    row_count = tokens.shape[2]
    model_width = tokens.shape[3]
    slot_count = row_count * lax.axis_size("fsdp")
    micro_count = lengths.shape[0]
    weights = tuple(
        gather_spread(value[0])
        for value in (
            w_qkv, w_out, norm1_gain, norm1_bias, w_gate, w_up, w_down, norm2_gain, norm2_bias,
        )
    )
    own_tokens = tokens[0, 0]
    own_cotangent = cotangent[0, 0]
    arrived = partner(jnp.where(is_first, own_cotangent, own_tokens), "section", 0)
    batch_tokens = [
        jnp.where(is_first, own_tokens, arrived),
        jnp.where(is_first, arrived, own_tokens),
    ]
    batch_cotangents = [
        jnp.where(is_first, own_cotangent, arrived),
        jnp.where(is_first, arrived, own_cotangent),
    ]
    cosine_table, sine_table = rotary_tables(fsdp_index * row_count, row_count)
    row_slots = fsdp_index * row_count + jnp.arange(row_count)
    key_slots = jnp.arange(slot_count)
    length_column = lengths[:, 0]
    empty_rows = jnp.zeros((row_count, model_width), jnp.bfloat16)
    carried = empty_rows
    kept_list = []
    layer_outputs = []
    for tick_index in range(micro_count + 1):
        length_now = batch_length(length_column, tick_index - section_index)
        fresh_rows = batch_tokens[tick_index] if tick_index < micro_count else empty_rows
        inputs = jnp.where(is_first, fresh_rows, carried).astype(jnp.float32)
        result, kept_state = layer_forward(
            inputs, weights, key_slots < length_now, cosine_table, sine_table
        )
        result_low = result.astype(jnp.bfloat16)
        kept_list.append(kept_state)
        layer_outputs.append(result_low)
        if tick_index < micro_count:
            carried = shifted(result_low, "section", 1)
    arriving = empty_rows
    totals = None
    owned_total = None
    input_grads = []
    for tick_index in range(micro_count + 1):
        batch_now = tick_index - 1 + section_index
        length_now = batch_length(length_column, batch_now)
        is_valid = (batch_now >= 0) & (batch_now < micro_count)
        seed_rows = batch_cotangents[tick_index] if tick_index < micro_count else empty_rows
        seed_grad = (
            seed_rows.astype(jnp.float32) * (row_slots < length_now).astype(jnp.float32)[:, None]
        )
        grad_out = jnp.where(
            is_valid, jnp.where(is_first, arriving.astype(jnp.float32), seed_grad), 0.0
        )
        earlier_state = kept_list[max(tick_index - 1, 0)]
        later_state = kept_list[min(tick_index + 1, micro_count)]
        kept_state = jax.tree.map(
            lambda first_arr, second_arr: jnp.where(is_first, first_arr, second_arr),
            earlier_state,
            later_state,
        )
        grad_inputs, weight_grads = layer_backward(
            grad_out, kept_state, weights, key_slots < length_now, cosine_table, sine_table
        )
        grad_low = grad_inputs.astype(jnp.bfloat16)
        input_grads.append(grad_low)
        if tick_index < micro_count:
            arriving = shifted(grad_low, "section", -1)
        totals = weight_grads if totals is None else jax.tree.map(jnp.add, totals, weight_grads)
    owned_total = tuple(sum_spread(total) for total in totals)
    outgoing = jnp.where(is_first, input_grads[2], layer_outputs[1])
    returned = partner(outgoing, "section", 0)
    output_rows = jnp.where(is_first, returned, layer_outputs[2])
    grad_rows = jnp.where(is_first, input_grads[1], returned)
    return (
        output_rows[None, None],
        grad_rows[None, None],
        owned_total[0][None],
        owned_total[1][None],
        owned_total[2][None],
        owned_total[3][None],
        owned_total[4][None],
        owned_total[5][None],
        owned_total[6][None],
        owned_total[7][None],
        owned_total[8][None],
    )


def solution(mesh):
    return jax.shard_map(
        shards,
        mesh=mesh,
        in_specs=(
            P("section", "rep", "fsdp", None),
            P(None, "rep"),
            P("section", "rep", "fsdp", None),
            P("section", "fsdp", None),
            P("section", "fsdp", None),
            P("section", "fsdp"),
            P("section", "fsdp"),
            P("section", "fsdp", None),
            P("section", "fsdp", None),
            P("section", "fsdp", None),
            P("section", "fsdp"),
            P("section", "fsdp"),
        ),
        out_specs=(
            P("section", "rep", "fsdp", None),
            P("section", "rep", "fsdp", None),
            P("section", "fsdp", None),
            P("section", "fsdp", None),
            P("section", "fsdp"),
            P("section", "fsdp"),
            P("section", "fsdp", None),
            P("section", "fsdp", None),
            P("section", "fsdp", None),
            P("section", "fsdp"),
            P("section", "fsdp"),
        ),
        check_vma=False,
    )
```

```python
import functools
import types

import jax
import jax.numpy as jnp
from jax import lax
from jax.experimental import pallas as pl
from jax.experimental.pallas import tpu as pltpu
from jax.sharding import PartitionSpec as P

HEADS = 12
HEAD_DIM = 64


norm_eps = 1e-05
masked_score = -1000000000.0
VMEM_LIMIT = 62 * 2**20


def partner(block, axis, distance):
    count = lax.axis_size(axis)
    route = []
    for low in range(count):
        high = low | 1 << distance
        if high != low and high < count:
            route += [(low, high), (high, low)]
    return lax.ppermute(block, axis, route)


def shifted(value, axis, steps):
    count = lax.axis_size(axis)
    initial, last = (max(0, -steps), min(count, count - steps))
    return lax.ppermute(value, axis, [(source, source + steps) for source in range(initial, last)])


def norm_rows(values, norm_gain, offset):
    centre = values - jnp.mean(values, axis=-1, keepdims=True)
    inverse = lax.rsqrt(jnp.mean(centre * centre, axis=-1, keepdims=True) + norm_eps)
    normed = centre * inverse
    return (normed * norm_gain + offset, normed, inverse)


def norm_back(grad_out, normed, inverse, norm_gain):
    scaled = grad_out * norm_gain
    return inverse * (
        scaled
        - jnp.mean(scaled, axis=-1, keepdims=True)
        - normed * jnp.mean(scaled * normed, axis=-1, keepdims=True)
    )


def rotary_tables(first_slot, row_count):
    half_dim = HEAD_DIM // 2
    inverse_freq = 1000.0 ** (-2.0 * jnp.arange(half_dim, dtype=jnp.float32) / HEAD_DIM)
    places = (first_slot + jnp.arange(row_count)).astype(jnp.float32)
    angles = places[:, None] * inverse_freq[None, :]
    angles = jnp.concatenate([angles, angles], axis=-1)[:, None, :]
    return (jnp.cos(angles), jnp.sin(angles))


def turn_half(values):
    half_dim = values.shape[-1] // 2
    return jnp.concatenate([-values[..., half_dim:], values[..., :half_dim]], axis=-1)


def rotate(values, cosine_table, sine_table):
    return values * cosine_table + turn_half(values) * sine_table


def rotate_back(values, cosine_table, sine_table):
    return values * cosine_table - turn_half(values) * sine_table


def masked_scores(query_rot, key_all, live_keys):
    key_heads = key_all.reshape(key_all.shape[0], HEADS, HEAD_DIM)
    scores = jnp.einsum(
        "qhd,khd->hqk", query_rot, key_heads, preferred_element_type=jnp.float32
    ) * HEAD_DIM ** (-0.5)
    return jnp.where(live_keys[None, None, :], scores, masked_score)


def batch_length(length_column, batch_now):
    picked = jnp.clip(batch_now, 0, length_column.shape[0] - 1)
    return lax.dynamic_index_in_dim(length_column, picked, 0, keepdims=False)


def layer_forward(inputs, weights, live_keys, cosine_table, sine_table):
    w_qkv, w_out, gain_one, offset_one, w_gate, w_up, w_down, gain_two, offset_two = weights
    row_count, model_width = inputs.shape
    head_shape = (row_count, HEADS, HEAD_DIM)
    inputs_low = inputs.astype(jnp.bfloat16)
    joined = jnp.dot(inputs_low, w_qkv, preferred_element_type=jnp.float32)
    query_rot = rotate(
        joined[:, :model_width].reshape(head_shape), cosine_table, sine_table
    ).astype(jnp.bfloat16)
    key_own = (
        rotate(
            joined[:, model_width : 2 * model_width].reshape(head_shape), cosine_table, sine_table
        )
        .reshape(row_count, model_width)
        .astype(jnp.bfloat16)
    )
    value_own = joined[:, 2 * model_width :].astype(jnp.bfloat16)
    key_all, value_all = (
        lax.all_gather(key_own, "fsdp", axis=0, tiled=True),
        lax.all_gather(value_own, "fsdp", axis=0, tiled=True),
    )
    scores = masked_scores(query_rot, key_all, live_keys)
    highest = jnp.max(scores, axis=-1, keepdims=True)
    log_total = highest + jnp.log(jnp.sum(jnp.exp(scores - highest), axis=-1, keepdims=True))
    softmax_weights = jnp.exp(scores - log_total).astype(jnp.bfloat16)
    value_heads = value_all.reshape(value_all.shape[0], HEADS, HEAD_DIM)
    mixed_heads = jnp.einsum(
        "hqk,khd->qhd", softmax_weights, value_heads, preferred_element_type=jnp.float32
    )
    mixed_heads = mixed_heads.reshape(row_count, model_width).astype(jnp.bfloat16)
    attended = jnp.dot(mixed_heads, w_out, preferred_element_type=jnp.float32)
    hidden, normed_one, inverse_one = norm_rows(inputs + attended, gain_one, offset_one)
    hidden_low = hidden.astype(jnp.bfloat16)
    gate_proj = jnp.dot(hidden_low, w_gate, preferred_element_type=jnp.float32)
    upward = jnp.dot(hidden_low, w_up, preferred_element_type=jnp.float32)
    product = (jax.nn.silu(gate_proj) * upward).astype(jnp.bfloat16)
    mlp_out = jnp.dot(product, w_down, preferred_element_type=jnp.float32)
    result, normed_two, inverse_two = norm_rows(hidden + mlp_out, gain_two, offset_two)
    key_saved, value_saved = (key_all, value_all)
    kept_state = (
        inputs_low,
        query_rot,
        key_saved,
        value_saved,
        log_total,
        mixed_heads,
        normed_one,
        inverse_one,
        hidden_low,
        gate_proj,
        upward,
        product,
        normed_two,
        inverse_two,
    )
    return (result, kept_state)


def layer_backward(grad_out, kept_state, weights, live_keys, cosine_table, sine_table):
    w_qkv, w_out, gain_one, offset_one, w_gate, w_up, w_down, gain_two, offset_two = weights
    (
        inputs_low,
        query_rot,
        key_saved,
        value_saved,
        log_total,
        mixed_heads,
        normed_one,
        inverse_one,
        hidden_low,
        gate_proj,
        upward,
        product,
        normed_two,
        inverse_two,
    ) = kept_state
    row_count, model_width = inputs_low.shape
    head_shape = (row_count, HEADS, HEAD_DIM)
    key_all, value_all = (key_saved, value_saved)
    grad_gain_two = jnp.sum(grad_out * normed_two, axis=0)
    grad_offset_two = jnp.sum(grad_out, axis=0)
    grad_second = norm_back(grad_out, normed_two, inverse_two, gain_two)
    grad_fed = grad_second.astype(jnp.bfloat16)
    grad_product = jnp.einsum("rd,fd->rf", grad_fed, w_down, preferred_element_type=jnp.float32)
    grad_w_down = jnp.einsum("rf,rd->fd", product, grad_fed, preferred_element_type=jnp.float32)
    sigmoid_gate = jax.nn.sigmoid(gate_proj)
    silu_gate = gate_proj * sigmoid_gate
    grad_gate = (
        grad_product * upward * sigmoid_gate * (1.0 + gate_proj * (1.0 - sigmoid_gate))
    ).astype(jnp.bfloat16)
    grad_upward = (grad_product * silu_gate).astype(jnp.bfloat16)
    grad_hidden = grad_second + jnp.einsum(
        "rf,df->rd", grad_gate, w_gate, preferred_element_type=jnp.float32
    )
    grad_hidden = grad_hidden + jnp.einsum(
        "rf,df->rd", grad_upward, w_up, preferred_element_type=jnp.float32
    )
    grad_w_gate = jnp.einsum("rd,rf->df", hidden_low, grad_gate, preferred_element_type=jnp.float32)
    grad_w_up = jnp.einsum("rd,rf->df", hidden_low, grad_upward, preferred_element_type=jnp.float32)
    grad_gain_one = jnp.sum(grad_hidden * normed_one, axis=0)
    grad_offset_one = jnp.sum(grad_hidden, axis=0)
    grad_first = norm_back(grad_hidden, normed_one, inverse_one, gain_one)
    grad_attended = grad_first.astype(jnp.bfloat16)
    grad_w_out = jnp.einsum(
        "rd,re->de", mixed_heads, grad_attended, preferred_element_type=jnp.float32
    )
    grad_mixed = (
        jnp.einsum("re,de->rd", grad_attended, w_out, preferred_element_type=jnp.float32)
        .astype(jnp.bfloat16)
        .reshape(head_shape)
    )
    scores = masked_scores(query_rot, key_all, live_keys)
    attention = jnp.exp(scores - log_total)
    key_count = key_all.shape[0]
    key_heads = key_all.reshape(key_count, HEADS, HEAD_DIM)
    value_heads = value_all.reshape(key_count, HEADS, HEAD_DIM)
    grad_attention = jnp.einsum(
        "qhd,khd->hqk", grad_mixed, value_heads, preferred_element_type=jnp.float32
    )
    centre_term = jnp.sum(grad_attention * attention, axis=-1, keepdims=True)
    grad_scores = (attention * (grad_attention - centre_term)).astype(jnp.bfloat16)
    score_scale = HEAD_DIM ** (-0.5)
    grad_query = (
        jnp.einsum("hqk,khd->qhd", grad_scores, key_heads, preferred_element_type=jnp.float32)
        * score_scale
    )
    attention_low = attention.astype(jnp.bfloat16)
    grad_value_all = jnp.einsum(
        "hqk,qhd->khd", attention_low, grad_mixed, preferred_element_type=jnp.float32
    )
    grad_key_all = (
        jnp.einsum("hqk,qhd->khd", grad_scores, query_rot, preferred_element_type=jnp.float32)
        * score_scale
    )
    grad_key, grad_value = (
        lax.psum_scatter(
            grad_key_all.reshape(key_count, model_width).astype(jnp.bfloat16),
            "fsdp",
            scatter_dimension=0,
            tiled=True,
        ).astype(jnp.float32),
        lax.psum_scatter(
            grad_value_all.reshape(key_count, model_width).astype(jnp.bfloat16),
            "fsdp",
            scatter_dimension=0,
            tiled=True,
        ).astype(jnp.float32),
    )
    grad_joined = jnp.concatenate(
        [
            rotate_back(grad_query, cosine_table, sine_table).reshape(row_count, model_width),
            rotate_back(grad_key.reshape(head_shape), cosine_table, sine_table).reshape(
                row_count, model_width
            ),
            grad_value,
        ],
        axis=1,
    ).astype(jnp.bfloat16)
    grad_w_qkv = jnp.einsum(
        "rd,re->de", inputs_low, grad_joined, preferred_element_type=jnp.float32
    )
    grad_inputs = grad_first + jnp.einsum(
        "re,de->rd", grad_joined, w_qkv, preferred_element_type=jnp.float32
    )
    weight_grads = (
        grad_w_qkv,
        grad_w_out,
        grad_gain_one,
        grad_offset_one,
        grad_w_gate,
        grad_w_up,
        grad_w_down,
        grad_gain_two,
        grad_offset_two,
    )
    return (grad_inputs, weight_grads)


def shards(
    tokens,
    lengths,
    cotangent,
    w_qkv,
    w_out,
    norm1_gain,
    norm1_bias,
    w_gate,
    w_up,
    w_down,
    norm2_gain,
    norm2_bias,
):
    section_index = lax.axis_index("section")
    fsdp_index = lax.axis_index("fsdp")
    is_first = section_index == 0
    row_count = tokens.shape[2]
    model_width = tokens.shape[3]
    slot_count = row_count * lax.axis_size("fsdp")
    micro_count = lengths.shape[0]
    weights = (
        lax.all_gather(w_qkv[0], "fsdp", axis=0, tiled=True),
        lax.all_gather(w_out[0], "fsdp", axis=0, tiled=True),
        lax.all_gather(norm1_gain[0], "fsdp", axis=0, tiled=True),
        lax.all_gather(norm1_bias[0], "fsdp", axis=0, tiled=True),
        lax.all_gather(w_gate[0], "fsdp", axis=0, tiled=True),
        lax.all_gather(w_up[0], "fsdp", axis=0, tiled=True),
        lax.all_gather(w_down[0], "fsdp", axis=0, tiled=True),
        lax.all_gather(norm2_gain[0], "fsdp", axis=0, tiled=True),
        lax.all_gather(norm2_bias[0], "fsdp", axis=0, tiled=True),
    )
    own_tokens = tokens[0, 0]
    own_cotangent = cotangent[0, 0]
    arrived = partner(jnp.where(is_first, own_cotangent, own_tokens), "section", 0)
    batch_tokens = [
        jnp.where(is_first, own_tokens, arrived),
        jnp.where(is_first, arrived, own_tokens),
    ]
    batch_cotangents = [
        jnp.where(is_first, own_cotangent, arrived),
        jnp.where(is_first, arrived, own_cotangent),
    ]
    cosine_table, sine_table = rotary_tables(fsdp_index * row_count, row_count)
    row_slots = fsdp_index * row_count + jnp.arange(row_count)
    key_slots = jnp.arange(slot_count)
    length_column = lengths[:, 0]
    empty_rows = jnp.zeros((row_count, model_width), jnp.bfloat16)
    carried = empty_rows
    kept_list = []
    layer_outputs = []
    for tick_index in range(micro_count + 1):
        length_now = batch_length(length_column, tick_index - section_index)
        fresh_rows = batch_tokens[tick_index] if tick_index < micro_count else empty_rows
        inputs = jnp.where(is_first, fresh_rows, carried).astype(jnp.float32)
        result, kept_state = layer_forward(
            inputs, weights, key_slots < length_now, cosine_table, sine_table
        )
        result_low = result.astype(jnp.bfloat16)
        kept_list.append(kept_state)
        layer_outputs.append(result_low)
        if tick_index < micro_count:
            carried = shifted(result_low, "section", 1)
    arriving = empty_rows
    totals = None
    owned_total = None
    input_grads = []
    for tick_index in range(micro_count + 1):
        batch_now = tick_index - 1 + section_index
        length_now = batch_length(length_column, batch_now)
        is_valid = (batch_now >= 0) & (batch_now < micro_count)
        seed_rows = batch_cotangents[tick_index] if tick_index < micro_count else empty_rows
        seed_grad = (
            seed_rows.astype(jnp.float32) * (row_slots < length_now).astype(jnp.float32)[:, None]
        )
        grad_out = jnp.where(
            is_valid, jnp.where(is_first, arriving.astype(jnp.float32), seed_grad), 0.0
        )
        earlier_state = kept_list[max(tick_index - 1, 0)]
        later_state = kept_list[min(tick_index + 1, micro_count)]
        kept_state = jax.tree.map(
            lambda first_arr, second_arr: jnp.where(is_first, first_arr, second_arr),
            earlier_state,
            later_state,
        )
        grad_inputs, weight_grads = layer_backward(
            grad_out, kept_state, weights, key_slots < length_now, cosine_table, sine_table
        )
        grad_low = grad_inputs.astype(jnp.bfloat16)
        input_grads.append(grad_low)
        if tick_index < micro_count:
            arriving = shifted(grad_low, "section", -1)
        totals = weight_grads if totals is None else jax.tree.map(jnp.add, totals, weight_grads)
    shares = (
        lax.psum_scatter(
            totals[0].astype(jnp.bfloat16), "fsdp", scatter_dimension=0, tiled=True
        ).astype(jnp.float32),
        lax.psum_scatter(
            totals[1].astype(jnp.bfloat16), "fsdp", scatter_dimension=0, tiled=True
        ).astype(jnp.float32),
        lax.psum_scatter(
            totals[2].astype(jnp.bfloat16), "fsdp", scatter_dimension=0, tiled=True
        ).astype(jnp.float32),
        lax.psum_scatter(
            totals[3].astype(jnp.bfloat16), "fsdp", scatter_dimension=0, tiled=True
        ).astype(jnp.float32),
        lax.psum_scatter(
            totals[4].astype(jnp.bfloat16), "fsdp", scatter_dimension=0, tiled=True
        ).astype(jnp.float32),
        lax.psum_scatter(
            totals[5].astype(jnp.bfloat16), "fsdp", scatter_dimension=0, tiled=True
        ).astype(jnp.float32),
        lax.psum_scatter(
            totals[6].astype(jnp.bfloat16), "fsdp", scatter_dimension=0, tiled=True
        ).astype(jnp.float32),
        lax.psum_scatter(
            totals[7].astype(jnp.bfloat16), "fsdp", scatter_dimension=0, tiled=True
        ).astype(jnp.float32),
        lax.psum_scatter(
            totals[8].astype(jnp.bfloat16), "fsdp", scatter_dimension=0, tiled=True
        ).astype(jnp.float32),
    )
    owned_total = (
        lax.psum(shares[0].astype(jnp.bfloat16), "rep").astype(jnp.float32),
        lax.psum(shares[1].astype(jnp.bfloat16), "rep").astype(jnp.float32),
        lax.psum(shares[2].astype(jnp.bfloat16), "rep").astype(jnp.float32),
        lax.psum(shares[3].astype(jnp.bfloat16), "rep").astype(jnp.float32),
        lax.psum(shares[4].astype(jnp.bfloat16), "rep").astype(jnp.float32),
        lax.psum(shares[5].astype(jnp.bfloat16), "rep").astype(jnp.float32),
        lax.psum(shares[6].astype(jnp.bfloat16), "rep").astype(jnp.float32),
        lax.psum(shares[7].astype(jnp.bfloat16), "rep").astype(jnp.float32),
        lax.psum(shares[8].astype(jnp.bfloat16), "rep").astype(jnp.float32),
    )
    outgoing = jnp.where(is_first, input_grads[2], layer_outputs[1])
    returned = partner(outgoing, "section", 0)
    output_rows = jnp.where(is_first, returned, layer_outputs[2])
    grad_rows = jnp.where(is_first, input_grads[1], returned)
    return (
        output_rows[None, None],
        grad_rows[None, None],
        owned_total[0][None],
        owned_total[1][None],
        owned_total[2][None],
        owned_total[3][None],
        owned_total[4][None],
        owned_total[5][None],
        owned_total[6][None],
        owned_total[7][None],
        owned_total[8][None],
    )


MESH = pl.DeviceIdType.MESH
BLOCK = 128
LANES = 128
QKV_PAD = 640
NORM_ROW = 64


def dot(left, right):
    return jnp.dot(left, right, preferred_element_type=jnp.float32)


def dot_rows(left, right):
    return lax.dot_general(left, right, (((1,), (1,)), ((), ())), preferred_element_type=jnp.float32)


def dot_cols(left, right):
    return lax.dot_general(left, right, (((0,), (0,)), ((), ())), preferred_element_type=jnp.float32)


def low(value):
    return value.astype(jnp.bfloat16)


def wide(value):
    return value.astype(jnp.float32)


def wait_for(ref, sem):
    pltpu.make_async_copy(ref, ref, sem).wait()


def turned(values):
    lane = lax.broadcasted_iota(jnp.int32, values.shape, 1)
    ahead = pltpu.roll(values, LANES - HEAD_DIM // 2, 1)
    behind = pltpu.roll(values, HEAD_DIM // 2, 1)
    return jnp.where(lane % HEAD_DIM < HEAD_DIM // 2, ahead, behind)


def relay_scratch(width, hidden):
    vm = pltpu.VMEM
    bf, f32 = jnp.bfloat16, jnp.float32
    slots = 4 * BLOCK
    own = 2 * BLOCK
    dma = pltpu.SemaphoreType.DMA
    part = width // 4
    share = part // 4
    fpart = hidden // 4
    fshare = fpart // 4
    return dict(
        wq=vm((2, width, QKV_PAD), bf), wo=vm((2, 256, width), bf), wgu=vm((2, width, 2 * fpart), bf),
        wd=vm((2, fpart, width), bf),
        x=vm((2, slots, width), bf), hid=vm((2, slots, width), bf), dfed=vm((2, slots, width), bf),
        datt=vm((2, slots, width), bf),
        q=vm((2, 3, slots, LANES), bf), k=vm((2, 3, slots, LANES), bf), v=vm((2, slots, 256), bf),
        pr=vm((2, 3, slots, slots), bf), mix=vm((2, slots, 256), bf), gu=vm((2, slots, 2 * fpart), bf),
        act=vm((2, slots, fpart), bf),
        n1=vm((2, own, width), f32), n2=vm((2, own, width), f32),
        i1=vm((2, own, LANES), f32), i2=vm((2, own, LANES), f32),
        dgu=vm((slots, 2 * fpart), bf), dmix=vm((slots, 256), bf), dqkv=vm((slots, QKV_PAD), bf),
        ds=vm((slots, slots), bf), dq=vm((slots, LANES), f32),
        hidf=vm((own, width), f32), dres=vm((own, width), f32), dy=vm((own, width), f32),
        mine=vm((own, width), f32), cot=vm((own, width), bf), outb=vm((own, width), bf), tgb=vm((own, width), bf),
        sa=vm((2, 2, BLOCK, width), bf), ra=vm((2, 2, BLOCK, width), bf),
        sb=vm((2, 2, BLOCK, width), bf), rb=vm((2, 2, BLOCK, width), bf),
        par=vm((2, LANES, width), f32), ng=vm((2, LANES, width), f32),
        r1q=vm((2, 3, part, QKV_PAD), bf), r1g=vm((2, 3, part, 2 * fpart), bf),
        r1o=vm((2, 3, share, width), bf), r1d=vm((2, 3, fshare, width), bf),
        s2q=vm((2, part, QKV_PAD), bf), s2g=vm((2, part, 2 * fpart), bf),
        s2o=vm((2, share, width), bf), s2d=vm((2, fshare, width), bf),
        r2q=vm((8, share, QKV_PAD), bf), r2g=vm((8, share, 2 * fpart), bf),
        r2o=vm((2, share, width), bf), r2d=vm((2, fshare, width), bf),
        s3q=vm((4, share, QKV_PAD), bf), s3g=vm((4, share, 2 * fpart), bf),
        s3o=vm((share, width), bf), s3d=vm((fshare, width), bf),
        tok_s=dma((2,)), tok_r=dma, cot_s=dma((2,)), cot_r=dma, xc_s=dma((2,)), xc_r=dma((2,)),
        wz=dma((2, 4, 4)), wss=dma((2, 2)), wso=dma((2, 2, 2)), wfs=dma((2, 4)), wp=dma((2, 4)),
        a_s=dma((2, 2)), a_r=dma((2, 2)), b_s=dma((2, 2)), b_r=dma((2, 2)), c_s=dma((8, 2)), c_r=dma((8, 2)),
        s1s=dma((2, 4)), s1r=dma((2, 4)), s2s=dma((2, 4)), s2r=dma((4,)), s3s=dma((4,)), s3r=dma((4,)),
        o_s=dma((2,)), o_r=dma((2,)),
    )


def relay_kernel(names, length_ref, cos_ref, sin_ref, tok_ref, cot_ref, wq_ref, wo_ref, wg_ref, wu_ref, wd_ref,
                 out_ref, tg_ref, oq_ref, oo_ref, og_ref, od_ref, *scratch):
    m = types.SimpleNamespace(**dict(zip(names, scratch)))
    width = tok_ref.shape[3]
    slots = 4 * BLOCK
    part = width // 4
    share = part // 4
    fpart = wd_ref.shape[1]
    fshare = fpart // 4
    s, z, r = lax.axis_index("section"), lax.axis_index("fsdp"), lax.axis_index("rep")
    zp, zh = z % 2, z // 2
    r0, r1 = r % 2, r // 2
    t = 2 * zp + s
    other = 1 - s

    def mixed(low_bit, high_bit, k):
        a = 1 - low_bit if k & 1 else low_bit
        b = 1 - high_bit if k & 2 else high_bit
        return a + 2 * b

    z_of = [mixed(zp, zh, k) for k in range(4)]
    r_of = [mixed(r0, r1, k) for k in range(4)]
    zp_of = [zp, 1 - zp, zp, 1 - zp]
    across = (other, z, r)
    along = (s, z_of[1], r)

    def remote(src, dst, send, recv, device):
        return pltpu.make_async_remote_copy(
            src_ref=src, dst_ref=dst, send_sem=send, recv_sem=recv, device_id=device, device_id_type=MESH)

    def rows(start, size):
        return pl.ds(pl.multiple_of(start, 16), size)

    barrier = pltpu.get_barrier_semaphore()
    greeted = [(other, z_of[0], r)] + [(c, z_of[k], r) for k in (1, 2, 3) for c in (0, 1)]
    greeted += [(s, z, r_of[k]) for k in (1, 2, 3)]
    for device in greeted:
        pl.semaphore_signal(barrier, inc=1, device_id=device, device_id_type=MESH)
    pl.semaphore_wait(barrier, len(greeted))

    def scatter_rows(src, dst, send, recv, step):
        for i in range(2):
            target = 2 * s + i
            is_self = (target == z) & (s == zp)

            @pl.when(is_self)
            def _():
                if step == "start":
                    pltpu.make_async_copy(src, dst, recv).start()

            @pl.when(jnp.logical_not(is_self))
            def _():
                copy = remote(src, dst, send.at[i], recv, (zp, target, r))
                if step == "start":
                    copy.start()
                else:
                    copy.wait_send()

    tok_args = (tok_ref.at[0, 0], m.x.at[0, rows(z * BLOCK, BLOCK)], m.tok_s, m.tok_r)
    cot_args = (cot_ref.at[0, 0], m.cot.at[rows(zh * BLOCK, BLOCK)], m.cot_s, m.cot_r)
    scatter_rows(*tok_args, "start")

    Q, G, O, D = range(4)
    weight = [m.wq, m.wgu, m.wo, m.wd]
    count = [share, share, share, fshare]

    def source_fan(l, kind):
        for k in range(4):
            size = part if k == 0 else share
            start = 0 if k == 0 else r * share
            here = rows(z * part + start, size)
            for c in range(2):
                target = 2 * zp_of[k] + c
                device = (c, z_of[k], r)
                if kind == Q:
                    pairs = [(wq_ref.at[target, rows(start, size)], m.wq.at[l, here])]
                else:
                    cols = pl.ds(pl.multiple_of(target * fpart, LANES), fpart)
                    pairs = [
                        (wg_ref.at[0, rows(start, size), cols], m.wgu.at[l, here, pl.ds(0, fpart)]),
                        (wu_ref.at[0, rows(start, size), cols], m.wgu.at[l, here, pl.ds(fpart, fpart)]),
                    ]
                for src, dst in pairs:
                    if k == 0 and c == l:
                        pltpu.make_async_copy(src, dst, m.wz.at[l, kind, k]).start()
                    else:
                        remote(src, dst, m.wss.at[l, kind], m.wz.at[l, kind, k], device).start()

    def source_own(l, kind, step):
        ref = wo_ref if kind == O else wd_ref
        n = count[kind]
        for i in range(2):
            target = zh + 2 * i
            own = target == z

            def send(src, dst):
                copy = remote(src, dst, m.wso.at[l, kind - O, i], m.wz.at[l, kind, 0], (zp, target, r))
                if step == "start":
                    copy.start()
                else:
                    copy.wait_send()

            @pl.when(own & (zp == l))
            def _():
                if step == "start":
                    pltpu.make_async_copy(
                        ref.at[0], weight[kind].at[l, pl.ds(0, 4 * n)], m.wz.at[l, kind, 0]).start()

            @pl.when(own & (zp != l))
            def _():
                send(ref.at[0], weight[kind].at[l, pl.ds(0, 4 * n)])

            @pl.when(jnp.logical_not(own))
            def _():
                send(ref.at[0, rows(r * n, n)], weight[kind].at[l, rows(r * n, n)])

    def source(l):
        @pl.when(s == l)
        def _():
            source_fan(l, Q)
            source_own(l, O, "start")
            source_fan(l, G)
            source_own(l, D, "start")

    def source_done(l):
        @pl.when(s == l)
        def _():
            size = 6 * share + part
            wait_for(m.wq.at[l, pl.ds(0, size)], m.wss.at[l, Q])
            wait_for(m.wgu.at[l, pl.ds(0, size)], m.wss.at[l, G])
            source_own(l, O, "wait")
            source_own(l, D, "wait")

    def pass_on(l, kind, here):
        for k in (1, 2, 3):
            block = weight[kind].at[l, here]
            remote(block, block, m.wfs.at[l, kind], m.wp.at[l, kind], (s, z, r_of[k])).start()

    def forward(l, kind):
        n = count[kind]
        if kind in (Q, G):
            for k in (1, 2, 3):
                here = rows(z_of[k] * part + r * n, n)
                wait_for(weight[kind].at[l, here], m.wz.at[l, kind, k])
                pass_on(l, kind, here)
        else:
            @pl.when(t != z)
            def _():
                here = rows(r * n, n)
                wait_for(weight[kind].at[l, here], m.wz.at[l, kind, 0])
                pass_on(l, kind, here)

    def need(l, kind):
        n = count[kind]
        if kind in (Q, G):
            wait_for(weight[kind].at[l, rows(z * part, part)], m.wz.at[l, kind, 0])
            wait_for(weight[kind].at[l, pl.ds(0, 9 * n)], m.wp.at[l, kind])
        else:
            @pl.when(t != z)
            def _():
                wait_for(weight[kind].at[l, pl.ds(0, 3 * n)], m.wp.at[l, kind])

            @pl.when(t == z)
            def _():
                wait_for(weight[kind].at[l, pl.ds(0, 4 * n)], m.wz.at[l, kind, 0])

    def forward_done(l, kind):
        n = count[kind]
        if kind in (Q, G):
            wait_for(weight[kind].at[l, pl.ds(0, 9 * n)], m.wfs.at[l, kind])
        else:
            @pl.when(t != z)
            def _():
                wait_for(weight[kind].at[l, pl.ds(0, 3 * n)], m.wfs.at[l, kind])

    def own_rows(j):
        return rows((2 * j + s) * BLOCK, BLOCK)

    def other_rows(j):
        return rows((2 * j + other) * BLOCK, BLOCK)

    def kept(j):
        return pl.ds(j * BLOCK, BLOCK)

    def send_partial(e, j, left, right, multiply):
        p = e % 2
        m.sa[p, j] = low(multiply(left[other_rows(j)], right))
        copy = remote(m.sa.at[p, j], m.ra.at[p, j], m.a_s.at[p, j], m.a_r.at[p, j], across)
        copy.start()
        m.mine[kept(j)] = multiply(left[own_rows(j)], right)
        return copy

    def send_sum(e, j, copy):
        p = e % 2
        copy.wait()
        m.sb[p, j] = low(m.mine[kept(j)] + wide(m.ra[p, j]))
        copy = remote(m.sb.at[p, j], m.rb.at[p, j], m.b_s.at[p, j], m.b_r.at[p, j], along)
        copy.start()
        return copy

    def summed(e, j, copy):
        p = e % 2
        copy.wait()
        return wide(m.sb[p, j]) + wide(m.rb[p, j])

    def share_rows(e, j, ref):
        block = ref.at[own_rows(j)]
        copy = remote(block, block, m.c_s.at[e, j], m.c_r.at[e, j], across)
        copy.start()
        return copy

    lane = lax.broadcasted_iota(jnp.int32, (BLOCK, LANES), 1)
    lane2 = lax.broadcasted_iota(jnp.int32, (BLOCK, 256), 1)
    length = length_ref[0]
    live_keys = lax.broadcasted_iota(jnp.int32, (BLOCK, slots), 1) < length
    scale = HEAD_DIM ** (-0.5)

    def param(l, i):
        return m.par[l, pl.ds(NORM_ROW + i, 1), :]

    def read_params(l):
        for i in range(width // LANES):
            cols = pl.ds(i * LANES, LANES)
            m.par[l, :, cols] = jnp.transpose(wide(m.wq[l, cols, pl.ds(QKV_PAD - LANES, LANES)]))

    def project(l, j):
        @pl.loop(2 * j, 2 * j + 2)
        def _(i):
            here = rows(i * BLOCK, BLOCK)
            joined = dot(m.x[l, here], m.wq[l])
            cosine, sine = cos_ref[here], sin_ref[here]
            for h in range(3):
                values = joined[:, h * LANES:(h + 1) * LANES]
                values = values * cosine + turned(values) * sine
                m.q[l, h, here] = low(jnp.where(lane < HEAD_DIM, values, 0.0))
                m.k[l, h, here] = low(pltpu.roll(values, HEAD_DIM, 1))
            m.v[l, here] = low(jnp.where(lane2 < 3 * HEAD_DIM, joined[:, 3 * LANES:], 0.0))

    def attend(l):
        @pl.loop(0, slots // BLOCK)
        def _(i):
            here = rows(i * BLOCK, BLOCK)
            total = jnp.zeros((BLOCK, 256), jnp.float32)
            for h in range(3):
                scores = dot_rows(m.q[l, h, here], m.k[l, h]) * scale
                scores = jnp.where(live_keys, scores, masked_score)
                top = jnp.max(scores, axis=-1, keepdims=True)
                weights = jnp.exp(scores - top)
                weights = low(weights / jnp.sum(weights, axis=-1, keepdims=True))
                m.pr[l, h, here] = weights
                inside = lane2 // HEAD_DIM == h
                total = jnp.where(inside, dot(weights, m.v[l]), total)
            m.mix[l, here] = low(total)

    def normed(values):
        centre = values - jnp.mean(values, axis=-1, keepdims=True)
        inverse = lax.rsqrt(jnp.mean(centre * centre, axis=-1, keepdims=True) + norm_eps)
        return centre * inverse, inverse

    def finish_attention(e, l, j, copy):
        values = wide(m.x[l, own_rows(j)]) + summed(e, j, copy)
        norm, inverse = normed(values)
        m.n1[l, kept(j)] = norm
        m.i1[l, kept(j)] = jnp.broadcast_to(inverse, (BLOCK, LANES))
        hidden = norm * param(l, 0) + param(l, 1)
        m.hidf[kept(j)] = hidden
        m.hid[l, own_rows(j)] = low(hidden)
        return share_rows(l, j, m.hid.at[l])

    def feed(l, j):
        @pl.loop(2 * j, 2 * j + 2)
        def _(i):
            here = rows(i * BLOCK, BLOCK)
            rows_in = m.hid[l, here]
            gate = dot(rows_in, m.wgu[l, :, pl.ds(0, fpart)])
            up = dot(rows_in, m.wgu[l, :, pl.ds(fpart, fpart)])
            m.gu[l, here, pl.ds(0, fpart)] = low(gate)
            m.gu[l, here, pl.ds(fpart, fpart)] = low(up)
            m.act[l, here] = low(gate * jax.nn.sigmoid(gate) * up)

    def finish_feed(e, l, j, copy):
        values = m.hidf[kept(j)] + summed(e, j, copy)
        norm, inverse = normed(values)
        m.n2[l, kept(j)] = norm
        m.i2[l, kept(j)] = jnp.broadcast_to(inverse, (BLOCK, LANES))
        result = low(norm * param(l, 2) + param(l, 3))
        if l == 0:
            m.x[1, own_rows(j)] = result
            return share_rows(2, j, m.x.at[1])
        m.outb[kept(j)] = result
        return None

    counts = jnp.where(zp == 0, 1.0, 0.0)

    def add_norm_grads(l, i, dy, norm):
        for k, value in enumerate((dy * norm, dy)):
            at = pl.ds(NORM_ROW + i + k, 1)
            m.ng[l, at, :] += jnp.sum(value, axis=0, keepdims=True) * counts

    def norm_grad(dy, norm, inverse, gain):
        scaled = dy * gain
        return inverse * (
            scaled - jnp.mean(scaled, axis=-1, keepdims=True)
            - norm * jnp.mean(scaled * norm, axis=-1, keepdims=True))

    def back_second(l, j):
        dy = m.dy[kept(j)]
        norm = m.n2[l, kept(j)]
        add_norm_grads(l, 2, dy, norm)
        grad = norm_grad(dy, norm, m.i2[l, kept(j), pl.ds(0, 1)], param(l, 2))
        m.dres[kept(j)] = grad
        m.dfed[l, own_rows(j)] = low(grad)
        return share_rows(3 + l, j, m.dfed.at[l])

    def back_feed(l, j):
        @pl.loop(2 * j, 2 * j + 2)
        def _(i):
            here = rows(i * BLOCK, BLOCK)
            dact = dot_rows(m.dfed[l, here], m.wd[l])
            gate = wide(m.gu[l, here, pl.ds(0, fpart)])
            up = wide(m.gu[l, here, pl.ds(fpart, fpart)])
            sig = jax.nn.sigmoid(gate)
            m.dgu[here, pl.ds(0, fpart)] = low(dact * up * sig * (1.0 + gate * (1.0 - sig)))
            m.dgu[here, pl.ds(fpart, fpart)] = low(dact * gate * sig)

    def back_first(e, l, j, copy):
        dhidden = m.dres[kept(j)] + summed(e, j, copy)
        norm = m.n1[l, kept(j)]
        add_norm_grads(l, 0, dhidden, norm)
        grad = norm_grad(dhidden, norm, m.i1[l, kept(j), pl.ds(0, 1)], param(l, 0))
        m.dres[kept(j)] = grad
        m.datt[l, own_rows(j)] = low(grad)
        return share_rows(5 + l, j, m.datt.at[l])

    def back_mix(l, j):
        @pl.loop(2 * j, 2 * j + 2)
        def _(i):
            here = rows(i * BLOCK, BLOCK)
            m.dmix[here] = low(dot_rows(m.datt[l, here], m.wo[l]))

    def back_attend(l):
        for h in range(3):
            inside = lane2 // HEAD_DIM == h

            @pl.loop(0, slots // BLOCK)
            def _(i):
                here = rows(i * BLOCK, BLOCK)
                grad = m.dmix[here]
                grad = jnp.where(inside, grad, jnp.zeros_like(grad))
                dprobs = dot_rows(grad, m.v[l])
                probs = wide(m.pr[l, h, here])
                centre = jnp.sum(dprobs * probs, axis=-1, keepdims=True)
                dscores = low(probs * (dprobs - centre))
                m.ds[here] = dscores
                m.dq[here] = dot(dscores, m.k[l, h]) * scale

            @pl.loop(0, slots // BLOCK)
            def _(i):
                here = rows(i * BLOCK, BLOCK)
                cols = pl.ds(pl.multiple_of(i * BLOCK, LANES), BLOCK)
                dkey = dot_cols(m.ds[:, cols], m.q[l, h]) * scale
                values = jnp.where(lane < HEAD_DIM, m.dq[here], pltpu.roll(dkey, HEAD_DIM, 1))
                values = values * cos_ref[here] - turned(values) * sin_ref[here]
                m.dqkv[here, pl.ds(h * LANES, LANES)] = low(values)
                dvalue = low(dot_cols(m.pr[l, h, :, cols], m.dmix[...]))
                before = jnp.zeros_like(dvalue) if h == 0 else m.dqkv[here, pl.ds(3 * LANES, 256)]
                m.dqkv[here, pl.ds(3 * LANES, 256)] = jnp.where(inside, dvalue, before)

    def weight_grad(l, kind):
        left, right = (
            (m.x.at[l], m.dqkv), (m.hid.at[l], m.dgu), (m.mix.at[l], m.datt.at[l]),
            (m.act.at[l], m.dfed.at[l]),
        )[kind]

        @pl.loop(0, left.shape[1] // LANES)
        def _(i):
            cols = pl.ds(pl.multiple_of(i * LANES, LANES), LANES)
            grad = dot_cols(left[:, cols], right[...])
            if kind == Q:
                tail = grad[:, QKV_PAD - LANES:] + jnp.transpose(m.ng[l, :, cols])
                weight[kind][l, cols, pl.ds(0, QKV_PAD - LANES)] = low(grad[:, :QKV_PAD - LANES])
                weight[kind][l, cols, pl.ds(QKV_PAD - LANES, LANES)] = low(tail)
            else:
                weight[kind][l, cols] = low(grad)

    first_in = [m.r1q, m.r1g, m.r1o, m.r1d]
    second_out = [m.s2q, m.s2g, m.s2o, m.s2d]
    second_in = [m.r2q, m.r2g, m.r2o, m.r2d]
    third_out = [m.s3q, m.s3g, m.s3o, m.s3d]
    final = [oq_ref, og_ref, oo_ref, od_ref]

    def spread_plane(l, kind):
        n = count[kind]
        for k in (1, 2, 3):
            for b in range(4 if kind in (Q, G) else 1):
                start = (b * part if kind in (Q, G) else 0) + r_of[k] * n
                remote(
                    weight[kind].at[l, rows(start, n)], first_in[kind].at[l, k - 1, pl.ds(b * n, n)],
                    m.s1s.at[l, kind], m.s1r.at[l, kind], (s, z, r_of[k])).start()

    def spread_line(l, kind):
        n = count[kind]
        wait_for(first_in[kind].at[l], m.s1r.at[l, kind])
        for b in range(4 if kind in (Q, G) else 1):
            start = (b * part if kind in (Q, G) else 0) + r * n
            total = wide(weight[kind][l, rows(start, n)])
            for k in range(3):
                total += wide(first_in[kind][l, k, pl.ds(b * n, n)])
            second_out[kind][l, pl.ds(b * n, n)] = low(total)
        if kind in (Q, G):
            slot = 2 * z + s
            for k in range(4):
                src = second_out[kind].at[l, rows(z_of[k] * n, n)]
                dst = second_in[kind].at[slot]
                if k == 0:
                    @pl.when(s == l)
                    def _():
                        pltpu.make_async_copy(src, dst, m.s2r.at[kind]).start()

                    @pl.when(s != l)
                    def _():
                        remote(src, dst, m.s2s.at[l, kind], m.s2r.at[kind], across).start()
                else:
                    remote(src, dst, m.s2s.at[l, kind], m.s2r.at[kind], (l, z_of[k], r)).start()
        else:
            src, dst = second_out[kind].at[l], second_in[kind].at[zh]
            is_self = (t == z) & (s == l)

            @pl.when(is_self)
            def _():
                pltpu.make_async_copy(src, dst, m.s2r.at[kind]).start()

            @pl.when(jnp.logical_not(is_self))
            def _():
                remote(src, dst, m.s2s.at[l, kind], m.s2r.at[kind], (l, t, r)).start()

    def line_done(l, kind):
        wait_for(first_in[kind].at[l], m.s1s.at[l, kind])
        n = count[kind]
        if kind in (Q, G):
            @pl.when(s == l)
            def _():
                wait_for(second_out[kind].at[l, pl.ds(0, 3 * n)], m.s2s.at[l, kind])

            @pl.when(s != l)
            def _():
                wait_for(second_out[kind].at[l], m.s2s.at[l, kind])
        else:
            @pl.when(jnp.logical_not((t == z) & (s == l)))
            def _():
                wait_for(second_out[kind].at[l], m.s2s.at[l, kind])

    def finish(kind):
        n = count[kind]
        wait_for(second_in[kind], m.s2r.at[kind])
        if kind in (Q, G):
            for b in range(4):
                near = 2 * (b // 2) + b % 2
                total = wide(second_in[kind][near]) + wide(second_in[kind][near + 4])
                third_out[kind][b] = low(total)
            dst = final[kind].at[:, rows(r * n, n), :]
        else:
            third_out[kind][...] = low(wide(second_in[kind][0]) + wide(second_in[kind][1]))
            dst = final[kind].at[rows(r * n, n), :]
        for k in (1, 2, 3):
            remote(third_out[kind], dst, m.s3s.at[kind], m.s3r.at[kind], (s, z, r_of[k])).start()
        pltpu.make_async_copy(third_out[kind], dst, m.s3r.at[kind]).start()

    def finish_done(kind):
        wait_for(final[kind], m.s3r.at[kind])
        wait_for(first_in[kind].at[0], m.s3s.at[kind])

    def send_rows(i, src, dst, step):
        block = src.at[rows(zp * BLOCK, BLOCK)]
        is_self = (zh == s) & (t == z)

        @pl.when(is_self)
        def _():
            if step == "start":
                pltpu.make_async_copy(block, dst, m.o_r.at[i]).start()

        @pl.when(jnp.logical_not(is_self))
        def _():
            copy = remote(block, dst, m.o_s.at[i], m.o_r.at[i], (zh, t, r))
            if step == "start":
                copy.start()
            else:
                copy.wait_send()

        if step == "wait":
            wait_for(dst, m.o_r.at[i])

    source(0)
    scatter_rows(*cot_args, "start")
    for l in range(2):
        m.wo[l, pl.ds(part, 256 - part)] = jnp.zeros((256 - part, width), jnp.bfloat16)
        m.ng[l] = jnp.zeros((LANES, width), jnp.float32)
    wait_for(m.x.at[0, pl.ds(0, 2 * BLOCK)], m.tok_r)
    halves = []
    for j in range(2):
        block = m.x.at[0, own_rows(j)]
        copy = remote(block, block, m.xc_s.at[j], m.xc_r.at[j], across)
        copy.start()
        halves.append(copy)
    forward(0, Q)
    need(0, Q)
    read_params(0)
    for j in range(2):
        halves[j].wait()
        project(0, j)
    forward(0, O)
    forward(0, G)
    source(1)
    e = 0
    for l in range(2):
        attend(l)
        if l == 0:
            forward(0, D)
        need(l, O)
        a = [send_partial(e, j, m.mix.at[l], m.wo[l], dot) for j in range(2)]
        b = [send_sum(e, j, a[j]) for j in range(2)]
        if l == 0:
            forward(1, Q)
            forward(1, O)
        c0 = finish_attention(e, l, 0, b[0])
        need(l, G)
        need(l, D)
        c0.wait()
        feed(l, 0)
        a0 = send_partial(e + 1, 0, m.act.at[l], m.wd[l], dot)
        c1 = finish_attention(e, l, 1, b[1])
        b0 = send_sum(e + 1, 0, a0)
        c1.wait()
        feed(l, 1)
        a1 = send_partial(e + 1, 1, m.act.at[l], m.wd[l], dot)
        b1 = send_sum(e + 1, 1, a1)
        if l == 0:
            forward(1, G)
            forward(1, D)
            need(1, Q)
            read_params(1)
        e += 1
        for j, copy in ((0, b0), (1, b1)):
            done = finish_feed(e, l, j, copy)
            if l == 0:
                done.wait()
                project(1, j)
        e += 1
    send_rows(0, m.outb, out_ref.at[0, 0], "start")
    for l in range(2):
        source_done(l)
        for kind in (Q, O, G, D):
            forward_done(l, kind)
    wait_for(m.cot, m.cot_r)
    for j in range(2):
        slot = (2 * j + s) * BLOCK + lax.broadcasted_iota(jnp.int32, (BLOCK, width), 0)
        m.dy[kept(j)] = jnp.where(slot < length, wide(m.cot[kept(j)]), 0.0)
    for l in (1, 0):
        c = [back_second(l, j) for j in range(2)]
        a = []
        for j in range(2):
            c[j].wait()
            back_feed(l, j)
            a.append(send_partial(e, j, m.dgu, m.wgu[l], dot_rows))
        b0 = send_sum(e, 0, a[0])
        weight_grad(l, D)
        spread_plane(l, D)
        b1 = send_sum(e, 1, a[1])
        weight_grad(l, G)
        spread_plane(l, G)
        c = [back_first(e, l, j, copy) for j, copy in ((0, b0), (1, b1))]
        e += 1
        for j in range(2):
            c[j].wait()
            back_mix(l, j)
        back_attend(l)
        a = [send_partial(e, j, m.dqkv, m.wq[l], dot_rows) for j in range(2)]
        b0 = send_sum(e, 0, a[0])
        weight_grad(l, O)
        spread_plane(l, O)
        b1 = send_sum(e, 1, a[1])
        weight_grad(l, Q)
        spread_plane(l, Q)
        for j, copy in ((0, b0), (1, b1)):
            result = low(m.dres[kept(j)] + summed(e, j, copy))
            if l == 1:
                m.dy[kept(j)] = wide(result)
            else:
                m.tgb[kept(j)] = result
        e += 1
    send_rows(1, m.tgb, tg_ref.at[0, 0], "start")
    for l in (1, 0):
        for kind in (D, G, O, Q):
            spread_line(l, kind)

        @pl.when(s == l)
        def _():
            for kind in (D, G, O, Q):
                finish(kind)
    for kind in (D, G, O, Q):
        finish_done(kind)
        for l in (1, 0):
            line_done(l, kind)
    scatter_rows(*tok_args, "wait")
    scatter_rows(*cot_args, "wait")
    send_rows(0, m.outb, out_ref.at[0, 0], "wait")
    send_rows(1, m.tgb, tg_ref.at[0, 0], "wait")


def relay(tokens, lengths, cotangent, w_qkv, w_out, norm1_gain, norm1_bias, w_gate, w_up, w_down, norm2_gain, norm2_bias):
    bf = jnp.bfloat16
    part, width = w_qkv.shape[1], tokens.shape[3]
    hidden = w_gate.shape[2]
    slots = 4 * BLOCK
    cosine, sine = rotary_tables(0, slots)
    sign = jnp.where(jnp.arange(HEAD_DIM) < HEAD_DIM // 2, -1.0, 1.0)
    cosine = jnp.tile(cosine[:, 0], (1, 2))
    sine = jnp.tile(sine[:, 0] * sign, (1, 2))
    length = lax.dynamic_slice_in_dim(lengths[:, 0], lax.axis_index("fsdp") // 2, 1, 0)
    query, key, value = jnp.split(w_qkv[0], 3, axis=1)
    heads = (part, 4, 3, HEAD_DIM)
    joined = jnp.stack([query.reshape(heads), key.reshape(heads)], axis=3).reshape(part, 4, 6 * HEAD_DIM)
    norms = jnp.stack([norm1_gain[0], norm1_bias[0], norm2_gain[0], norm2_bias[0]], axis=1)
    norms = jnp.broadcast_to(jnp.pad(norms, ((0, 0), (0, HEAD_DIM - 4)))[:, None], (part, 4, HEAD_DIM))
    packed = jnp.concatenate([joined, value.reshape(part, 4, 3 * HEAD_DIM), norms], axis=2).transpose(1, 0, 2)
    scratch = relay_scratch(width, hidden)
    any_space, vmem = pl.BlockSpec(memory_space=pl.ANY), pl.BlockSpec(memory_space=pltpu.VMEM)
    fpart = hidden // 4
    outs = pl.pallas_call(
        functools.partial(relay_kernel, tuple(scratch)),
        out_shape=(
            jax.ShapeDtypeStruct(tokens.shape, bf), jax.ShapeDtypeStruct(tokens.shape, bf),
            jax.ShapeDtypeStruct((4, part, QKV_PAD), bf), jax.ShapeDtypeStruct((part, width), bf),
            jax.ShapeDtypeStruct((4, part, 2 * fpart), bf), jax.ShapeDtypeStruct((fpart, width), bf),
        ),
        in_specs=[pl.BlockSpec(memory_space=pltpu.SMEM), vmem, vmem] + [any_space] * 7,
        out_specs=[any_space] * 6,
        scratch_shapes=list(scratch.values()),
        compiler_params=pltpu.CompilerParams(
            collective_id=1, has_side_effects=True, vmem_limit_bytes=VMEM_LIMIT),
    )(length, cosine, sine, tokens, cotangent, packed, w_out, w_gate, w_up, w_down)
    output, token_grad, grad_q, grad_out, grad_gu, grad_down = outs
    pairs = grad_q[:, :, :6 * HEAD_DIM].reshape(4, part, 3, 2, HEAD_DIM).transpose(3, 1, 0, 2, 4).reshape(2, part, width)
    values = grad_q[:, :, 6 * HEAD_DIM:9 * HEAD_DIM].transpose(1, 0, 2).reshape(part, width)
    grad_qkv = jnp.concatenate([pairs[0], pairs[1], values], axis=1).astype(jnp.float32)
    norms = jnp.sum(grad_q[:, :, 9 * HEAD_DIM:9 * HEAD_DIM + 4].astype(jnp.float32), axis=0)
    halves = grad_gu.reshape(4, part, 2, fpart).transpose(2, 1, 0, 3).reshape(2, part, hidden).astype(jnp.float32)
    return (
        output, token_grad, grad_qkv[None], grad_out.astype(jnp.float32)[None], norms[:, 0][None], norms[:, 1][None],
        halves[0][None], halves[1][None], grad_down.astype(jnp.float32)[None], norms[:, 2][None], norms[:, 3][None],
    )


def fits_relay(args):
    tokens, lengths, w_qkv, w_gate, w_down = args[0], args[1], args[3], args[7], args[9]
    axes = tuple(lax.axis_size(axis) for axis in ("section", "fsdp", "rep"))
    return (
        axes == (2, 4, 4)
        and tokens.shape == (1, 1, BLOCK, 768)
        and lengths.shape == (2, 1)
        and w_qkv.shape == (1, 192, 2304)
        and w_gate.shape == (1, 192, 3072)
        and w_down.shape == (1, 768, 768)
    )


def program(*args):
    return relay(*args) if fits_relay(args) else shards(*args)


def solution(mesh):
    return jax.shard_map(
        program,
        mesh=mesh,
        in_specs=(
            P("section", "rep", "fsdp", None),
            P(None, "rep"),
            P("section", "rep", "fsdp", None),
            P("section", "fsdp", None),
            P("section", "fsdp", None),
            P("section", "fsdp"),
            P("section", "fsdp"),
            P("section", "fsdp", None),
            P("section", "fsdp", None),
            P("section", "fsdp", None),
            P("section", "fsdp"),
            P("section", "fsdp"),
        ),
        out_specs=(
            P("section", "rep", "fsdp", None),
            P("section", "rep", "fsdp", None),
            P("section", "fsdp", None),
            P("section", "fsdp", None),
            P("section", "fsdp"),
            P("section", "fsdp"),
            P("section", "fsdp", None),
            P("section", "fsdp", None),
            P("section", "fsdp", None),
            P("section", "fsdp"),
            P("section", "fsdp"),
        ),
        check_vma=False,
    )
```

```python
import functools
import types

import jax
import jax.numpy as jnp
from jax import lax
from jax.experimental import pallas as pl
from jax.experimental.pallas import tpu as pltpu
from jax.sharding import PartitionSpec as P

HEADS = 12
HEAD_DIM = 64


norm_eps = 1e-05
masked_score = -1000000000.0
VMEM_LIMIT = 62 * 2**20


def partner(block, axis, distance):
    count = lax.axis_size(axis)
    route = []
    for low in range(count):
        high = low | 1 << distance
        if high != low and high < count:
            route += [(low, high), (high, low)]
    return lax.ppermute(block, axis, route)


def shifted(value, axis, steps):
    count = lax.axis_size(axis)
    initial, last = (max(0, -steps), min(count, count - steps))
    return lax.ppermute(value, axis, [(source, source + steps) for source in range(initial, last)])


def norm_rows(values, norm_gain, offset):
    centre = values - jnp.mean(values, axis=-1, keepdims=True)
    inverse = lax.rsqrt(jnp.mean(centre * centre, axis=-1, keepdims=True) + norm_eps)
    normed = centre * inverse
    return (normed * norm_gain + offset, normed, inverse)


def norm_back(grad_out, normed, inverse, norm_gain):
    scaled = grad_out * norm_gain
    return inverse * (
        scaled
        - jnp.mean(scaled, axis=-1, keepdims=True)
        - normed * jnp.mean(scaled * normed, axis=-1, keepdims=True)
    )


def rotary_tables(first_slot, row_count):
    half_dim = HEAD_DIM // 2
    inverse_freq = 1000.0 ** (-2.0 * jnp.arange(half_dim, dtype=jnp.float32) / HEAD_DIM)
    places = (first_slot + jnp.arange(row_count)).astype(jnp.float32)
    angles = places[:, None] * inverse_freq[None, :]
    angles = jnp.concatenate([angles, angles], axis=-1)[:, None, :]
    return (jnp.cos(angles), jnp.sin(angles))


def turn_half(values):
    half_dim = values.shape[-1] // 2
    return jnp.concatenate([-values[..., half_dim:], values[..., :half_dim]], axis=-1)


def rotate(values, cosine_table, sine_table):
    return values * cosine_table + turn_half(values) * sine_table


def rotate_back(values, cosine_table, sine_table):
    return values * cosine_table - turn_half(values) * sine_table


def masked_scores(query_rot, key_all, live_keys):
    key_heads = key_all.reshape(key_all.shape[0], HEADS, HEAD_DIM)
    scores = jnp.einsum(
        "qhd,khd->hqk", query_rot, key_heads, preferred_element_type=jnp.float32
    ) * HEAD_DIM ** (-0.5)
    return jnp.where(live_keys[None, None, :], scores, masked_score)


def batch_length(length_column, batch_now):
    picked = jnp.clip(batch_now, 0, length_column.shape[0] - 1)
    return lax.dynamic_index_in_dim(length_column, picked, 0, keepdims=False)


def layer_forward(inputs, weights, live_keys, cosine_table, sine_table):
    w_qkv, w_out, gain_one, offset_one, w_gate, w_up, w_down, gain_two, offset_two = weights
    row_count, model_width = inputs.shape
    head_shape = (row_count, HEADS, HEAD_DIM)
    inputs_low = inputs.astype(jnp.bfloat16)
    joined = jnp.dot(inputs_low, w_qkv, preferred_element_type=jnp.float32)
    query_rot = rotate(
        joined[:, :model_width].reshape(head_shape), cosine_table, sine_table
    ).astype(jnp.bfloat16)
    key_own = (
        rotate(
            joined[:, model_width : 2 * model_width].reshape(head_shape), cosine_table, sine_table
        )
        .reshape(row_count, model_width)
        .astype(jnp.bfloat16)
    )
    value_own = joined[:, 2 * model_width :].astype(jnp.bfloat16)
    key_all, value_all = (
        lax.all_gather(key_own, "fsdp", axis=0, tiled=True),
        lax.all_gather(value_own, "fsdp", axis=0, tiled=True),
    )
    scores = masked_scores(query_rot, key_all, live_keys)
    highest = jnp.max(scores, axis=-1, keepdims=True)
    log_total = highest + jnp.log(jnp.sum(jnp.exp(scores - highest), axis=-1, keepdims=True))
    softmax_weights = jnp.exp(scores - log_total).astype(jnp.bfloat16)
    value_heads = value_all.reshape(value_all.shape[0], HEADS, HEAD_DIM)
    mixed_heads = jnp.einsum(
        "hqk,khd->qhd", softmax_weights, value_heads, preferred_element_type=jnp.float32
    )
    mixed_heads = mixed_heads.reshape(row_count, model_width).astype(jnp.bfloat16)
    attended = jnp.dot(mixed_heads, w_out, preferred_element_type=jnp.float32)
    hidden, normed_one, inverse_one = norm_rows(inputs + attended, gain_one, offset_one)
    hidden_low = hidden.astype(jnp.bfloat16)
    gate_proj = jnp.dot(hidden_low, w_gate, preferred_element_type=jnp.float32)
    upward = jnp.dot(hidden_low, w_up, preferred_element_type=jnp.float32)
    product = (jax.nn.silu(gate_proj) * upward).astype(jnp.bfloat16)
    mlp_out = jnp.dot(product, w_down, preferred_element_type=jnp.float32)
    result, normed_two, inverse_two = norm_rows(hidden + mlp_out, gain_two, offset_two)
    key_saved, value_saved = (key_all, value_all)
    kept_state = (
        inputs_low,
        query_rot,
        key_saved,
        value_saved,
        log_total,
        mixed_heads,
        normed_one,
        inverse_one,
        hidden_low,
        gate_proj,
        upward,
        product,
        normed_two,
        inverse_two,
    )
    return (result, kept_state)


def layer_backward(grad_out, kept_state, weights, live_keys, cosine_table, sine_table):
    w_qkv, w_out, gain_one, offset_one, w_gate, w_up, w_down, gain_two, offset_two = weights
    (
        inputs_low,
        query_rot,
        key_saved,
        value_saved,
        log_total,
        mixed_heads,
        normed_one,
        inverse_one,
        hidden_low,
        gate_proj,
        upward,
        product,
        normed_two,
        inverse_two,
    ) = kept_state
    row_count, model_width = inputs_low.shape
    head_shape = (row_count, HEADS, HEAD_DIM)
    key_all, value_all = (key_saved, value_saved)
    grad_gain_two = jnp.sum(grad_out * normed_two, axis=0)
    grad_offset_two = jnp.sum(grad_out, axis=0)
    grad_second = norm_back(grad_out, normed_two, inverse_two, gain_two)
    grad_fed = grad_second.astype(jnp.bfloat16)
    grad_product = jnp.einsum("rd,fd->rf", grad_fed, w_down, preferred_element_type=jnp.float32)
    grad_w_down = jnp.einsum("rf,rd->fd", product, grad_fed, preferred_element_type=jnp.float32)
    sigmoid_gate = jax.nn.sigmoid(gate_proj)
    silu_gate = gate_proj * sigmoid_gate
    grad_gate = (
        grad_product * upward * sigmoid_gate * (1.0 + gate_proj * (1.0 - sigmoid_gate))
    ).astype(jnp.bfloat16)
    grad_upward = (grad_product * silu_gate).astype(jnp.bfloat16)
    grad_hidden = grad_second + jnp.einsum(
        "rf,df->rd", grad_gate, w_gate, preferred_element_type=jnp.float32
    )
    grad_hidden = grad_hidden + jnp.einsum(
        "rf,df->rd", grad_upward, w_up, preferred_element_type=jnp.float32
    )
    grad_w_gate = jnp.einsum("rd,rf->df", hidden_low, grad_gate, preferred_element_type=jnp.float32)
    grad_w_up = jnp.einsum("rd,rf->df", hidden_low, grad_upward, preferred_element_type=jnp.float32)
    grad_gain_one = jnp.sum(grad_hidden * normed_one, axis=0)
    grad_offset_one = jnp.sum(grad_hidden, axis=0)
    grad_first = norm_back(grad_hidden, normed_one, inverse_one, gain_one)
    grad_attended = grad_first.astype(jnp.bfloat16)
    grad_w_out = jnp.einsum(
        "rd,re->de", mixed_heads, grad_attended, preferred_element_type=jnp.float32
    )
    grad_mixed = (
        jnp.einsum("re,de->rd", grad_attended, w_out, preferred_element_type=jnp.float32)
        .astype(jnp.bfloat16)
        .reshape(head_shape)
    )
    scores = masked_scores(query_rot, key_all, live_keys)
    attention = jnp.exp(scores - log_total)
    key_count = key_all.shape[0]
    key_heads = key_all.reshape(key_count, HEADS, HEAD_DIM)
    value_heads = value_all.reshape(key_count, HEADS, HEAD_DIM)
    grad_attention = jnp.einsum(
        "qhd,khd->hqk", grad_mixed, value_heads, preferred_element_type=jnp.float32
    )
    centre_term = jnp.sum(grad_attention * attention, axis=-1, keepdims=True)
    grad_scores = (attention * (grad_attention - centre_term)).astype(jnp.bfloat16)
    score_scale = HEAD_DIM ** (-0.5)
    grad_query = (
        jnp.einsum("hqk,khd->qhd", grad_scores, key_heads, preferred_element_type=jnp.float32)
        * score_scale
    )
    attention_low = attention.astype(jnp.bfloat16)
    grad_value_all = jnp.einsum(
        "hqk,qhd->khd", attention_low, grad_mixed, preferred_element_type=jnp.float32
    )
    grad_key_all = (
        jnp.einsum("hqk,qhd->khd", grad_scores, query_rot, preferred_element_type=jnp.float32)
        * score_scale
    )
    grad_key, grad_value = (
        lax.psum_scatter(
            grad_key_all.reshape(key_count, model_width).astype(jnp.bfloat16),
            "fsdp",
            scatter_dimension=0,
            tiled=True,
        ).astype(jnp.float32),
        lax.psum_scatter(
            grad_value_all.reshape(key_count, model_width).astype(jnp.bfloat16),
            "fsdp",
            scatter_dimension=0,
            tiled=True,
        ).astype(jnp.float32),
    )
    grad_joined = jnp.concatenate(
        [
            rotate_back(grad_query, cosine_table, sine_table).reshape(row_count, model_width),
            rotate_back(grad_key.reshape(head_shape), cosine_table, sine_table).reshape(
                row_count, model_width
            ),
            grad_value,
        ],
        axis=1,
    ).astype(jnp.bfloat16)
    grad_w_qkv = jnp.einsum(
        "rd,re->de", inputs_low, grad_joined, preferred_element_type=jnp.float32
    )
    grad_inputs = grad_first + jnp.einsum(
        "re,de->rd", grad_joined, w_qkv, preferred_element_type=jnp.float32
    )
    weight_grads = (
        grad_w_qkv,
        grad_w_out,
        grad_gain_one,
        grad_offset_one,
        grad_w_gate,
        grad_w_up,
        grad_w_down,
        grad_gain_two,
        grad_offset_two,
    )
    return (grad_inputs, weight_grads)


def shards(
    tokens,
    lengths,
    cotangent,
    w_qkv,
    w_out,
    norm1_gain,
    norm1_bias,
    w_gate,
    w_up,
    w_down,
    norm2_gain,
    norm2_bias,
):
    section_index = lax.axis_index("section")
    fsdp_index = lax.axis_index("fsdp")
    is_first = section_index == 0
    row_count = tokens.shape[2]
    model_width = tokens.shape[3]
    slot_count = row_count * lax.axis_size("fsdp")
    micro_count = lengths.shape[0]
    weights = (
        lax.all_gather(w_qkv[0], "fsdp", axis=0, tiled=True),
        lax.all_gather(w_out[0], "fsdp", axis=0, tiled=True),
        lax.all_gather(norm1_gain[0], "fsdp", axis=0, tiled=True),
        lax.all_gather(norm1_bias[0], "fsdp", axis=0, tiled=True),
        lax.all_gather(w_gate[0], "fsdp", axis=0, tiled=True),
        lax.all_gather(w_up[0], "fsdp", axis=0, tiled=True),
        lax.all_gather(w_down[0], "fsdp", axis=0, tiled=True),
        lax.all_gather(norm2_gain[0], "fsdp", axis=0, tiled=True),
        lax.all_gather(norm2_bias[0], "fsdp", axis=0, tiled=True),
    )
    own_tokens = tokens[0, 0]
    own_cotangent = cotangent[0, 0]
    arrived = partner(jnp.where(is_first, own_cotangent, own_tokens), "section", 0)
    batch_tokens = [
        jnp.where(is_first, own_tokens, arrived),
        jnp.where(is_first, arrived, own_tokens),
    ]
    batch_cotangents = [
        jnp.where(is_first, own_cotangent, arrived),
        jnp.where(is_first, arrived, own_cotangent),
    ]
    cosine_table, sine_table = rotary_tables(fsdp_index * row_count, row_count)
    row_slots = fsdp_index * row_count + jnp.arange(row_count)
    key_slots = jnp.arange(slot_count)
    length_column = lengths[:, 0]
    empty_rows = jnp.zeros((row_count, model_width), jnp.bfloat16)
    carried = empty_rows
    kept_list = []
    layer_outputs = []
    for tick_index in range(micro_count + 1):
        length_now = batch_length(length_column, tick_index - section_index)
        fresh_rows = batch_tokens[tick_index] if tick_index < micro_count else empty_rows
        inputs = jnp.where(is_first, fresh_rows, carried).astype(jnp.float32)
        result, kept_state = layer_forward(
            inputs, weights, key_slots < length_now, cosine_table, sine_table
        )
        result_low = result.astype(jnp.bfloat16)
        kept_list.append(kept_state)
        layer_outputs.append(result_low)
        if tick_index < micro_count:
            carried = shifted(result_low, "section", 1)
    arriving = empty_rows
    totals = None
    owned_total = None
    input_grads = []
    for tick_index in range(micro_count + 1):
        batch_now = tick_index - 1 + section_index
        length_now = batch_length(length_column, batch_now)
        is_valid = (batch_now >= 0) & (batch_now < micro_count)
        seed_rows = batch_cotangents[tick_index] if tick_index < micro_count else empty_rows
        seed_grad = (
            seed_rows.astype(jnp.float32) * (row_slots < length_now).astype(jnp.float32)[:, None]
        )
        grad_out = jnp.where(
            is_valid, jnp.where(is_first, arriving.astype(jnp.float32), seed_grad), 0.0
        )
        earlier_state = kept_list[max(tick_index - 1, 0)]
        later_state = kept_list[min(tick_index + 1, micro_count)]
        kept_state = jax.tree.map(
            lambda first_arr, second_arr: jnp.where(is_first, first_arr, second_arr),
            earlier_state,
            later_state,
        )
        grad_inputs, weight_grads = layer_backward(
            grad_out, kept_state, weights, key_slots < length_now, cosine_table, sine_table
        )
        grad_low = grad_inputs.astype(jnp.bfloat16)
        input_grads.append(grad_low)
        if tick_index < micro_count:
            arriving = shifted(grad_low, "section", -1)
        totals = weight_grads if totals is None else jax.tree.map(jnp.add, totals, weight_grads)
    shares = (
        lax.psum_scatter(
            totals[0].astype(jnp.bfloat16), "fsdp", scatter_dimension=0, tiled=True
        ).astype(jnp.float32),
        lax.psum_scatter(
            totals[1].astype(jnp.bfloat16), "fsdp", scatter_dimension=0, tiled=True
        ).astype(jnp.float32),
        lax.psum_scatter(
            totals[2].astype(jnp.bfloat16), "fsdp", scatter_dimension=0, tiled=True
        ).astype(jnp.float32),
        lax.psum_scatter(
            totals[3].astype(jnp.bfloat16), "fsdp", scatter_dimension=0, tiled=True
        ).astype(jnp.float32),
        lax.psum_scatter(
            totals[4].astype(jnp.bfloat16), "fsdp", scatter_dimension=0, tiled=True
        ).astype(jnp.float32),
        lax.psum_scatter(
            totals[5].astype(jnp.bfloat16), "fsdp", scatter_dimension=0, tiled=True
        ).astype(jnp.float32),
        lax.psum_scatter(
            totals[6].astype(jnp.bfloat16), "fsdp", scatter_dimension=0, tiled=True
        ).astype(jnp.float32),
        lax.psum_scatter(
            totals[7].astype(jnp.bfloat16), "fsdp", scatter_dimension=0, tiled=True
        ).astype(jnp.float32),
        lax.psum_scatter(
            totals[8].astype(jnp.bfloat16), "fsdp", scatter_dimension=0, tiled=True
        ).astype(jnp.float32),
    )
    owned_total = (
        lax.psum(shares[0].astype(jnp.bfloat16), "rep").astype(jnp.float32),
        lax.psum(shares[1].astype(jnp.bfloat16), "rep").astype(jnp.float32),
        lax.psum(shares[2].astype(jnp.bfloat16), "rep").astype(jnp.float32),
        lax.psum(shares[3].astype(jnp.bfloat16), "rep").astype(jnp.float32),
        lax.psum(shares[4].astype(jnp.bfloat16), "rep").astype(jnp.float32),
        lax.psum(shares[5].astype(jnp.bfloat16), "rep").astype(jnp.float32),
        lax.psum(shares[6].astype(jnp.bfloat16), "rep").astype(jnp.float32),
        lax.psum(shares[7].astype(jnp.bfloat16), "rep").astype(jnp.float32),
        lax.psum(shares[8].astype(jnp.bfloat16), "rep").astype(jnp.float32),
    )
    outgoing = jnp.where(is_first, input_grads[2], layer_outputs[1])
    returned = partner(outgoing, "section", 0)
    output_rows = jnp.where(is_first, returned, layer_outputs[2])
    grad_rows = jnp.where(is_first, input_grads[1], returned)
    return (
        output_rows[None, None],
        grad_rows[None, None],
        owned_total[0][None],
        owned_total[1][None],
        owned_total[2][None],
        owned_total[3][None],
        owned_total[4][None],
        owned_total[5][None],
        owned_total[6][None],
        owned_total[7][None],
        owned_total[8][None],
    )


MESH = pl.DeviceIdType.MESH
BLOCK = 128
LANES = 128
QKV_PAD = 640
NORM_ROW = 64


def dot(left, right):
    return jnp.dot(left, right, preferred_element_type=jnp.float32)


def dot_rows(left, right):
    return lax.dot_general(left, right, (((1,), (1,)), ((), ())), preferred_element_type=jnp.float32)


def dot_cols(left, right):
    return lax.dot_general(left, right, (((0,), (0,)), ((), ())), preferred_element_type=jnp.float32)


def low(value):
    return value.astype(jnp.bfloat16)


def wide(value):
    return value.astype(jnp.float32)


def wait_for(ref, sem):
    pltpu.make_async_copy(ref, ref, sem).wait()


def turned(values):
    lane = lax.broadcasted_iota(jnp.int32, values.shape, 1)
    ahead = pltpu.roll(values, LANES - HEAD_DIM // 2, 1)
    behind = pltpu.roll(values, HEAD_DIM // 2, 1)
    return jnp.where(lane % HEAD_DIM < HEAD_DIM // 2, ahead, behind)


def relay_scratch(width, hidden):
    vm = pltpu.VMEM
    bf, f32 = jnp.bfloat16, jnp.float32
    slots = 4 * BLOCK
    own = 2 * BLOCK
    dma = pltpu.SemaphoreType.DMA
    part = width // 4
    share = part // 4
    fpart = hidden // 4
    fshare = fpart // 4
    return dict(
        wq=vm((2, width, QKV_PAD), bf), wo=vm((2, 256, width), bf), wgu=vm((2, width, 2 * fpart), bf),
        wd=vm((2, fpart, width), bf),
        x=vm((2, slots, width), bf), hid=vm((2, slots, width), bf), dfed=vm((2, slots, width), bf),
        datt=vm((2, slots, width), bf),
        q=vm((2, 3, slots, LANES), bf), k=vm((2, 3, slots, LANES), bf), v=vm((2, slots, 256), bf),
        pr=vm((2, 3, slots, slots), bf), mix=vm((2, slots, 256), bf), gu=vm((2, slots, 2 * fpart), bf),
        act=vm((2, slots, fpart), bf),
        n1=vm((2, own, width), f32), n2=vm((2, own, width), f32),
        i1=vm((2, own, LANES), f32), i2=vm((2, own, LANES), f32),
        dgu=vm((slots, 2 * fpart), bf), dmix=vm((slots, 256), bf), dqkv=vm((slots, QKV_PAD), bf),
        ds=vm((slots, slots), bf), dq=vm((slots, LANES), f32),
        hidf=vm((own, width), f32), dres=vm((own, width), f32), dy=vm((own, width), f32),
        mine=vm((own, width), f32), cot=vm((own, width), bf), outb=vm((own, width), bf), tgb=vm((own, width), bf),
        sa=vm((2, 2, BLOCK, width), bf), ra=vm((2, 2, BLOCK, width), bf),
        sb=vm((2, 2, BLOCK, width), bf), rb=vm((2, 2, BLOCK, width), bf),
        par=vm((2, LANES, width), f32), ng=vm((2, LANES, width), f32),
        r1q=vm((2, 3, part, QKV_PAD), bf), r1g=vm((2, 3, part, 2 * fpart), bf),
        r1o=vm((2, 3, share, width), bf), r1d=vm((2, 3, fshare, width), bf),
        s2q=vm((2, part, QKV_PAD), bf), s2g=vm((2, part, 2 * fpart), bf),
        s2o=vm((2, share, width), bf), s2d=vm((2, fshare, width), bf),
        r2q=vm((8, share, QKV_PAD), bf), r2g=vm((8, share, 2 * fpart), bf),
        r2o=vm((2, share, width), bf), r2d=vm((2, fshare, width), bf),
        s3q=vm((share, 3 * width + LANES), bf), s3g=vm((share, 2 * hidden), bf),
        cos=vm((slots, LANES), f32), sin=vm((slots, LANES), f32), tab=dma((2,)),
        s3o=vm((share, width), bf), s3d=vm((fshare, width), bf),
        tok_s=dma((2,)), tok_r=dma, cot_s=dma((2,)), cot_r=dma, xc_s=dma((2,)), xc_r=dma((2,)),
        wz=dma((2, 4, 4)), wss=dma((2, 2)), wso=dma((2, 2, 2)), wfs=dma((2, 4)), wrs=dma((2, 4)), wpx=dma((2, 4, 3)), wpy=dma((2, 4, 3)), wpd=dma((2, 4)),
        a_s=dma((2, 2)), a_r=dma((2, 2)), b_s=dma((2, 2)), b_r=dma((2, 2)), c_s=dma((8, 2)), c_r=dma((8, 2)),
        s1s=dma((2, 4)), s1a=dma((2, 4)), s1b=dma((2, 4)), s1t=dma((2, 4)), s1r=dma((2, 4)),
        s2s=dma((2, 4)), s2r=dma((4,)),
        s3s=dma((4, 2)), s3x=dma((4,)), s3y=dma((4,)), s3l=dma((4,)), s3t=dma((4,)), s3e=dma((4,)),
        o_s=dma((2,)), o_r=dma((2,)),
    )


def relay_kernel(names, length_ref, cos_in, sin_in, tok_ref, cot_ref, wq_ref, wo_ref, wg_ref, wu_ref, wd_ref,
                 out_ref, tg_ref, oq_ref, oo_ref, og_ref, od_ref, *scratch):
    m = types.SimpleNamespace(**dict(zip(names, scratch)))
    width = tok_ref.shape[3]
    slots = 4 * BLOCK
    part = width // 4
    share = part // 4
    fpart = wd_ref.shape[1]
    fshare = fpart // 4
    s, z, r = lax.axis_index("section"), lax.axis_index("fsdp"), lax.axis_index("rep")
    zp, zh = z % 2, z // 2
    r0, r1 = r % 2, r // 2
    t = 2 * zp + s
    other = 1 - s

    def mixed(low_bit, high_bit, k):
        a = 1 - low_bit if k & 1 else low_bit
        b = 1 - high_bit if k & 2 else high_bit
        return a + 2 * b

    z_of = [mixed(zp, zh, k) for k in range(4)]
    r_of = [mixed(r0, r1, k) for k in range(4)]
    zp_of = [zp, 1 - zp, zp, 1 - zp]
    across = (other, z, r)
    along = (s, z_of[1], r)

    def remote(src, dst, send, recv, device):
        return pltpu.make_async_remote_copy(
            src_ref=src, dst_ref=dst, send_sem=send, recv_sem=recv, device_id=device, device_id_type=MESH)

    def rows(start, size):
        return pl.ds(pl.multiple_of(start, 16), size)

    barrier = pltpu.get_barrier_semaphore()
    greeted = [(other, z_of[0], r)] + [(c, z_of[k], r) for k in (1, 2, 3) for c in (0, 1)]
    greeted += [(s, z, r_of[k]) for k in (1, 2, 3)]
    for device in greeted:
        pl.semaphore_signal(barrier, inc=1, device_id=device, device_id_type=MESH)
    pl.semaphore_wait(barrier, len(greeted))

    def scatter_rows(src, dst, send, recv, step):
        for i in range(2):
            target = 2 * s + i
            is_self = (target == z) & (s == zp)

            @pl.when(is_self)
            def _():
                if step == "start":
                    pltpu.make_async_copy(src, dst, recv).start()

            @pl.when(jnp.logical_not(is_self))
            def _():
                copy = remote(src, dst, send.at[i], recv, (zp, target, r))
                if step == "start":
                    copy.start()
                else:
                    copy.wait_send()

    tok_args = (tok_ref.at[0, 0], m.x.at[0, rows(z * BLOCK, BLOCK)], m.tok_s, m.tok_r)
    cot_args = (cot_ref.at[0, 0], m.cot.at[rows(zh * BLOCK, BLOCK)], m.cot_s, m.cot_r)
    scatter_rows(*tok_args, "start")

    Q, G, O, D = range(4)
    weight = [m.wq, m.wgu, m.wo, m.wd]
    count = [share, share, share, fshare]

    def source_fan(l, kind):
        for k in range(4):
            size = part if k == 0 else share
            start = 0 if k == 0 else r * share
            here = rows(z * part + start, size)
            for c in range(2):
                target = 2 * zp_of[k] + c
                device = (c, z_of[k], r)
                if kind == Q:
                    pairs = [(wq_ref.at[target, rows(start, size)], m.wq.at[l, here])]
                else:
                    cols = pl.ds(pl.multiple_of(target * fpart, LANES), fpart)
                    pairs = [
                        (wg_ref.at[0, rows(start, size), cols], m.wgu.at[l, here, pl.ds(0, fpart)]),
                        (wu_ref.at[0, rows(start, size), cols], m.wgu.at[l, here, pl.ds(fpart, fpart)]),
                    ]
                for src, dst in pairs:
                    if k == 0 and c == l:
                        pltpu.make_async_copy(src, dst, m.wz.at[l, kind, k]).start()
                    else:
                        remote(src, dst, m.wss.at[l, kind], m.wz.at[l, kind, k], device).start()

    def source_own(l, kind, step):
        ref = wo_ref if kind == O else wd_ref
        n = count[kind]
        for i in range(2):
            target = zh + 2 * i
            own = target == z

            def send(src, dst):
                copy = remote(src, dst, m.wso.at[l, kind - O, i], m.wz.at[l, kind, 0], (zp, target, r))
                if step == "start":
                    copy.start()
                else:
                    copy.wait_send()

            @pl.when(own & (zp == l))
            def _():
                if step == "start":
                    pltpu.make_async_copy(
                        ref.at[0], weight[kind].at[l, pl.ds(0, 4 * n)], m.wz.at[l, kind, 0]).start()

            @pl.when(own & (zp != l))
            def _():
                send(ref.at[0], weight[kind].at[l, pl.ds(0, 4 * n)])

            @pl.when(jnp.logical_not(own))
            def _():
                send(ref.at[0, rows(r * n, n)], weight[kind].at[l, rows(r * n, n)])

    def source(l):
        @pl.when(s == l)
        def _():
            source_fan(l, Q)
            source_own(l, O, "start")
            source_fan(l, G)
            source_own(l, D, "start")

    def source_done(l):
        @pl.when(s == l)
        def _():
            size = 6 * share + part
            wait_for(m.wq.at[l, pl.ds(0, size)], m.wss.at[l, Q])
            wait_for(m.wgu.at[l, pl.ds(0, size)], m.wss.at[l, G])
            source_own(l, O, "wait")
            source_own(l, D, "wait")

    xn, yn = (s, z, r_of[1]), (s, z, r_of[2])
    cut = [3 * LANES, fpart, width // 2, width // 2]

    def halves_of(kind, lanes):
        return pl.ds(0, cut[kind]), pl.ds(cut[kind], lanes - cut[kind])

    def block_rows(kind, k, rep):
        n = count[kind]
        return rows((z_of[k] * part if kind in (Q, G) else 0) + rep * n, n)

    def pass_on(l, kind, k):
        block = weight[kind].at[l, block_rows(kind, k, r)]
        wait_for(block, m.wz.at[l, kind, k if kind in (Q, G) else 0])
        remote(block, block, m.wfs.at[l, kind], m.wpx.at[l, kind, k - 1], xn).start()
        remote(block, block, m.wfs.at[l, kind], m.wpy.at[l, kind, k - 1], yn).start()

    def pass_half(l, kind, k):
        first, second = halves_of(kind, weight[kind].shape[2])
        here = block_rows(kind, k, r_of[1])
        wait_for(weight[kind].at[l, here], m.wpx.at[l, kind, k - 1])
        half = weight[kind].at[l, here, first]
        remote(half, half, m.wrs.at[l, kind], m.wpd.at[l, kind], yn).start()
        here = block_rows(kind, k, r_of[2])
        wait_for(weight[kind].at[l, here], m.wpy.at[l, kind, k - 1])
        half = weight[kind].at[l, here, second]
        remote(half, half, m.wrs.at[l, kind], m.wpd.at[l, kind], xn).start()

    def each_block(kind, step):
        if kind in (Q, G):
            for k in (1, 2, 3):
                step(k)
        else:
            pl.when(t != z)(lambda: step(1))

    def forward(l, kind):
        each_block(kind, lambda k: pass_on(l, kind, k))

    def relay_on(l, kind):
        each_block(kind, lambda k: pass_half(l, kind, k))

    def need(l, kind):
        n = count[kind]
        if kind in (Q, G):
            wait_for(weight[kind].at[l, rows(z * part, part)], m.wz.at[l, kind, 0])
            wait_for(weight[kind].at[l, pl.ds(0, 3 * n)], m.wpd.at[l, kind])
        else:
            @pl.when(t != z)
            def _():
                wait_for(weight[kind].at[l, pl.ds(0, n)], m.wpd.at[l, kind])

            @pl.when(t == z)
            def _():
                wait_for(weight[kind].at[l, pl.ds(0, 4 * n)], m.wz.at[l, kind, 0])

    def forward_done(l, kind):
        n = count[kind]

        def wait(blocks):
            wait_for(weight[kind].at[l, pl.ds(0, 2 * blocks * n)], m.wfs.at[l, kind])
            wait_for(weight[kind].at[l, pl.ds(0, blocks * n)], m.wrs.at[l, kind])

        if kind in (Q, G):
            wait(3)
        else:
            pl.when(t != z)(lambda: wait(1))

    def own_rows(j):
        return rows((2 * j + s) * BLOCK, BLOCK)

    def other_rows(j):
        return rows((2 * j + other) * BLOCK, BLOCK)

    def kept(j):
        return pl.ds(j * BLOCK, BLOCK)

    def send_partial(e, j, left, right, multiply):
        p = e % 2
        m.sa[p, j] = low(multiply(left[other_rows(j)], right))
        copy = remote(m.sa.at[p, j], m.ra.at[p, j], m.a_s.at[p, j], m.a_r.at[p, j], across)
        copy.start()
        m.mine[kept(j)] = multiply(left[own_rows(j)], right)
        return copy

    def send_sum(e, j, copy):
        p = e % 2
        copy.wait()
        m.sb[p, j] = low(m.mine[kept(j)] + wide(m.ra[p, j]))
        copy = remote(m.sb.at[p, j], m.rb.at[p, j], m.b_s.at[p, j], m.b_r.at[p, j], along)
        copy.start()
        return copy

    def summed(e, j, copy):
        p = e % 2
        copy.wait()
        return wide(m.sb[p, j]) + wide(m.rb[p, j])

    def share_rows(e, j, ref):
        block = ref.at[own_rows(j)]
        copy = remote(block, block, m.c_s.at[e, j], m.c_r.at[e, j], across)
        copy.start()
        return copy

    lane = lax.broadcasted_iota(jnp.int32, (BLOCK, LANES), 1)
    lane2 = lax.broadcasted_iota(jnp.int32, (BLOCK, 256), 1)
    length = length_ref[zh, 0]
    cos_ref, sin_ref = m.cos, m.sin
    live_keys = lax.broadcasted_iota(jnp.int32, (BLOCK, slots), 1) < length
    scale = HEAD_DIM ** (-0.5)

    def param(l, i):
        return m.par[l, pl.ds(NORM_ROW + i, 1), :]

    def read_params(l):
        for i in range(width // LANES):
            cols = pl.ds(i * LANES, LANES)
            m.par[l, :, cols] = jnp.transpose(wide(m.wq[l, cols, pl.ds(QKV_PAD - LANES, LANES)]))

    def project(l, j):
        @pl.loop(2 * j, 2 * j + 2)
        def _(i):
            here = rows(i * BLOCK, BLOCK)
            joined = dot(m.x[l, here], m.wq[l])
            cosine, sine = cos_ref[here], sin_ref[here]
            for h in range(3):
                values = joined[:, h * LANES:(h + 1) * LANES]
                values = values * cosine + turned(values) * sine
                m.q[l, h, here] = low(jnp.where(lane < HEAD_DIM, values, 0.0))
                m.k[l, h, here] = low(pltpu.roll(values, HEAD_DIM, 1))
            m.v[l, here] = low(jnp.where(lane2 < 3 * HEAD_DIM, joined[:, 3 * LANES:], 0.0))

    def attend(l):
        @pl.loop(0, slots // BLOCK)
        def _(i):
            here = rows(i * BLOCK, BLOCK)
            total = jnp.zeros((BLOCK, 256), jnp.float32)
            for h in range(3):
                scores = dot_rows(m.q[l, h, here], m.k[l, h]) * scale
                scores = jnp.where(live_keys, scores, masked_score)
                top = jnp.max(scores, axis=-1, keepdims=True)
                weights = jnp.exp(scores - top)
                weights = low(weights / jnp.sum(weights, axis=-1, keepdims=True))
                m.pr[l, h, here] = weights
                inside = lane2 // HEAD_DIM == h
                total = jnp.where(inside, dot(weights, m.v[l]), total)
            m.mix[l, here] = low(total)

    def normed(values):
        centre = values - jnp.mean(values, axis=-1, keepdims=True)
        inverse = lax.rsqrt(jnp.mean(centre * centre, axis=-1, keepdims=True) + norm_eps)
        return centre * inverse, inverse

    def finish_attention(e, l, j, copy):
        values = wide(m.x[l, own_rows(j)]) + summed(e, j, copy)
        norm, inverse = normed(values)
        m.n1[l, kept(j)] = norm
        m.i1[l, kept(j)] = jnp.broadcast_to(inverse, (BLOCK, LANES))
        hidden = norm * param(l, 0) + param(l, 1)
        m.hidf[kept(j)] = hidden
        m.hid[l, own_rows(j)] = low(hidden)
        return share_rows(l, j, m.hid.at[l])

    def feed(l, j):
        @pl.loop(2 * j, 2 * j + 2)
        def _(i):
            here = rows(i * BLOCK, BLOCK)
            rows_in = m.hid[l, here]
            gate = dot(rows_in, m.wgu[l, :, pl.ds(0, fpart)])
            up = dot(rows_in, m.wgu[l, :, pl.ds(fpart, fpart)])
            m.gu[l, here, pl.ds(0, fpart)] = low(gate)
            m.gu[l, here, pl.ds(fpart, fpart)] = low(up)
            m.act[l, here] = low(gate * jax.nn.sigmoid(gate) * up)

    def finish_feed(e, l, j, copy):
        values = m.hidf[kept(j)] + summed(e, j, copy)
        norm, inverse = normed(values)
        m.n2[l, kept(j)] = norm
        m.i2[l, kept(j)] = jnp.broadcast_to(inverse, (BLOCK, LANES))
        result = low(norm * param(l, 2) + param(l, 3))
        if l == 0:
            m.x[1, own_rows(j)] = result
            return share_rows(2, j, m.x.at[1])
        m.outb[kept(j)] = result
        return None

    counts = jnp.where(zp == 0, 1.0, 0.0)

    def add_norm_grads(l, i, dy, norm):
        for k, value in enumerate((dy * norm, dy)):
            at = pl.ds(NORM_ROW + i + k, 1)
            m.ng[l, at, :] += jnp.sum(value, axis=0, keepdims=True) * counts

    def norm_grad(dy, norm, inverse, gain):
        scaled = dy * gain
        return inverse * (
            scaled - jnp.mean(scaled, axis=-1, keepdims=True)
            - norm * jnp.mean(scaled * norm, axis=-1, keepdims=True))

    def back_second(l, j):
        dy = m.dy[kept(j)]
        norm = m.n2[l, kept(j)]
        add_norm_grads(l, 2, dy, norm)
        grad = norm_grad(dy, norm, m.i2[l, kept(j), pl.ds(0, 1)], param(l, 2))
        m.dres[kept(j)] = grad
        m.dfed[l, own_rows(j)] = low(grad)
        return share_rows(3 + l, j, m.dfed.at[l])

    def back_feed(l, j):
        @pl.loop(2 * j, 2 * j + 2)
        def _(i):
            here = rows(i * BLOCK, BLOCK)
            dact = dot_rows(m.dfed[l, here], m.wd[l])
            gate = wide(m.gu[l, here, pl.ds(0, fpart)])
            up = wide(m.gu[l, here, pl.ds(fpart, fpart)])
            sig = jax.nn.sigmoid(gate)
            m.dgu[here, pl.ds(0, fpart)] = low(dact * up * sig * (1.0 + gate * (1.0 - sig)))
            m.dgu[here, pl.ds(fpart, fpart)] = low(dact * gate * sig)

    def back_first(e, l, j, copy):
        dhidden = m.dres[kept(j)] + summed(e, j, copy)
        norm = m.n1[l, kept(j)]
        add_norm_grads(l, 0, dhidden, norm)
        grad = norm_grad(dhidden, norm, m.i1[l, kept(j), pl.ds(0, 1)], param(l, 0))
        m.dres[kept(j)] = grad
        m.datt[l, own_rows(j)] = low(grad)
        return share_rows(5 + l, j, m.datt.at[l])

    def back_mix(l, j):
        @pl.loop(2 * j, 2 * j + 2)
        def _(i):
            here = rows(i * BLOCK, BLOCK)
            m.dmix[here] = low(dot_rows(m.datt[l, here], m.wo[l]))

    def back_attend(l):
        for h in range(3):
            inside = lane2 // HEAD_DIM == h

            @pl.loop(0, slots // BLOCK)
            def _(i):
                here = rows(i * BLOCK, BLOCK)
                grad = m.dmix[here]
                grad = jnp.where(inside, grad, jnp.zeros_like(grad))
                dprobs = dot_rows(grad, m.v[l])
                probs = wide(m.pr[l, h, here])
                centre = jnp.sum(dprobs * probs, axis=-1, keepdims=True)
                dscores = low(probs * (dprobs - centre))
                m.ds[here] = dscores
                m.dq[here] = dot(dscores, m.k[l, h]) * scale

            @pl.loop(0, slots // BLOCK)
            def _(i):
                here = rows(i * BLOCK, BLOCK)
                cols = pl.ds(pl.multiple_of(i * BLOCK, LANES), BLOCK)
                dkey = dot_cols(m.ds[:, cols], m.q[l, h]) * scale
                values = jnp.where(lane < HEAD_DIM, m.dq[here], pltpu.roll(dkey, HEAD_DIM, 1))
                values = values * cos_ref[here] - turned(values) * sin_ref[here]
                m.dqkv[here, pl.ds(h * LANES, LANES)] = low(values)
                dvalue = low(dot_cols(m.pr[l, h, :, cols], m.dmix[...]))
                before = jnp.zeros_like(dvalue) if h == 0 else m.dqkv[here, pl.ds(3 * LANES, 256)]
                m.dqkv[here, pl.ds(3 * LANES, 256)] = jnp.where(inside, dvalue, before)

    def weight_grad(l, kind):
        left, right = (
            (m.x.at[l], m.dqkv), (m.hid.at[l], m.dgu), (m.mix.at[l], m.datt.at[l]),
            (m.act.at[l], m.dfed.at[l]),
        )[kind]

        @pl.loop(0, left.shape[1] // LANES)
        def _(i):
            cols = pl.ds(pl.multiple_of(i * LANES, LANES), LANES)
            grad = dot_cols(left[:, cols], right[...])
            if kind == Q:
                tail = grad[:, QKV_PAD - LANES:] + jnp.transpose(m.ng[l, :, cols])
                weight[kind][l, cols, pl.ds(0, QKV_PAD - LANES)] = low(grad[:, :QKV_PAD - LANES])
                weight[kind][l, cols, pl.ds(QKV_PAD - LANES, LANES)] = low(tail)
            else:
                weight[kind][l, cols] = low(grad)

    first_in = [m.r1q, m.r1g, m.r1o, m.r1d]
    second_out = [m.s2q, m.s2g, m.s2o, m.s2d]
    second_in = [m.r2q, m.r2g, m.r2o, m.r2d]
    third_out = [m.s3q, m.s3g, m.s3o, m.s3d]
    final = [oq_ref, og_ref, oo_ref, od_ref]

    def blocks_of(kind):
        return range(4 if kind in (Q, G) else 1)

    def grad_rows(kind, b, rep):
        n = count[kind]
        return rows((b * part if kind in (Q, G) else 0) + rep * n, n)

    def plane_first(l, kind):
        n = count[kind]
        first, second = halves_of(kind, weight[kind].shape[2])
        for b in blocks_of(kind):
            for slot, rep in ((1, r_of[3]), (0, None)):
                for lanes, device, near, sem in ((first, xn, r_of[1], m.s1a), (second, yn, r_of[2], m.s1b)):
                    block = grad_rows(kind, b, near if rep is None else rep)
                    remote(
                        weight[kind].at[l, block, lanes], first_in[kind].at[l, slot, pl.ds(b * n, n), lanes],
                        m.s1s.at[l, kind], sem.at[l, kind], device).start()

    def plane_second(l, kind):
        n = count[kind]
        first, second = halves_of(kind, weight[kind].shape[2])
        for lanes, device, rep, sem in ((first, yn, r_of[2], m.s1a), (second, xn, r_of[1], m.s1b)):
            wait_for(first_in[kind].at[l, pl.ds(0, 2), :, lanes], sem.at[l, kind])
            for b in blocks_of(kind):
                block = grad_rows(kind, b, rep)
                here = pl.ds(b * n, n)
                weight[kind][l, block, lanes] = low(
                    wide(weight[kind][l, block, lanes]) + wide(first_in[kind][l, 1, here, lanes]))
                remote(
                    weight[kind].at[l, block, lanes], first_in[kind].at[l, 2, here, lanes],
                    m.s1t.at[l, kind], m.s1r.at[l, kind], device).start()

    def spread_line(l, kind):
        n = count[kind]
        wait_for(first_in[kind].at[l, 2], m.s1r.at[l, kind])
        for b in blocks_of(kind):
            here = pl.ds(b * n, n)
            total = wide(weight[kind][l, grad_rows(kind, b, r)])
            total += wide(first_in[kind][l, 0, here]) + wide(first_in[kind][l, 2, here])
            second_out[kind][l, here] = low(total)
        if kind in (Q, G):
            slot = 2 * z + s
            for k in range(4):
                src = second_out[kind].at[l, rows(z_of[k] * n, n)]
                dst = second_in[kind].at[slot]
                if k == 0:
                    @pl.when(s == l)
                    def _():
                        pltpu.make_async_copy(src, dst, m.s2r.at[kind]).start()

                    @pl.when(s != l)
                    def _():
                        remote(src, dst, m.s2s.at[l, kind], m.s2r.at[kind], across).start()
                else:
                    remote(src, dst, m.s2s.at[l, kind], m.s2r.at[kind], (l, z_of[k], r)).start()
        else:
            src, dst = second_out[kind].at[l], second_in[kind].at[zh]
            is_self = (t == z) & (s == l)

            @pl.when(is_self)
            def _():
                pltpu.make_async_copy(src, dst, m.s2r.at[kind]).start()

            @pl.when(jnp.logical_not(is_self))
            def _():
                remote(src, dst, m.s2s.at[l, kind], m.s2r.at[kind], (l, t, r)).start()

    def line_done(l, kind):
        wait_for(first_in[kind].at[l, pl.ds(0, 2)], m.s1s.at[l, kind])
        wait_for(first_in[kind].at[l, 2], m.s1t.at[l, kind])
        n = count[kind]
        if kind in (Q, G):
            @pl.when(s == l)
            def _():
                wait_for(second_out[kind].at[l, pl.ds(0, 3 * n)], m.s2s.at[l, kind])

            @pl.when(s != l)
            def _():
                wait_for(second_out[kind].at[l], m.s2s.at[l, kind])
        else:
            @pl.when(jnp.logical_not((t == z) & (s == l)))
            def _():
                wait_for(second_out[kind].at[l], m.s2s.at[l, kind])

    def in_order(parts):
        low_half = lax.broadcasted_iota(jnp.int32, (share, LANES), 1) < HEAD_DIM

        def swapped(values):
            return pltpu.roll(values, HEAD_DIM, 1)

        def pair(head):
            return parts[head // 3][:, head % 3 * LANES:(head % 3 + 1) * LANES]

        def value(head, at_low):
            h = head % 3
            start = 3 * LANES + h // 2 * LANES
            values = parts[head // 3][:, start:start + LANES]
            return values if (h != 1) == at_low else swapped(values)

        for c in range(HEADS // 2):
            even, odd = pair(2 * c), pair(2 * c + 1)
            for i, values in enumerate((
                jnp.where(low_half, even, swapped(odd)), jnp.where(low_half, swapped(even), odd),
                jnp.where(low_half, value(2 * c, True), value(2 * c + 1, False)),
            )):
                m.s3q[:, pl.ds(i * width + c * LANES, LANES)] = low(values)
        norms = sum(values[:, QKV_PAD - LANES:] for values in parts)
        m.s3q[:, pl.ds(3 * width, LANES)] = low(norms)

    def out_cut(kind):
        lanes = third_out[kind].shape[1]
        middle = lanes // 2 // LANES * LANES
        return pl.ds(0, middle), pl.ds(middle, lanes - middle)

    def finish(kind):
        wait_for(second_in[kind], m.s2r.at[kind])
        if kind in (Q, G):
            parts = []
            for b in range(4):
                near = 2 * (b // 2) + b % 2
                parts.append(wide(second_in[kind][near]) + wide(second_in[kind][near + 4]))
                if kind == G:
                    for i in range(2):
                        m.s3g[:, pl.ds((4 * i + b) * fpart, fpart)] = low(parts[b][:, i * fpart:(i + 1) * fpart])
            if kind == Q:
                in_order(parts)
        else:
            third_out[kind][...] = low(wide(second_in[kind][0]) + wide(second_in[kind][1]))
        dst = final[kind].at[rows(r * count[kind], count[kind])]
        remote(third_out[kind], dst, m.s3s.at[kind, 0], m.s3x.at[kind], xn).start()
        remote(third_out[kind], dst, m.s3s.at[kind, 1], m.s3y.at[kind], yn).start()
        pltpu.make_async_copy(third_out[kind], dst, m.s3l.at[kind]).start()

    def finish_half(kind):
        n = count[kind]
        for lanes, rep, device, sem in zip(out_cut(kind), r_of[1:3], (yn, xn), (m.s3x, m.s3y)):
            wait_for(final[kind].at[rows(rep * n, n)], sem.at[kind])
            half = final[kind].at[rows(rep * n, n), lanes]
            remote(half, half, m.s3t.at[kind], m.s3e.at[kind], device).start()

    def finish_done(kind):
        block = final[kind].at[pl.ds(0, count[kind])]
        wait_for(block, m.s3l.at[kind])
        wait_for(block, m.s3e.at[kind])
        wait_for(third_out[kind], m.s3s.at[kind, 0])
        wait_for(third_out[kind], m.s3s.at[kind, 1])
        wait_for(block, m.s3t.at[kind])

    def send_rows(i, src, dst, step):
        block = src.at[rows(zp * BLOCK, BLOCK)]
        is_self = (zh == s) & (t == z)

        @pl.when(is_self)
        def _():
            if step == "start":
                pltpu.make_async_copy(block, dst, m.o_r.at[i]).start()

        @pl.when(jnp.logical_not(is_self))
        def _():
            copy = remote(block, dst, m.o_s.at[i], m.o_r.at[i], (zh, t, r))
            if step == "start":
                copy.start()
            else:
                copy.wait_send()

        if step == "wait":
            wait_for(dst, m.o_r.at[i])

    source(0)
    tables = [pltpu.make_async_copy(src, dst, m.tab.at[i]) for i, (src, dst) in enumerate(((cos_in, m.cos), (sin_in, m.sin)))]
    for copy in tables:
        copy.start()
    scatter_rows(*cot_args, "start")
    for l in range(2):
        m.wo[l, pl.ds(part, 256 - part)] = jnp.zeros((256 - part, width), jnp.bfloat16)
        m.ng[l] = jnp.zeros((LANES, width), jnp.float32)
    wait_for(m.x.at[0, pl.ds(0, 2 * BLOCK)], m.tok_r)
    halves = []
    for j in range(2):
        block = m.x.at[0, own_rows(j)]
        copy = remote(block, block, m.xc_s.at[j], m.xc_r.at[j], across)
        copy.start()
        halves.append(copy)
    forward(0, Q)
    forward(0, O)
    relay_on(0, Q)
    relay_on(0, O)
    for copy in tables:
        copy.wait()
    need(0, Q)
    read_params(0)
    for j in range(2):
        halves[j].wait()
        project(0, j)
    forward(0, G)
    source(1)
    e = 0
    for l in range(2):
        attend(l)
        if l == 0:
            relay_on(0, G)
            forward(0, D)
        need(l, O)
        a = [send_partial(e, j, m.mix.at[l], m.wo[l], dot) for j in range(2)]
        b = [send_sum(e, j, a[j]) for j in range(2)]
        if l == 0:
            relay_on(0, D)
            forward(1, Q)
            forward(1, O)
        else:
            relay_on(1, D)
        c0 = finish_attention(e, l, 0, b[0])
        need(l, G)
        c0.wait()
        feed(l, 0)
        need(l, D)
        a0 = send_partial(e + 1, 0, m.act.at[l], m.wd[l], dot)
        c1 = finish_attention(e, l, 1, b[1])
        b0 = send_sum(e + 1, 0, a0)
        if l == 0:
            relay_on(1, Q)
            relay_on(1, O)
        c1.wait()
        feed(l, 1)
        a1 = send_partial(e + 1, 1, m.act.at[l], m.wd[l], dot)
        b1 = send_sum(e + 1, 1, a1)
        if l == 0:
            forward(1, G)
            need(1, Q)
            read_params(1)
        e += 1
        for j, copy in ((0, b0), (1, b1)):
            done = finish_feed(e, l, j, copy)
            if l == 0:
                done.wait()
                project(1, j)
        if l == 0:
            relay_on(1, G)
            forward(1, D)
        e += 1
    send_rows(0, m.outb, out_ref.at[0, 0], "start")
    for l in range(2):
        source_done(l)
        for kind in (Q, O, G, D):
            forward_done(l, kind)
    wait_for(m.cot, m.cot_r)
    for j in range(2):
        slot = (2 * j + s) * BLOCK + lax.broadcasted_iota(jnp.int32, (BLOCK, width), 0)
        m.dy[kept(j)] = jnp.where(slot < length, wide(m.cot[kept(j)]), 0.0)
    for l in (1, 0):
        c = [back_second(l, j) for j in range(2)]
        a = []
        for j in range(2):
            c[j].wait()
            back_feed(l, j)
            a.append(send_partial(e, j, m.dgu, m.wgu[l], dot_rows))
        b0 = send_sum(e, 0, a[0])
        weight_grad(l, D)
        plane_first(l, D)
        b1 = send_sum(e, 1, a[1])
        weight_grad(l, G)
        plane_first(l, G)
        if l == 0:
            plane_second(1, O)
            plane_second(1, Q)
            spread_line(1, D)
        c = [back_first(e, l, j, copy) for j, copy in ((0, b0), (1, b1))]
        e += 1
        for j in range(2):
            c[j].wait()
            back_mix(l, j)
        back_attend(l)
        a = [send_partial(e, j, m.dqkv, m.wq[l], dot_rows) for j in range(2)]
        b0 = send_sum(e, 0, a[0])
        weight_grad(l, O)
        plane_first(l, O)
        b1 = send_sum(e, 1, a[1])
        weight_grad(l, Q)
        plane_first(l, Q)
        plane_second(l, D)
        for j, copy in ((0, b0), (1, b1)):
            result = low(m.dres[kept(j)] + summed(e, j, copy))
            if l == 1:
                m.dy[kept(j)] = wide(result)
            else:
                m.tgb[kept(j)] = result
        plane_second(l, G)
        e += 1
    send_rows(1, m.tgb, tg_ref.at[0, 0], "start")
    for kind in (G, O, Q):
        spread_line(1, kind)

    @pl.when(s == 1)
    def _():
        for kind in (D, G, O, Q):
            finish(kind)
    plane_second(0, O)
    plane_second(0, Q)
    for kind in (D, G, O, Q):
        spread_line(0, kind)

    @pl.when(s == 1)
    def _():
        for kind in (D, G, O, Q):
            finish_half(kind)

    @pl.when(s == 0)
    def _():
        finish(D)
        finish(G)
        finish_half(D)
        finish(O)
        finish_half(G)
        finish(Q)
        finish_half(O)
        finish_half(Q)
    for kind in (D, G, O, Q):
        finish_done(kind)
        for l in (1, 0):
            line_done(l, kind)
    scatter_rows(*tok_args, "wait")
    scatter_rows(*cot_args, "wait")
    send_rows(0, m.outb, out_ref.at[0, 0], "wait")
    send_rows(1, m.tgb, tg_ref.at[0, 0], "wait")


def relay(tokens, lengths, cotangent, w_qkv, w_out, norm1_gain, norm1_bias, w_gate, w_up, w_down, norm2_gain, norm2_bias):
    bf = jnp.bfloat16
    part, width = w_qkv.shape[1], tokens.shape[3]
    hidden = w_gate.shape[2]
    slots = 4 * BLOCK
    cosine, sine = rotary_tables(0, slots)
    sign = jnp.where(jnp.arange(HEAD_DIM) < HEAD_DIM // 2, -1.0, 1.0)
    cosine = jnp.tile(cosine[:, 0], (1, 2))
    sine = jnp.tile(sine[:, 0] * sign, (1, 2))
    query, key, value = jnp.split(w_qkv[0], 3, axis=1)
    heads = (part, 4, 3, HEAD_DIM)
    joined = jnp.stack([query.reshape(heads), key.reshape(heads)], axis=3).reshape(part, 4, 6 * HEAD_DIM)
    norms = jnp.stack([norm1_gain[0], norm1_bias[0], norm2_gain[0], norm2_bias[0]], axis=1)
    norms = jnp.broadcast_to(jnp.pad(norms, ((0, 0), (0, HEAD_DIM - 4)))[:, None], (part, 4, HEAD_DIM))
    packed = jnp.concatenate([joined, value.reshape(part, 4, 3 * HEAD_DIM), norms], axis=2).transpose(1, 0, 2)
    scratch = relay_scratch(width, hidden)
    any_space = pl.BlockSpec(memory_space=pl.ANY)
    fpart = hidden // 4
    outs = pl.pallas_call(
        functools.partial(relay_kernel, tuple(scratch)),
        out_shape=(
            jax.ShapeDtypeStruct(tokens.shape, bf), jax.ShapeDtypeStruct(tokens.shape, bf),
            jax.ShapeDtypeStruct((part, 3 * width + LANES), bf), jax.ShapeDtypeStruct((part, width), bf),
            jax.ShapeDtypeStruct((part, 2 * hidden), bf), jax.ShapeDtypeStruct((fpart, width), bf),
        ),
        in_specs=[pl.BlockSpec(memory_space=pltpu.SMEM)] + [any_space] * 9,
        out_specs=[any_space] * 6,
        scratch_shapes=list(scratch.values()),
        compiler_params=pltpu.CompilerParams(
            collective_id=1, has_side_effects=True, vmem_limit_bytes=VMEM_LIMIT),
    )(lengths, cosine, sine, tokens, cotangent, packed, w_out, w_gate, w_up, w_down)
    output, token_grad, grad_q, grad_out, grad_gu, grad_down = outs
    grad_q, grad_out, grad_gu, grad_down = (grad.astype(jnp.float32) for grad in (grad_q, grad_out, grad_gu, grad_down))
    norms = grad_q[:, 3 * width + NORM_ROW:3 * width + NORM_ROW + 4]
    return (
        output, token_grad, grad_q[None, :, :3 * width], grad_out[None], norms[:, 0][None], norms[:, 1][None],
        grad_gu[None, :, :hidden], grad_gu[None, :, hidden:], grad_down[None], norms[:, 2][None], norms[:, 3][None],
    )


def fits_relay(args):
    tokens, lengths, w_qkv, w_gate, w_down = args[0], args[1], args[3], args[7], args[9]
    axes = tuple(lax.axis_size(axis) for axis in ("section", "fsdp", "rep"))
    return (
        axes == (2, 4, 4)
        and tokens.shape == (1, 1, BLOCK, 768)
        and lengths.shape == (2, 1)
        and w_qkv.shape == (1, 192, 2304)
        and w_gate.shape == (1, 192, 3072)
        and w_down.shape == (1, 768, 768)
    )


def program(*args):
    return relay(*args) if fits_relay(args) else shards(*args)


def solution(mesh):
    return jax.shard_map(
        program,
        mesh=mesh,
        in_specs=(
            P("section", "rep", "fsdp", None),
            P(None, "rep"),
            P("section", "rep", "fsdp", None),
            P("section", "fsdp", None),
            P("section", "fsdp", None),
            P("section", "fsdp"),
            P("section", "fsdp"),
            P("section", "fsdp", None),
            P("section", "fsdp", None),
            P("section", "fsdp", None),
            P("section", "fsdp"),
            P("section", "fsdp"),
        ),
        out_specs=(
            P("section", "rep", "fsdp", None),
            P("section", "rep", "fsdp", None),
            P("section", "fsdp", None),
            P("section", "fsdp", None),
            P("section", "fsdp"),
            P("section", "fsdp"),
            P("section", "fsdp", None),
            P("section", "fsdp", None),
            P("section", "fsdp", None),
            P("section", "fsdp"),
            P("section", "fsdp"),
        ),
        check_vma=False,
    )
```

```python
import functools
import types

import jax
import jax.numpy as jnp
from jax import lax
from jax.experimental import pallas as pl
from jax.experimental.pallas import tpu as pltpu
from jax.sharding import PartitionSpec as P

HEADS = 12
HEAD_DIM = 64


norm_eps = 1e-05
masked_score = -1000000000.0
VMEM_LIMIT = 62 * 2**20


def partner(block, axis, distance):
    count = lax.axis_size(axis)
    route = []
    for low in range(count):
        high = low | 1 << distance
        if high != low and high < count:
            route += [(low, high), (high, low)]
    return lax.ppermute(block, axis, route)


def shifted(value, axis, steps):
    count = lax.axis_size(axis)
    initial, last = (max(0, -steps), min(count, count - steps))
    return lax.ppermute(value, axis, [(source, source + steps) for source in range(initial, last)])


def norm_rows(values, norm_gain, offset):
    centre = values - jnp.mean(values, axis=-1, keepdims=True)
    inverse = lax.rsqrt(jnp.mean(centre * centre, axis=-1, keepdims=True) + norm_eps)
    normed = centre * inverse
    return (normed * norm_gain + offset, normed, inverse)


def norm_back(grad_out, normed, inverse, norm_gain):
    scaled = grad_out * norm_gain
    return inverse * (
        scaled
        - jnp.mean(scaled, axis=-1, keepdims=True)
        - normed * jnp.mean(scaled * normed, axis=-1, keepdims=True)
    )


def rotary_tables(first_slot, row_count):
    half_dim = HEAD_DIM // 2
    inverse_freq = 1000.0 ** (-2.0 * jnp.arange(half_dim, dtype=jnp.float32) / HEAD_DIM)
    places = (first_slot + jnp.arange(row_count)).astype(jnp.float32)
    angles = places[:, None] * inverse_freq[None, :]
    angles = jnp.concatenate([angles, angles], axis=-1)[:, None, :]
    return (jnp.cos(angles), jnp.sin(angles))


def turn_half(values):
    half_dim = values.shape[-1] // 2
    return jnp.concatenate([-values[..., half_dim:], values[..., :half_dim]], axis=-1)


def rotate(values, cosine_table, sine_table):
    return values * cosine_table + turn_half(values) * sine_table


def rotate_back(values, cosine_table, sine_table):
    return values * cosine_table - turn_half(values) * sine_table


def masked_scores(query_rot, key_all, live_keys):
    key_heads = key_all.reshape(key_all.shape[0], HEADS, HEAD_DIM)
    scores = jnp.einsum(
        "qhd,khd->hqk", query_rot, key_heads, preferred_element_type=jnp.float32
    ) * HEAD_DIM ** (-0.5)
    return jnp.where(live_keys[None, None, :], scores, masked_score)


def batch_length(length_column, batch_now):
    picked = jnp.clip(batch_now, 0, length_column.shape[0] - 1)
    return lax.dynamic_index_in_dim(length_column, picked, 0, keepdims=False)


def layer_forward(inputs, weights, live_keys, cosine_table, sine_table):
    w_qkv, w_out, gain_one, offset_one, w_gate, w_up, w_down, gain_two, offset_two = weights
    row_count, model_width = inputs.shape
    head_shape = (row_count, HEADS, HEAD_DIM)
    inputs_low = inputs.astype(jnp.bfloat16)
    joined = jnp.dot(inputs_low, w_qkv, preferred_element_type=jnp.float32)
    query_rot = rotate(
        joined[:, :model_width].reshape(head_shape), cosine_table, sine_table
    ).astype(jnp.bfloat16)
    key_own = (
        rotate(
            joined[:, model_width : 2 * model_width].reshape(head_shape), cosine_table, sine_table
        )
        .reshape(row_count, model_width)
        .astype(jnp.bfloat16)
    )
    value_own = joined[:, 2 * model_width :].astype(jnp.bfloat16)
    key_all, value_all = (
        lax.all_gather(key_own, "fsdp", axis=0, tiled=True),
        lax.all_gather(value_own, "fsdp", axis=0, tiled=True),
    )
    scores = masked_scores(query_rot, key_all, live_keys)
    highest = jnp.max(scores, axis=-1, keepdims=True)
    log_total = highest + jnp.log(jnp.sum(jnp.exp(scores - highest), axis=-1, keepdims=True))
    softmax_weights = jnp.exp(scores - log_total).astype(jnp.bfloat16)
    value_heads = value_all.reshape(value_all.shape[0], HEADS, HEAD_DIM)
    mixed_heads = jnp.einsum(
        "hqk,khd->qhd", softmax_weights, value_heads, preferred_element_type=jnp.float32
    )
    mixed_heads = mixed_heads.reshape(row_count, model_width).astype(jnp.bfloat16)
    attended = jnp.dot(mixed_heads, w_out, preferred_element_type=jnp.float32)
    hidden, normed_one, inverse_one = norm_rows(inputs + attended, gain_one, offset_one)
    hidden_low = hidden.astype(jnp.bfloat16)
    gate_proj = jnp.dot(hidden_low, w_gate, preferred_element_type=jnp.float32)
    upward = jnp.dot(hidden_low, w_up, preferred_element_type=jnp.float32)
    product = (jax.nn.silu(gate_proj) * upward).astype(jnp.bfloat16)
    mlp_out = jnp.dot(product, w_down, preferred_element_type=jnp.float32)
    result, normed_two, inverse_two = norm_rows(hidden + mlp_out, gain_two, offset_two)
    key_saved, value_saved = (key_all, value_all)
    kept_state = (
        inputs_low,
        query_rot,
        key_saved,
        value_saved,
        log_total,
        mixed_heads,
        normed_one,
        inverse_one,
        hidden_low,
        gate_proj,
        upward,
        product,
        normed_two,
        inverse_two,
    )
    return (result, kept_state)


def layer_backward(grad_out, kept_state, weights, live_keys, cosine_table, sine_table):
    w_qkv, w_out, gain_one, offset_one, w_gate, w_up, w_down, gain_two, offset_two = weights
    (
        inputs_low,
        query_rot,
        key_saved,
        value_saved,
        log_total,
        mixed_heads,
        normed_one,
        inverse_one,
        hidden_low,
        gate_proj,
        upward,
        product,
        normed_two,
        inverse_two,
    ) = kept_state
    row_count, model_width = inputs_low.shape
    head_shape = (row_count, HEADS, HEAD_DIM)
    key_all, value_all = (key_saved, value_saved)
    grad_gain_two = jnp.sum(grad_out * normed_two, axis=0)
    grad_offset_two = jnp.sum(grad_out, axis=0)
    grad_second = norm_back(grad_out, normed_two, inverse_two, gain_two)
    grad_fed = grad_second.astype(jnp.bfloat16)
    grad_product = jnp.einsum("rd,fd->rf", grad_fed, w_down, preferred_element_type=jnp.float32)
    grad_w_down = jnp.einsum("rf,rd->fd", product, grad_fed, preferred_element_type=jnp.float32)
    sigmoid_gate = jax.nn.sigmoid(gate_proj)
    silu_gate = gate_proj * sigmoid_gate
    grad_gate = (
        grad_product * upward * sigmoid_gate * (1.0 + gate_proj * (1.0 - sigmoid_gate))
    ).astype(jnp.bfloat16)
    grad_upward = (grad_product * silu_gate).astype(jnp.bfloat16)
    grad_hidden = grad_second + jnp.einsum(
        "rf,df->rd", grad_gate, w_gate, preferred_element_type=jnp.float32
    )
    grad_hidden = grad_hidden + jnp.einsum(
        "rf,df->rd", grad_upward, w_up, preferred_element_type=jnp.float32
    )
    grad_w_gate = jnp.einsum("rd,rf->df", hidden_low, grad_gate, preferred_element_type=jnp.float32)
    grad_w_up = jnp.einsum("rd,rf->df", hidden_low, grad_upward, preferred_element_type=jnp.float32)
    grad_gain_one = jnp.sum(grad_hidden * normed_one, axis=0)
    grad_offset_one = jnp.sum(grad_hidden, axis=0)
    grad_first = norm_back(grad_hidden, normed_one, inverse_one, gain_one)
    grad_attended = grad_first.astype(jnp.bfloat16)
    grad_w_out = jnp.einsum(
        "rd,re->de", mixed_heads, grad_attended, preferred_element_type=jnp.float32
    )
    grad_mixed = (
        jnp.einsum("re,de->rd", grad_attended, w_out, preferred_element_type=jnp.float32)
        .astype(jnp.bfloat16)
        .reshape(head_shape)
    )
    scores = masked_scores(query_rot, key_all, live_keys)
    attention = jnp.exp(scores - log_total)
    key_count = key_all.shape[0]
    key_heads = key_all.reshape(key_count, HEADS, HEAD_DIM)
    value_heads = value_all.reshape(key_count, HEADS, HEAD_DIM)
    grad_attention = jnp.einsum(
        "qhd,khd->hqk", grad_mixed, value_heads, preferred_element_type=jnp.float32
    )
    centre_term = jnp.sum(grad_attention * attention, axis=-1, keepdims=True)
    grad_scores = (attention * (grad_attention - centre_term)).astype(jnp.bfloat16)
    score_scale = HEAD_DIM ** (-0.5)
    grad_query = (
        jnp.einsum("hqk,khd->qhd", grad_scores, key_heads, preferred_element_type=jnp.float32)
        * score_scale
    )
    attention_low = attention.astype(jnp.bfloat16)
    grad_value_all = jnp.einsum(
        "hqk,qhd->khd", attention_low, grad_mixed, preferred_element_type=jnp.float32
    )
    grad_key_all = (
        jnp.einsum("hqk,qhd->khd", grad_scores, query_rot, preferred_element_type=jnp.float32)
        * score_scale
    )
    grad_key, grad_value = (
        lax.psum_scatter(
            grad_key_all.reshape(key_count, model_width).astype(jnp.bfloat16),
            "fsdp",
            scatter_dimension=0,
            tiled=True,
        ).astype(jnp.float32),
        lax.psum_scatter(
            grad_value_all.reshape(key_count, model_width).astype(jnp.bfloat16),
            "fsdp",
            scatter_dimension=0,
            tiled=True,
        ).astype(jnp.float32),
    )
    grad_joined = jnp.concatenate(
        [
            rotate_back(grad_query, cosine_table, sine_table).reshape(row_count, model_width),
            rotate_back(grad_key.reshape(head_shape), cosine_table, sine_table).reshape(
                row_count, model_width
            ),
            grad_value,
        ],
        axis=1,
    ).astype(jnp.bfloat16)
    grad_w_qkv = jnp.einsum(
        "rd,re->de", inputs_low, grad_joined, preferred_element_type=jnp.float32
    )
    grad_inputs = grad_first + jnp.einsum(
        "re,de->rd", grad_joined, w_qkv, preferred_element_type=jnp.float32
    )
    weight_grads = (
        grad_w_qkv,
        grad_w_out,
        grad_gain_one,
        grad_offset_one,
        grad_w_gate,
        grad_w_up,
        grad_w_down,
        grad_gain_two,
        grad_offset_two,
    )
    return (grad_inputs, weight_grads)


def shards(
    tokens,
    lengths,
    cotangent,
    w_qkv,
    w_out,
    norm1_gain,
    norm1_bias,
    w_gate,
    w_up,
    w_down,
    norm2_gain,
    norm2_bias,
):
    section_index = lax.axis_index("section")
    fsdp_index = lax.axis_index("fsdp")
    is_first = section_index == 0
    row_count = tokens.shape[2]
    model_width = tokens.shape[3]
    slot_count = row_count * lax.axis_size("fsdp")
    micro_count = lengths.shape[0]
    weights = (
        lax.all_gather(w_qkv[0], "fsdp", axis=0, tiled=True),
        lax.all_gather(w_out[0], "fsdp", axis=0, tiled=True),
        lax.all_gather(norm1_gain[0], "fsdp", axis=0, tiled=True),
        lax.all_gather(norm1_bias[0], "fsdp", axis=0, tiled=True),
        lax.all_gather(w_gate[0], "fsdp", axis=0, tiled=True),
        lax.all_gather(w_up[0], "fsdp", axis=0, tiled=True),
        lax.all_gather(w_down[0], "fsdp", axis=0, tiled=True),
        lax.all_gather(norm2_gain[0], "fsdp", axis=0, tiled=True),
        lax.all_gather(norm2_bias[0], "fsdp", axis=0, tiled=True),
    )
    own_tokens = tokens[0, 0]
    own_cotangent = cotangent[0, 0]
    arrived = partner(jnp.where(is_first, own_cotangent, own_tokens), "section", 0)
    batch_tokens = [
        jnp.where(is_first, own_tokens, arrived),
        jnp.where(is_first, arrived, own_tokens),
    ]
    batch_cotangents = [
        jnp.where(is_first, own_cotangent, arrived),
        jnp.where(is_first, arrived, own_cotangent),
    ]
    cosine_table, sine_table = rotary_tables(fsdp_index * row_count, row_count)
    row_slots = fsdp_index * row_count + jnp.arange(row_count)
    key_slots = jnp.arange(slot_count)
    length_column = lengths[:, 0]
    empty_rows = jnp.zeros((row_count, model_width), jnp.bfloat16)
    carried = empty_rows
    kept_list = []
    layer_outputs = []
    for tick_index in range(micro_count + 1):
        length_now = batch_length(length_column, tick_index - section_index)
        fresh_rows = batch_tokens[tick_index] if tick_index < micro_count else empty_rows
        inputs = jnp.where(is_first, fresh_rows, carried).astype(jnp.float32)
        result, kept_state = layer_forward(
            inputs, weights, key_slots < length_now, cosine_table, sine_table
        )
        result_low = result.astype(jnp.bfloat16)
        kept_list.append(kept_state)
        layer_outputs.append(result_low)
        if tick_index < micro_count:
            carried = shifted(result_low, "section", 1)
    arriving = empty_rows
    totals = None
    owned_total = None
    input_grads = []
    for tick_index in range(micro_count + 1):
        batch_now = tick_index - 1 + section_index
        length_now = batch_length(length_column, batch_now)
        is_valid = (batch_now >= 0) & (batch_now < micro_count)
        seed_rows = batch_cotangents[tick_index] if tick_index < micro_count else empty_rows
        seed_grad = (
            seed_rows.astype(jnp.float32) * (row_slots < length_now).astype(jnp.float32)[:, None]
        )
        grad_out = jnp.where(
            is_valid, jnp.where(is_first, arriving.astype(jnp.float32), seed_grad), 0.0
        )
        earlier_state = kept_list[max(tick_index - 1, 0)]
        later_state = kept_list[min(tick_index + 1, micro_count)]
        kept_state = jax.tree.map(
            lambda first_arr, second_arr: jnp.where(is_first, first_arr, second_arr),
            earlier_state,
            later_state,
        )
        grad_inputs, weight_grads = layer_backward(
            grad_out, kept_state, weights, key_slots < length_now, cosine_table, sine_table
        )
        grad_low = grad_inputs.astype(jnp.bfloat16)
        input_grads.append(grad_low)
        if tick_index < micro_count:
            arriving = shifted(grad_low, "section", -1)
        totals = weight_grads if totals is None else jax.tree.map(jnp.add, totals, weight_grads)
    shares = (
        lax.psum_scatter(
            totals[0].astype(jnp.bfloat16), "fsdp", scatter_dimension=0, tiled=True
        ).astype(jnp.float32),
        lax.psum_scatter(
            totals[1].astype(jnp.bfloat16), "fsdp", scatter_dimension=0, tiled=True
        ).astype(jnp.float32),
        lax.psum_scatter(
            totals[2].astype(jnp.bfloat16), "fsdp", scatter_dimension=0, tiled=True
        ).astype(jnp.float32),
        lax.psum_scatter(
            totals[3].astype(jnp.bfloat16), "fsdp", scatter_dimension=0, tiled=True
        ).astype(jnp.float32),
        lax.psum_scatter(
            totals[4].astype(jnp.bfloat16), "fsdp", scatter_dimension=0, tiled=True
        ).astype(jnp.float32),
        lax.psum_scatter(
            totals[5].astype(jnp.bfloat16), "fsdp", scatter_dimension=0, tiled=True
        ).astype(jnp.float32),
        lax.psum_scatter(
            totals[6].astype(jnp.bfloat16), "fsdp", scatter_dimension=0, tiled=True
        ).astype(jnp.float32),
        lax.psum_scatter(
            totals[7].astype(jnp.bfloat16), "fsdp", scatter_dimension=0, tiled=True
        ).astype(jnp.float32),
        lax.psum_scatter(
            totals[8].astype(jnp.bfloat16), "fsdp", scatter_dimension=0, tiled=True
        ).astype(jnp.float32),
    )
    owned_total = (
        lax.psum(shares[0].astype(jnp.bfloat16), "rep").astype(jnp.float32),
        lax.psum(shares[1].astype(jnp.bfloat16), "rep").astype(jnp.float32),
        lax.psum(shares[2].astype(jnp.bfloat16), "rep").astype(jnp.float32),
        lax.psum(shares[3].astype(jnp.bfloat16), "rep").astype(jnp.float32),
        lax.psum(shares[4].astype(jnp.bfloat16), "rep").astype(jnp.float32),
        lax.psum(shares[5].astype(jnp.bfloat16), "rep").astype(jnp.float32),
        lax.psum(shares[6].astype(jnp.bfloat16), "rep").astype(jnp.float32),
        lax.psum(shares[7].astype(jnp.bfloat16), "rep").astype(jnp.float32),
        lax.psum(shares[8].astype(jnp.bfloat16), "rep").astype(jnp.float32),
    )
    outgoing = jnp.where(is_first, input_grads[2], layer_outputs[1])
    returned = partner(outgoing, "section", 0)
    output_rows = jnp.where(is_first, returned, layer_outputs[2])
    grad_rows = jnp.where(is_first, input_grads[1], returned)
    return (
        output_rows[None, None],
        grad_rows[None, None],
        owned_total[0][None],
        owned_total[1][None],
        owned_total[2][None],
        owned_total[3][None],
        owned_total[4][None],
        owned_total[5][None],
        owned_total[6][None],
        owned_total[7][None],
        owned_total[8][None],
    )


MESH = pl.DeviceIdType.MESH
BLOCK = 128
LANES = 128
QKV_PAD = 640
NORM_ROW = 64


def dot(left, right):
    return jnp.dot(left, right, preferred_element_type=jnp.float32)


def dot_rows(left, right):
    return lax.dot_general(left, right, (((1,), (1,)), ((), ())), preferred_element_type=jnp.float32)


def dot_cols(left, right):
    return lax.dot_general(left, right, (((0,), (0,)), ((), ())), preferred_element_type=jnp.float32)


def low(value):
    return value.astype(jnp.bfloat16)


def wide(value):
    return value.astype(jnp.float32)


def wait_for(ref, sem):
    pltpu.make_async_copy(ref, ref, sem).wait()


def turned(values):
    lane = lax.broadcasted_iota(jnp.int32, values.shape, 1)
    ahead = pltpu.roll(values, LANES - HEAD_DIM // 2, 1)
    behind = pltpu.roll(values, HEAD_DIM // 2, 1)
    return jnp.where(lane % HEAD_DIM < HEAD_DIM // 2, ahead, behind)


def relay_scratch(width, hidden):
    vm = pltpu.VMEM
    bf, f32 = jnp.bfloat16, jnp.float32
    slots = 4 * BLOCK
    own = 2 * BLOCK
    dma = pltpu.SemaphoreType.DMA
    part = width // 4
    share = part // 4
    fpart = hidden // 4
    fshare = fpart // 4
    return dict(
        wq=vm((2, width, QKV_PAD), bf), wo=vm((2, 256, width), bf), wgu=vm((2, width, 2 * fpart), bf),
        wd=vm((2, fpart, width), bf),
        x=vm((2, slots, width), bf), hid=vm((2, slots, width), bf), dfed=vm((2, slots, width), bf),
        datt=vm((2, slots, width), bf),
        q=vm((2, 3, slots, LANES), bf), k=vm((2, 3, slots, LANES), bf), v=vm((2, slots, 256), bf),
        pr=vm((2, 3, slots, slots), bf), mix=vm((2, slots, 256), bf), gu=vm((2, slots, 2 * fpart), bf),
        act=vm((2, slots, fpart), bf),
        n1=vm((2, own, width), f32), n2=vm((2, own, width), f32),
        i1=vm((2, own, LANES), f32), i2=vm((2, own, LANES), f32),
        dgu=vm((slots, 2 * fpart), bf), dmix=vm((slots, 256), bf), dqkv=vm((slots, QKV_PAD), bf),
        ds=vm((slots, slots), bf), dq=vm((slots, LANES), f32),
        hidf=vm((own, width), f32), dres=vm((own, width), f32), dy=vm((own, width), f32),
        part=vm((2, own, width), f32), cot=vm((own, width), bf), outb=vm((own, width), bf), tgb=vm((own, width), bf),
        sa=vm((2, 2, BLOCK, width), bf), ra=vm((2, 2, BLOCK, width), bf),
        sb=vm((2, 2, BLOCK, width), bf), rb=vm((2, 2, BLOCK, width), bf),
        par=vm((2, LANES, width), f32), ng=vm((2, LANES, width), f32),
        r1q=vm((2, 3, part, QKV_PAD), bf), r1g=vm((2, 3, part, 2 * fpart), bf),
        r1o=vm((2, 3, share, width), bf), r1d=vm((2, 3, fshare, width), bf),
        s2q=vm((2, part, QKV_PAD), bf), s2g=vm((2, part, 2 * fpart), bf),
        s2o=vm((2, share, width), bf), s2d=vm((2, fshare, width), bf),
        r2q=vm((8, share, QKV_PAD), bf), r2g=vm((8, share, 2 * fpart), bf),
        r2o=vm((2, share, width), bf), r2d=vm((2, fshare, width), bf),
        s3q=vm((share, 3 * width + LANES), bf), s3g=vm((share, 2 * hidden), bf),
        cos=vm((slots, LANES), f32), sin=vm((slots, LANES), f32), tab=dma((2,)),
        s3o=vm((share, width), bf), s3d=vm((fshare, width), bf),
        tok_s=dma((2,)), tok_r=dma, cot_s=dma((2,)), cot_r=dma, xc_s=dma((2,)), xc_r=dma((2,)),
        wz=dma((2, 4, 4)), wss=dma((2, 2)), wso=dma((2, 2, 2)), wfs=dma((2, 4)), wrs=dma((2, 4)), wpx=dma((2, 4, 3)), wpy=dma((2, 4, 3)), wpd=dma((2, 4)),
        a_s=dma((2, 2)), a_r=dma((2, 2)), b_s=dma((2, 2)), b_r=dma((2, 2)), c_s=dma((8, 2)), c_r=dma((8, 2)),
        s1s=dma((2, 4)), s1a=dma((2, 4)), s1b=dma((2, 4)), s1t=dma((2, 4)), s1r=dma((2, 4)),
        s2s=dma((2, 4)), s2r=dma((4,)),
        s3s=dma((4, 2)), s3x=dma((4,)), s3y=dma((4,)), s3l=dma((4,)), s3t=dma((4,)), s3e=dma((4,)),
        o_s=dma((2,)), o_r=dma((2,)),
    )


def relay_kernel(names, length_ref, cos_in, sin_in, tok_ref, cot_ref, wq_ref, wo_ref, wg_ref, wu_ref, wd_ref,
                 out_ref, tg_ref, oq_ref, oo_ref, og_ref, od_ref, *scratch):
    m = types.SimpleNamespace(**dict(zip(names, scratch)))
    width = tok_ref.shape[3]
    slots = 4 * BLOCK
    part = width // 4
    share = part // 4
    fpart = wd_ref.shape[1]
    fshare = fpart // 4
    s, z, r = lax.axis_index("section"), lax.axis_index("fsdp"), lax.axis_index("rep")
    zp, zh = z % 2, z // 2
    r0, r1 = r % 2, r // 2
    t = 2 * zp + s
    other = 1 - s

    def mixed(low_bit, high_bit, k):
        a = 1 - low_bit if k & 1 else low_bit
        b = 1 - high_bit if k & 2 else high_bit
        return a + 2 * b

    z_of = [mixed(zp, zh, k) for k in range(4)]
    r_of = [mixed(r0, r1, k) for k in range(4)]
    zp_of = [zp, 1 - zp, zp, 1 - zp]
    across = (other, z, r)
    along = (s, z_of[1], r)

    def remote(src, dst, send, recv, device):
        return pltpu.make_async_remote_copy(
            src_ref=src, dst_ref=dst, send_sem=send, recv_sem=recv, device_id=device, device_id_type=MESH)

    def rows(start, size):
        return pl.ds(pl.multiple_of(start, 16), size)

    barrier = pltpu.get_barrier_semaphore()
    greeted = [(other, z_of[0], r)] + [(c, z_of[k], r) for k in (1, 2, 3) for c in (0, 1)]
    greeted += [(s, z, r_of[k]) for k in (1, 2, 3)]
    for device in greeted:
        pl.semaphore_signal(barrier, inc=1, device_id=device, device_id_type=MESH)
    pl.semaphore_wait(barrier, len(greeted))

    def scatter_rows(src, dst, send, recv, step):
        for i in range(2):
            target = 2 * s + i
            is_self = (target == z) & (s == zp)

            @pl.when(is_self)
            def _():
                if step == "start":
                    pltpu.make_async_copy(src, dst, recv).start()

            @pl.when(jnp.logical_not(is_self))
            def _():
                copy = remote(src, dst, send.at[i], recv, (zp, target, r))
                if step == "start":
                    copy.start()
                else:
                    copy.wait_send()

    tok_args = (tok_ref.at[0, 0], m.x.at[0, rows(z * BLOCK, BLOCK)], m.tok_s, m.tok_r)
    cot_args = (cot_ref.at[0, 0], m.cot.at[rows(zh * BLOCK, BLOCK)], m.cot_s, m.cot_r)

    Q, G, O, D = range(4)
    weight = [m.wq, m.wgu, m.wo, m.wd]
    count = [share, share, share, fshare]

    def source_fan(l, kind):
        for k in range(4):
            size = part if k == 0 else share
            start = 0 if k == 0 else r * share
            here = rows(z * part + start, size)
            for c in range(2):
                target = 2 * zp_of[k] + c
                device = (c, z_of[k], r)
                if kind == Q:
                    pairs = [(wq_ref.at[target, rows(start, size)], m.wq.at[l, here])]
                else:
                    cols = pl.ds(pl.multiple_of(target * fpart, LANES), fpart)
                    pairs = [
                        (wg_ref.at[0, rows(start, size), cols], m.wgu.at[l, here, pl.ds(0, fpart)]),
                        (wu_ref.at[0, rows(start, size), cols], m.wgu.at[l, here, pl.ds(fpart, fpart)]),
                    ]
                for src, dst in pairs:
                    if k == 0 and c == l:
                        pltpu.make_async_copy(src, dst, m.wz.at[l, kind, k]).start()
                    else:
                        remote(src, dst, m.wss.at[l, kind], m.wz.at[l, kind, k], device).start()

    def source_own(l, kind, step):
        ref = wo_ref if kind == O else wd_ref
        n = count[kind]
        for i in range(2):
            target = zh + 2 * i
            own = target == z

            def send(src, dst):
                copy = remote(src, dst, m.wso.at[l, kind - O, i], m.wz.at[l, kind, 0], (zp, target, r))
                if step == "start":
                    copy.start()
                else:
                    copy.wait_send()

            @pl.when(own & (zp == l))
            def _():
                if step == "start":
                    pltpu.make_async_copy(
                        ref.at[0], weight[kind].at[l, pl.ds(0, 4 * n)], m.wz.at[l, kind, 0]).start()

            @pl.when(own & (zp != l))
            def _():
                send(ref.at[0], weight[kind].at[l, pl.ds(0, 4 * n)])

            @pl.when(jnp.logical_not(own))
            def _():
                send(ref.at[0, rows(r * n, n)], weight[kind].at[l, rows(r * n, n)])

    def source(l, kinds):
        @pl.when(s == l)
        def _():
            for kind in kinds:
                if kind in (Q, G):
                    source_fan(l, kind)
                else:
                    source_own(l, kind, "start")

    def source_done(l):
        @pl.when(s == l)
        def _():
            size = 6 * share + part
            wait_for(m.wq.at[l, pl.ds(0, size)], m.wss.at[l, Q])
            wait_for(m.wgu.at[l, pl.ds(0, size)], m.wss.at[l, G])
            source_own(l, O, "wait")
            source_own(l, D, "wait")

    xn, yn = (s, z, r_of[1]), (s, z, r_of[2])
    cut = [3 * LANES, fpart, width // 2, width // 2]

    def halves_of(kind, lanes):
        return pl.ds(0, cut[kind]), pl.ds(cut[kind], lanes - cut[kind])

    def block_rows(kind, k, rep):
        n = count[kind]
        return rows((z_of[k] * part if kind in (Q, G) else 0) + rep * n, n)

    def pass_on(l, kind, k):
        block = weight[kind].at[l, block_rows(kind, k, r)]
        wait_for(block, m.wz.at[l, kind, k if kind in (Q, G) else 0])
        remote(block, block, m.wfs.at[l, kind], m.wpx.at[l, kind, k - 1], xn).start()
        remote(block, block, m.wfs.at[l, kind], m.wpy.at[l, kind, k - 1], yn).start()

    def pass_half(l, kind, k):
        first, second = halves_of(kind, weight[kind].shape[2])
        here = block_rows(kind, k, r_of[1])
        wait_for(weight[kind].at[l, here], m.wpx.at[l, kind, k - 1])
        half = weight[kind].at[l, here, first]
        remote(half, half, m.wrs.at[l, kind], m.wpd.at[l, kind], yn).start()
        here = block_rows(kind, k, r_of[2])
        wait_for(weight[kind].at[l, here], m.wpy.at[l, kind, k - 1])
        half = weight[kind].at[l, here, second]
        remote(half, half, m.wrs.at[l, kind], m.wpd.at[l, kind], xn).start()

    def each_block(kind, step):
        if kind in (Q, G):
            for k in (1, 2, 3):
                step(k)
        else:
            pl.when(t != z)(lambda: step(1))

    def forward(l, kind):
        each_block(kind, lambda k: pass_on(l, kind, k))

    def relay_on(l, kind):
        each_block(kind, lambda k: pass_half(l, kind, k))

    def need(l, kind):
        n = count[kind]
        if kind in (Q, G):
            wait_for(weight[kind].at[l, rows(z * part, part)], m.wz.at[l, kind, 0])
            wait_for(weight[kind].at[l, pl.ds(0, 3 * n)], m.wpd.at[l, kind])
        else:
            @pl.when(t != z)
            def _():
                wait_for(weight[kind].at[l, pl.ds(0, n)], m.wpd.at[l, kind])

            @pl.when(t == z)
            def _():
                wait_for(weight[kind].at[l, pl.ds(0, 4 * n)], m.wz.at[l, kind, 0])

    def forward_done(l, kind):
        n = count[kind]

        def wait(blocks):
            wait_for(weight[kind].at[l, pl.ds(0, 2 * blocks * n)], m.wfs.at[l, kind])
            wait_for(weight[kind].at[l, pl.ds(0, blocks * n)], m.wrs.at[l, kind])

        if kind in (Q, G):
            wait(3)
        else:
            pl.when(t != z)(lambda: wait(1))

    def own_rows(j):
        return rows((2 * j + s) * BLOCK, BLOCK)

    def chunk(j):
        return pl.ds(2 * j * BLOCK, 2 * BLOCK)

    def kept(j):
        return pl.ds(j * BLOCK, BLOCK)

    def send_partial(e, j, left, right, multiply):
        p = e % 2
        m.part[j] = multiply(left[chunk(j)], right)
        m.sa[p, j] = low(m.part[j, rows(other * BLOCK, BLOCK)])
        copy = remote(m.sa.at[p, j], m.ra.at[p, j], m.a_s.at[p, j], m.a_r.at[p, j], across)
        copy.start()
        return copy

    def send_sum(e, j, copy):
        p = e % 2
        copy.wait()
        m.sb[p, j] = low(m.part[j, rows(s * BLOCK, BLOCK)] + wide(m.ra[p, j]))
        copy = remote(m.sb.at[p, j], m.rb.at[p, j], m.b_s.at[p, j], m.b_r.at[p, j], along)
        copy.start()
        return copy

    def summed(e, j, copy):
        p = e % 2
        copy.wait()
        return wide(m.sb[p, j]) + wide(m.rb[p, j])

    def share_rows(e, j, ref):
        block = ref.at[own_rows(j)]
        copy = remote(block, block, m.c_s.at[e, j], m.c_r.at[e, j], across)
        copy.start()
        return copy

    def lanes_of(size, width):
        return lax.broadcasted_iota(jnp.int32, (size, width), 1)

    pairs = 2 * BLOCK
    length = length_ref[zh, 0]
    cos_ref, sin_ref = m.cos, m.sin
    live_keys = lanes_of(pairs, slots) < length
    scale = HEAD_DIM ** (-0.5)

    def param(l, i):
        return m.par[l, pl.ds(NORM_ROW + i, 1), :]

    def read_params(l):
        for i in range(width // LANES):
            cols = pl.ds(i * LANES, LANES)
            m.par[l, :, cols] = jnp.transpose(wide(m.wq[l, cols, pl.ds(QKV_PAD - LANES, LANES)]))

    def project(l, j):
        here = chunk(j)
        joined = dot(m.x[l, here], m.wq[l])
        cosine, sine = cos_ref[here], sin_ref[here]
        for h in range(3):
            values = joined[:, h * LANES:(h + 1) * LANES]
            values = values * cosine + turned(values) * sine
            m.q[l, h, here] = low(jnp.where(lanes_of(pairs, LANES) < HEAD_DIM, values, 0.0))
            m.k[l, h, here] = low(pltpu.roll(values, HEAD_DIM, 1))
        m.v[l, here] = low(jnp.where(lanes_of(pairs, 256) < 3 * HEAD_DIM, joined[:, 3 * LANES:], 0.0))

    def attend(l):
        @pl.loop(0, 2)
        def _(i):
            here = rows(i * pairs, pairs)
            total = jnp.zeros((pairs, 256), jnp.float32)
            for h in range(3):
                scores = dot_rows(m.q[l, h, here], m.k[l, h]) * scale
                scores = jnp.where(live_keys, scores, masked_score)
                top = jnp.max(scores, axis=-1, keepdims=True)
                weights = jnp.exp(scores - top)
                weights = low(weights / jnp.sum(weights, axis=-1, keepdims=True))
                m.pr[l, h, here] = weights
                inside = lanes_of(pairs, 256) // HEAD_DIM == h
                total = jnp.where(inside, dot(weights, m.v[l]), total)
            m.mix[l, here] = low(total)

    def normed(values):
        centre = values - jnp.mean(values, axis=-1, keepdims=True)
        inverse = lax.rsqrt(jnp.mean(centre * centre, axis=-1, keepdims=True) + norm_eps)
        return centre * inverse, inverse

    def finish_attention(e, l, j, copy):
        values = wide(m.x[l, own_rows(j)]) + summed(e, j, copy)
        norm, inverse = normed(values)
        m.n1[l, kept(j)] = norm
        m.i1[l, kept(j)] = jnp.broadcast_to(inverse, (BLOCK, LANES))
        hidden = norm * param(l, 0) + param(l, 1)
        m.hidf[kept(j)] = hidden
        m.hid[l, own_rows(j)] = low(hidden)
        return share_rows(l, j, m.hid.at[l])

    def feed(l, j):
        here = chunk(j)
        rows_in = m.hid[l, here]
        gate = dot(rows_in, m.wgu[l, :, pl.ds(0, fpart)])
        up = dot(rows_in, m.wgu[l, :, pl.ds(fpart, fpart)])
        m.gu[l, here, pl.ds(0, fpart)] = low(gate)
        m.gu[l, here, pl.ds(fpart, fpart)] = low(up)
        m.act[l, here] = low(gate * jax.nn.sigmoid(gate) * up)

    def finish_feed(e, l, j, copy):
        values = m.hidf[kept(j)] + summed(e, j, copy)
        norm, inverse = normed(values)
        m.n2[l, kept(j)] = norm
        m.i2[l, kept(j)] = jnp.broadcast_to(inverse, (BLOCK, LANES))
        result = low(norm * param(l, 2) + param(l, 3))
        if l == 0:
            m.x[1, own_rows(j)] = result
            return share_rows(2, j, m.x.at[1])
        m.outb[kept(j)] = result
        return None

    counts = jnp.where(zp == 0, 1.0, 0.0)

    def add_norm_grads(l, i, dy, norm):
        for k, value in enumerate((dy * norm, dy)):
            at = pl.ds(NORM_ROW + i + k, 1)
            m.ng[l, at, :] += jnp.sum(value, axis=0, keepdims=True) * counts

    def norm_grad(dy, norm, inverse, gain):
        scaled = dy * gain
        return inverse * (
            scaled - jnp.mean(scaled, axis=-1, keepdims=True)
            - norm * jnp.mean(scaled * norm, axis=-1, keepdims=True))

    def back_second(l, j):
        dy = m.dy[kept(j)]
        norm = m.n2[l, kept(j)]
        add_norm_grads(l, 2, dy, norm)
        grad = norm_grad(dy, norm, m.i2[l, kept(j), pl.ds(0, 1)], param(l, 2))
        m.dres[kept(j)] = grad
        m.dfed[l, own_rows(j)] = low(grad)
        return share_rows(3 + l, j, m.dfed.at[l])

    def back_feed(l, j):
        here = chunk(j)
        dact = dot_rows(m.dfed[l, here], m.wd[l])
        gate = wide(m.gu[l, here, pl.ds(0, fpart)])
        up = wide(m.gu[l, here, pl.ds(fpart, fpart)])
        sig = jax.nn.sigmoid(gate)
        m.dgu[here, pl.ds(0, fpart)] = low(dact * up * sig * (1.0 + gate * (1.0 - sig)))
        m.dgu[here, pl.ds(fpart, fpart)] = low(dact * gate * sig)

    def back_first(e, l, j, copy):
        dhidden = m.dres[kept(j)] + summed(e, j, copy)
        norm = m.n1[l, kept(j)]
        add_norm_grads(l, 0, dhidden, norm)
        grad = norm_grad(dhidden, norm, m.i1[l, kept(j), pl.ds(0, 1)], param(l, 0))
        m.dres[kept(j)] = grad
        m.datt[l, own_rows(j)] = low(grad)
        return share_rows(5 + l, j, m.datt.at[l])

    def back_mix(l, j):
        m.dmix[chunk(j)] = low(dot_rows(m.datt[l, chunk(j)], m.wo[l]))

    def back_attend(l):
        for h in range(3):
            @pl.loop(0, 2)
            def _(i):
                here = rows(i * pairs, pairs)
                grad = m.dmix[here]
                grad = jnp.where(lanes_of(pairs, 256) // HEAD_DIM == h, grad, jnp.zeros_like(grad))
                dprobs = dot_rows(grad, m.v[l])
                probs = wide(m.pr[l, h, here])
                centre = jnp.sum(dprobs * probs, axis=-1, keepdims=True)
                dscores = low(probs * (dprobs - centre))
                m.ds[here] = dscores
                m.dq[here] = dot(dscores, m.k[l, h]) * scale

            dkey = dot_cols(m.ds[...], m.q[l, h]) * scale
            values = jnp.where(lanes_of(slots, LANES) < HEAD_DIM, m.dq[...], pltpu.roll(dkey, HEAD_DIM, 1))
            values = values * cos_ref[...] - turned(values) * sin_ref[...]
            m.dqkv[:, pl.ds(h * LANES, LANES)] = low(values)
            dvalue = low(dot_cols(m.pr[l, h], m.dmix[...]))
            before = jnp.zeros_like(dvalue) if h == 0 else m.dqkv[:, pl.ds(3 * LANES, 256)]
            inside = lanes_of(slots, 256) // HEAD_DIM == h
            m.dqkv[:, pl.ds(3 * LANES, 256)] = jnp.where(inside, dvalue, before)

    def weight_grad(l, kind):
        left, right = (
            (m.x.at[l], m.dqkv), (m.hid.at[l], m.dgu), (m.mix.at[l], m.datt.at[l]),
            (m.act.at[l], m.dfed.at[l]),
        )[kind]

        @pl.loop(0, left.shape[1] // pairs)
        def _(i):
            cols = pl.ds(pl.multiple_of(i * pairs, pairs), pairs)
            grad = dot_cols(left[:, cols], right[...])
            if kind == Q:
                tail = grad[:, QKV_PAD - LANES:] + jnp.transpose(m.ng[l, :, cols])
                weight[kind][l, cols, pl.ds(0, QKV_PAD - LANES)] = low(grad[:, :QKV_PAD - LANES])
                weight[kind][l, cols, pl.ds(QKV_PAD - LANES, LANES)] = low(tail)
            else:
                weight[kind][l, cols] = low(grad)

    first_in = [m.r1q, m.r1g, m.r1o, m.r1d]
    second_out = [m.s2q, m.s2g, m.s2o, m.s2d]
    second_in = [m.r2q, m.r2g, m.r2o, m.r2d]
    third_out = [m.s3q, m.s3g, m.s3o, m.s3d]
    final = [oq_ref, og_ref, oo_ref, od_ref]

    def blocks_of(kind):
        return range(4 if kind in (Q, G) else 1)

    def grad_rows(kind, b, rep):
        n = count[kind]
        return rows((b * part if kind in (Q, G) else 0) + rep * n, n)

    def plane_first(l, kind):
        n = count[kind]
        first, second = halves_of(kind, weight[kind].shape[2])
        for b in blocks_of(kind):
            for slot, rep in ((1, r_of[3]), (0, None)):
                for lanes, device, near, sem in ((first, xn, r_of[1], m.s1a), (second, yn, r_of[2], m.s1b)):
                    block = grad_rows(kind, b, near if rep is None else rep)
                    remote(
                        weight[kind].at[l, block, lanes], first_in[kind].at[l, slot, pl.ds(b * n, n), lanes],
                        m.s1s.at[l, kind], sem.at[l, kind], device).start()

    def plane_second(l, kind):
        n = count[kind]
        first, second = halves_of(kind, weight[kind].shape[2])
        for lanes, device, rep, sem in ((first, yn, r_of[2], m.s1a), (second, xn, r_of[1], m.s1b)):
            wait_for(first_in[kind].at[l, pl.ds(0, 2), :, lanes], sem.at[l, kind])
            for b in blocks_of(kind):
                block = grad_rows(kind, b, rep)
                here = pl.ds(b * n, n)
                weight[kind][l, block, lanes] = low(
                    wide(weight[kind][l, block, lanes]) + wide(first_in[kind][l, 1, here, lanes]))
                remote(
                    weight[kind].at[l, block, lanes], first_in[kind].at[l, 2, here, lanes],
                    m.s1t.at[l, kind], m.s1r.at[l, kind], device).start()

    def spread_line(l, kind):
        n = count[kind]
        wait_for(first_in[kind].at[l, 2], m.s1r.at[l, kind])
        for b in blocks_of(kind):
            here = pl.ds(b * n, n)
            total = wide(weight[kind][l, grad_rows(kind, b, r)])
            total += wide(first_in[kind][l, 0, here]) + wide(first_in[kind][l, 2, here])
            second_out[kind][l, here] = low(total)
        if kind in (Q, G):
            slot = 2 * z + s
            for k in range(4):
                src = second_out[kind].at[l, rows(z_of[k] * n, n)]
                dst = second_in[kind].at[slot]
                if k == 0:
                    @pl.when(s == l)
                    def _():
                        pltpu.make_async_copy(src, dst, m.s2r.at[kind]).start()

                    @pl.when(s != l)
                    def _():
                        remote(src, dst, m.s2s.at[l, kind], m.s2r.at[kind], across).start()
                else:
                    remote(src, dst, m.s2s.at[l, kind], m.s2r.at[kind], (l, z_of[k], r)).start()
        else:
            src, dst = second_out[kind].at[l], second_in[kind].at[zh]
            is_self = (t == z) & (s == l)

            @pl.when(is_self)
            def _():
                pltpu.make_async_copy(src, dst, m.s2r.at[kind]).start()

            @pl.when(jnp.logical_not(is_self))
            def _():
                remote(src, dst, m.s2s.at[l, kind], m.s2r.at[kind], (l, t, r)).start()

    def line_done(l, kind):
        wait_for(first_in[kind].at[l, pl.ds(0, 2)], m.s1s.at[l, kind])
        wait_for(first_in[kind].at[l, 2], m.s1t.at[l, kind])
        n = count[kind]
        if kind in (Q, G):
            @pl.when(s == l)
            def _():
                wait_for(second_out[kind].at[l, pl.ds(0, 3 * n)], m.s2s.at[l, kind])

            @pl.when(s != l)
            def _():
                wait_for(second_out[kind].at[l], m.s2s.at[l, kind])
        else:
            @pl.when(jnp.logical_not((t == z) & (s == l)))
            def _():
                wait_for(second_out[kind].at[l], m.s2s.at[l, kind])

    def in_order(parts):
        low_half = lax.broadcasted_iota(jnp.int32, (share, LANES), 1) < HEAD_DIM

        def swapped(values):
            return pltpu.roll(values, HEAD_DIM, 1)

        def pair(head):
            return parts[head // 3][:, head % 3 * LANES:(head % 3 + 1) * LANES]

        def value(head, at_low):
            h = head % 3
            start = 3 * LANES + h // 2 * LANES
            values = parts[head // 3][:, start:start + LANES]
            return values if (h != 1) == at_low else swapped(values)

        for c in range(HEADS // 2):
            even, odd = pair(2 * c), pair(2 * c + 1)
            for i, values in enumerate((
                jnp.where(low_half, even, swapped(odd)), jnp.where(low_half, swapped(even), odd),
                jnp.where(low_half, value(2 * c, True), value(2 * c + 1, False)),
            )):
                m.s3q[:, pl.ds(i * width + c * LANES, LANES)] = low(values)
        norms = sum(values[:, QKV_PAD - LANES:] for values in parts)
        m.s3q[:, pl.ds(3 * width, LANES)] = low(norms)

    def out_cut(kind):
        lanes = third_out[kind].shape[1]
        middle = lanes // 2 // LANES * LANES
        return pl.ds(0, middle), pl.ds(middle, lanes - middle)

    def finish(kind):
        wait_for(second_in[kind], m.s2r.at[kind])
        if kind in (Q, G):
            parts = []
            for b in range(4):
                near = 2 * (b // 2) + b % 2
                parts.append(wide(second_in[kind][near]) + wide(second_in[kind][near + 4]))
                if kind == G:
                    for i in range(2):
                        m.s3g[:, pl.ds((4 * i + b) * fpart, fpart)] = low(parts[b][:, i * fpart:(i + 1) * fpart])
            if kind == Q:
                in_order(parts)
        else:
            third_out[kind][...] = low(wide(second_in[kind][0]) + wide(second_in[kind][1]))
        dst = final[kind].at[rows(r * count[kind], count[kind])]
        remote(third_out[kind], dst, m.s3s.at[kind, 0], m.s3x.at[kind], xn).start()
        remote(third_out[kind], dst, m.s3s.at[kind, 1], m.s3y.at[kind], yn).start()
        pltpu.make_async_copy(third_out[kind], dst, m.s3l.at[kind]).start()

    def finish_half(kind):
        n = count[kind]
        for lanes, rep, device, sem in zip(out_cut(kind), r_of[1:3], (yn, xn), (m.s3x, m.s3y)):
            wait_for(final[kind].at[rows(rep * n, n)], sem.at[kind])
            half = final[kind].at[rows(rep * n, n), lanes]
            remote(half, half, m.s3t.at[kind], m.s3e.at[kind], device).start()

    def finish_done(kind):
        block = final[kind].at[pl.ds(0, count[kind])]
        wait_for(block, m.s3l.at[kind])
        wait_for(block, m.s3e.at[kind])
        wait_for(third_out[kind], m.s3s.at[kind, 0])
        wait_for(third_out[kind], m.s3s.at[kind, 1])
        wait_for(block, m.s3t.at[kind])

    def send_rows(i, src, dst, step):
        block = src.at[rows(zp * BLOCK, BLOCK)]
        is_self = (zh == s) & (t == z)

        @pl.when(is_self)
        def _():
            if step == "start":
                pltpu.make_async_copy(block, dst, m.o_r.at[i]).start()

        @pl.when(jnp.logical_not(is_self))
        def _():
            copy = remote(block, dst, m.o_s.at[i], m.o_r.at[i], (zh, t, r))
            if step == "start":
                copy.start()
            else:
                copy.wait_send()

        if step == "wait":
            wait_for(dst, m.o_r.at[i])

    source(0, (Q,))
    scatter_rows(*tok_args, "start")
    source(0, (O, G, D))
    tables = [pltpu.make_async_copy(src, dst, m.tab.at[i]) for i, (src, dst) in enumerate(((cos_in, m.cos), (sin_in, m.sin)))]
    for copy in tables:
        copy.start()
    for l in range(2):
        m.wo[l, pl.ds(part, 256 - part)] = jnp.zeros((256 - part, width), jnp.bfloat16)
        m.ng[l] = jnp.zeros((LANES, width), jnp.float32)
    forward(0, Q)
    wait_for(m.x.at[0, pl.ds(0, 2 * BLOCK)], m.tok_r)
    halves = []
    for j in range(2):
        block = m.x.at[0, own_rows(j)]
        copy = remote(block, block, m.xc_s.at[j], m.xc_r.at[j], across)
        copy.start()
        halves.append(copy)
    relay_on(0, Q)
    forward(0, O)
    for copy in tables:
        copy.wait()
    need(0, Q)
    read_params(0)
    relay_on(0, O)
    pass_on(0, G, 1)
    for j in range(2):
        halves[j].wait()
        project(0, j)
    pass_on(0, G, 2)
    attend(0)
    pass_on(0, G, 3)
    source(1, (Q, O))
    need(0, O)
    a = [send_partial(0, j, m.mix.at[0], m.wo[0], dot) for j in range(2)]
    b = [send_sum(0, j, a[j]) for j in range(2)]
    source(1, (G,))
    relay_on(0, G)
    forward(0, D)
    c = [finish_attention(0, 0, 0, b[0])]
    need(0, G)
    c[0].wait()
    feed(0, 0)
    c.append(finish_attention(0, 0, 1, b[1]))
    relay_on(0, D)
    forward(1, Q)
    forward(1, O)
    c[1].wait()
    feed(0, 1)
    need(0, D)
    a = [send_partial(1, j, m.act.at[0], m.wd[0], dot) for j in range(2)]
    b = [send_sum(1, j, a[j]) for j in range(2)]
    source(1, (D,))
    scatter_rows(*cot_args, "start")
    relay_on(1, Q)
    relay_on(1, O)
    forward(1, G)
    need(1, Q)
    read_params(1)
    for j in range(2):
        finish_feed(1, 0, j, b[j]).wait()
        project(1, j)
    attend(1)
    relay_on(1, G)
    need(1, O)
    a = [send_partial(2, j, m.mix.at[1], m.wo[1], dot) for j in range(2)]
    b = [send_sum(2, j, a[j]) for j in range(2)]
    forward(1, D)
    c = [finish_attention(2, 1, 0, b[0])]
    need(1, G)
    c[0].wait()
    feed(1, 0)
    c.append(finish_attention(2, 1, 1, b[1]))
    relay_on(1, D)
    c[1].wait()
    feed(1, 1)
    need(1, D)
    a = [send_partial(3, j, m.act.at[1], m.wd[1], dot) for j in range(2)]
    b = [send_sum(3, j, a[j]) for j in range(2)]
    for j in range(2):
        finish_feed(3, 1, j, b[j])
    e = 4
    send_rows(0, m.outb, out_ref.at[0, 0], "start")
    for l in range(2):
        source_done(l)
        for kind in (Q, O, G, D):
            forward_done(l, kind)
    wait_for(m.cot, m.cot_r)
    for j in range(2):
        slot = (2 * j + s) * BLOCK + lax.broadcasted_iota(jnp.int32, (BLOCK, width), 0)
        m.dy[kept(j)] = jnp.where(slot < length, wide(m.cot[kept(j)]), 0.0)
    for l in (1, 0):
        c = [back_second(l, j) for j in range(2)]
        a = []
        for j in range(2):
            c[j].wait()
            back_feed(l, j)
            if j == 1:
                b = [send_sum(e, 0, a[0])]
            a.append(send_partial(e, j, m.dgu, m.wgu[l], dot_rows))
        weight_grad(l, D)
        plane_first(l, D)
        b.append(send_sum(e, 1, a[1]))
        weight_grad(l, G)
        plane_first(l, G)
        if l == 0:
            spread_line(1, D)
            spread_line(1, G)
            plane_second(1, O)
            plane_second(1, Q)
        c = [back_first(e, l, j, b[j]) for j in range(2)]
        plane_second(l, D)
        e += 1
        for j in range(2):
            c[j].wait()
            back_mix(l, j)
        back_attend(l)
        a = [send_partial(e, j, m.dqkv, m.wq[l], dot_rows) for j in range(2)]
        b = [send_sum(e, 0, a[0])]
        weight_grad(l, O)
        plane_first(l, O)
        b.append(send_sum(e, 1, a[1]))
        weight_grad(l, Q)
        plane_first(l, Q)
        plane_second(l, G)
        if l == 0:
            spread_line(1, O)
            spread_line(1, Q)
            @pl.when(s == 1)
            def _():
                finish(D)
                finish(G)

        for j in range(2):
            result = low(m.dres[kept(j)] + summed(e, j, b[j]))
            if l == 1:
                m.dy[kept(j)] = wide(result)
            else:
                m.tgb[kept(j)] = result
        e += 1
    send_rows(1, m.tgb, tg_ref.at[0, 0], "start")
    spread_line(0, G)
    spread_line(0, D)
    plane_second(0, O)
    plane_second(0, Q)

    @pl.when(s == 1)
    def _():
        finish_half(D)
        finish_half(G)
        finish(O)
        finish(Q)

    spread_line(0, O)
    spread_line(0, Q)

    @pl.when(s == 1)
    def _():
        finish_half(O)
        finish_half(Q)

    @pl.when(s == 0)
    def _():
        finish(G)
        finish(D)
        finish_half(G)
        finish(O)
        finish_half(D)
        finish(Q)
        finish_half(O)
        finish_half(Q)
    for kind in (D, G, O, Q):
        finish_done(kind)
        for l in (1, 0):
            line_done(l, kind)
    scatter_rows(*tok_args, "wait")
    scatter_rows(*cot_args, "wait")
    send_rows(0, m.outb, out_ref.at[0, 0], "wait")
    send_rows(1, m.tgb, tg_ref.at[0, 0], "wait")


def relay(tokens, lengths, cotangent, w_qkv, w_out, norm1_gain, norm1_bias, w_gate, w_up, w_down, norm2_gain, norm2_bias):
    bf = jnp.bfloat16
    part, width = w_qkv.shape[1], tokens.shape[3]
    hidden = w_gate.shape[2]
    slots = 4 * BLOCK
    cosine, sine = rotary_tables(0, slots)
    sign = jnp.where(jnp.arange(HEAD_DIM) < HEAD_DIM // 2, -1.0, 1.0)
    cosine = jnp.tile(cosine[:, 0], (1, 2))
    sine = jnp.tile(sine[:, 0] * sign, (1, 2))
    query, key, value = jnp.split(w_qkv[0], 3, axis=1)
    heads = (part, 4, 3, HEAD_DIM)
    joined = jnp.stack([query.reshape(heads), key.reshape(heads)], axis=3).reshape(part, 4, 6 * HEAD_DIM)
    norms = jnp.stack([norm1_gain[0], norm1_bias[0], norm2_gain[0], norm2_bias[0]], axis=1)
    norms = jnp.broadcast_to(jnp.pad(norms, ((0, 0), (0, HEAD_DIM - 4)))[:, None], (part, 4, HEAD_DIM))
    packed = jnp.concatenate([joined, value.reshape(part, 4, 3 * HEAD_DIM), norms], axis=2).transpose(1, 0, 2)
    scratch = relay_scratch(width, hidden)
    any_space = pl.BlockSpec(memory_space=pl.ANY)
    fpart = hidden // 4
    outs = pl.pallas_call(
        functools.partial(relay_kernel, tuple(scratch)),
        out_shape=(
            jax.ShapeDtypeStruct(tokens.shape, bf), jax.ShapeDtypeStruct(tokens.shape, bf),
            jax.ShapeDtypeStruct((part, 3 * width + LANES), bf), jax.ShapeDtypeStruct((part, width), bf),
            jax.ShapeDtypeStruct((part, 2 * hidden), bf), jax.ShapeDtypeStruct((fpart, width), bf),
        ),
        in_specs=[pl.BlockSpec(memory_space=pltpu.SMEM)] + [any_space] * 9,
        out_specs=[any_space] * 6,
        scratch_shapes=list(scratch.values()),
        compiler_params=pltpu.CompilerParams(
            collective_id=1, has_side_effects=True, vmem_limit_bytes=VMEM_LIMIT),
    )(lengths, cosine, sine, tokens, cotangent, packed, w_out, w_gate, w_up, w_down)
    output, token_grad, grad_q, grad_out, grad_gu, grad_down = outs
    grad_q, grad_out, grad_gu, grad_down = (grad.astype(jnp.float32) for grad in (grad_q, grad_out, grad_gu, grad_down))
    norms = grad_q[:, 3 * width + NORM_ROW:3 * width + NORM_ROW + 4]
    return (
        output, token_grad, grad_q[None, :, :3 * width], grad_out[None], norms[:, 0][None], norms[:, 1][None],
        grad_gu[None, :, :hidden], grad_gu[None, :, hidden:], grad_down[None], norms[:, 2][None], norms[:, 3][None],
    )


def fits_relay(args):
    tokens, lengths, w_qkv, w_gate, w_down = args[0], args[1], args[3], args[7], args[9]
    axes = tuple(lax.axis_size(axis) for axis in ("section", "fsdp", "rep"))
    return (
        axes == (2, 4, 4)
        and tokens.shape == (1, 1, BLOCK, 768)
        and lengths.shape == (2, 1)
        and w_qkv.shape == (1, 192, 2304)
        and w_gate.shape == (1, 192, 3072)
        and w_down.shape == (1, 768, 768)
    )


def program(*args):
    return relay(*args) if fits_relay(args) else shards(*args)


def solution(mesh):
    return jax.shard_map(
        program,
        mesh=mesh,
        in_specs=(
            P("section", "rep", "fsdp", None),
            P(None, "rep"),
            P("section", "rep", "fsdp", None),
            P("section", "fsdp", None),
            P("section", "fsdp", None),
            P("section", "fsdp"),
            P("section", "fsdp"),
            P("section", "fsdp", None),
            P("section", "fsdp", None),
            P("section", "fsdp", None),
            P("section", "fsdp"),
            P("section", "fsdp"),
        ),
        out_specs=(
            P("section", "rep", "fsdp", None),
            P("section", "rep", "fsdp", None),
            P("section", "fsdp", None),
            P("section", "fsdp", None),
            P("section", "fsdp"),
            P("section", "fsdp"),
            P("section", "fsdp", None),
            P("section", "fsdp", None),
            P("section", "fsdp", None),
            P("section", "fsdp"),
            P("section", "fsdp"),
        ),
        check_vma=False,
    )
```

```python
import functools
import math
import types

import jax
import jax.numpy as jnp
from jax import lax
from jax.experimental import pallas as pl
from jax.experimental.pallas import tpu as pltpu
from jax.sharding import PartitionSpec as P

HEADS = 12
HEAD_DIM = 64


norm_eps = 1e-05
masked_score = -1000000000.0
VMEM_LIMIT = 62 * 2**20


def partner(block, axis, distance):
    count = lax.axis_size(axis)
    route = []
    for low in range(count):
        high = low | 1 << distance
        if high != low and high < count:
            route += [(low, high), (high, low)]
    return lax.ppermute(block, axis, route)


def shifted(value, axis, steps):
    count = lax.axis_size(axis)
    initial, last = (max(0, -steps), min(count, count - steps))
    return lax.ppermute(value, axis, [(source, source + steps) for source in range(initial, last)])


def norm_rows(values, norm_gain, offset):
    centre = values - jnp.mean(values, axis=-1, keepdims=True)
    inverse = lax.rsqrt(jnp.mean(centre * centre, axis=-1, keepdims=True) + norm_eps)
    normed = centre * inverse
    return (normed * norm_gain + offset, normed, inverse)


def norm_back(grad_out, normed, inverse, norm_gain):
    scaled = grad_out * norm_gain
    return inverse * (
        scaled
        - jnp.mean(scaled, axis=-1, keepdims=True)
        - normed * jnp.mean(scaled * normed, axis=-1, keepdims=True)
    )


def rotary_tables(first_slot, row_count):
    half_dim = HEAD_DIM // 2
    inverse_freq = 1000.0 ** (-2.0 * jnp.arange(half_dim, dtype=jnp.float32) / HEAD_DIM)
    places = (first_slot + jnp.arange(row_count)).astype(jnp.float32)
    angles = places[:, None] * inverse_freq[None, :]
    angles = jnp.concatenate([angles, angles], axis=-1)[:, None, :]
    return (jnp.cos(angles), jnp.sin(angles))


def turn_half(values):
    half_dim = values.shape[-1] // 2
    return jnp.concatenate([-values[..., half_dim:], values[..., :half_dim]], axis=-1)


def rotate(values, cosine_table, sine_table):
    return values * cosine_table + turn_half(values) * sine_table


def rotate_back(values, cosine_table, sine_table):
    return values * cosine_table - turn_half(values) * sine_table


def masked_scores(query_rot, key_all, live_keys):
    key_heads = key_all.reshape(key_all.shape[0], HEADS, HEAD_DIM)
    scores = jnp.einsum(
        "qhd,khd->hqk", query_rot, key_heads, preferred_element_type=jnp.float32
    ) * HEAD_DIM ** (-0.5)
    return jnp.where(live_keys[None, None, :], scores, masked_score)


def batch_length(length_column, batch_now):
    picked = jnp.clip(batch_now, 0, length_column.shape[0] - 1)
    return lax.dynamic_index_in_dim(length_column, picked, 0, keepdims=False)


def layer_forward(inputs, weights, live_keys, cosine_table, sine_table):
    w_qkv, w_out, gain_one, offset_one, w_gate, w_up, w_down, gain_two, offset_two = weights
    row_count, model_width = inputs.shape
    head_shape = (row_count, HEADS, HEAD_DIM)
    inputs_low = inputs.astype(jnp.bfloat16)
    joined = jnp.dot(inputs_low, w_qkv, preferred_element_type=jnp.float32)
    query_rot = rotate(
        joined[:, :model_width].reshape(head_shape), cosine_table, sine_table
    ).astype(jnp.bfloat16)
    key_own = (
        rotate(
            joined[:, model_width : 2 * model_width].reshape(head_shape), cosine_table, sine_table
        )
        .reshape(row_count, model_width)
        .astype(jnp.bfloat16)
    )
    value_own = joined[:, 2 * model_width :].astype(jnp.bfloat16)
    key_all, value_all = (
        lax.all_gather(key_own, "fsdp", axis=0, tiled=True),
        lax.all_gather(value_own, "fsdp", axis=0, tiled=True),
    )
    scores = masked_scores(query_rot, key_all, live_keys)
    highest = jnp.max(scores, axis=-1, keepdims=True)
    log_total = highest + jnp.log(jnp.sum(jnp.exp(scores - highest), axis=-1, keepdims=True))
    softmax_weights = jnp.exp(scores - log_total).astype(jnp.bfloat16)
    value_heads = value_all.reshape(value_all.shape[0], HEADS, HEAD_DIM)
    mixed_heads = jnp.einsum(
        "hqk,khd->qhd", softmax_weights, value_heads, preferred_element_type=jnp.float32
    )
    mixed_heads = mixed_heads.reshape(row_count, model_width).astype(jnp.bfloat16)
    attended = jnp.dot(mixed_heads, w_out, preferred_element_type=jnp.float32)
    hidden, normed_one, inverse_one = norm_rows(inputs + attended, gain_one, offset_one)
    hidden_low = hidden.astype(jnp.bfloat16)
    gate_proj = jnp.dot(hidden_low, w_gate, preferred_element_type=jnp.float32)
    upward = jnp.dot(hidden_low, w_up, preferred_element_type=jnp.float32)
    product = (jax.nn.silu(gate_proj) * upward).astype(jnp.bfloat16)
    mlp_out = jnp.dot(product, w_down, preferred_element_type=jnp.float32)
    result, normed_two, inverse_two = norm_rows(hidden + mlp_out, gain_two, offset_two)
    key_saved, value_saved = (key_all, value_all)
    kept_state = (
        inputs_low,
        query_rot,
        key_saved,
        value_saved,
        log_total,
        mixed_heads,
        normed_one,
        inverse_one,
        hidden_low,
        gate_proj,
        upward,
        product,
        normed_two,
        inverse_two,
    )
    return (result, kept_state)


def layer_backward(grad_out, kept_state, weights, live_keys, cosine_table, sine_table):
    w_qkv, w_out, gain_one, offset_one, w_gate, w_up, w_down, gain_two, offset_two = weights
    (
        inputs_low,
        query_rot,
        key_saved,
        value_saved,
        log_total,
        mixed_heads,
        normed_one,
        inverse_one,
        hidden_low,
        gate_proj,
        upward,
        product,
        normed_two,
        inverse_two,
    ) = kept_state
    row_count, model_width = inputs_low.shape
    head_shape = (row_count, HEADS, HEAD_DIM)
    key_all, value_all = (key_saved, value_saved)
    grad_gain_two = jnp.sum(grad_out * normed_two, axis=0)
    grad_offset_two = jnp.sum(grad_out, axis=0)
    grad_second = norm_back(grad_out, normed_two, inverse_two, gain_two)
    grad_fed = grad_second.astype(jnp.bfloat16)
    grad_product = jnp.einsum("rd,fd->rf", grad_fed, w_down, preferred_element_type=jnp.float32)
    grad_w_down = jnp.einsum("rf,rd->fd", product, grad_fed, preferred_element_type=jnp.float32)
    sigmoid_gate = jax.nn.sigmoid(gate_proj)
    silu_gate = gate_proj * sigmoid_gate
    grad_gate = (
        grad_product * upward * sigmoid_gate * (1.0 + gate_proj * (1.0 - sigmoid_gate))
    ).astype(jnp.bfloat16)
    grad_upward = (grad_product * silu_gate).astype(jnp.bfloat16)
    grad_hidden = grad_second + jnp.einsum(
        "rf,df->rd", grad_gate, w_gate, preferred_element_type=jnp.float32
    )
    grad_hidden = grad_hidden + jnp.einsum(
        "rf,df->rd", grad_upward, w_up, preferred_element_type=jnp.float32
    )
    grad_w_gate = jnp.einsum("rd,rf->df", hidden_low, grad_gate, preferred_element_type=jnp.float32)
    grad_w_up = jnp.einsum("rd,rf->df", hidden_low, grad_upward, preferred_element_type=jnp.float32)
    grad_gain_one = jnp.sum(grad_hidden * normed_one, axis=0)
    grad_offset_one = jnp.sum(grad_hidden, axis=0)
    grad_first = norm_back(grad_hidden, normed_one, inverse_one, gain_one)
    grad_attended = grad_first.astype(jnp.bfloat16)
    grad_w_out = jnp.einsum(
        "rd,re->de", mixed_heads, grad_attended, preferred_element_type=jnp.float32
    )
    grad_mixed = (
        jnp.einsum("re,de->rd", grad_attended, w_out, preferred_element_type=jnp.float32)
        .astype(jnp.bfloat16)
        .reshape(head_shape)
    )
    scores = masked_scores(query_rot, key_all, live_keys)
    attention = jnp.exp(scores - log_total)
    key_count = key_all.shape[0]
    key_heads = key_all.reshape(key_count, HEADS, HEAD_DIM)
    value_heads = value_all.reshape(key_count, HEADS, HEAD_DIM)
    grad_attention = jnp.einsum(
        "qhd,khd->hqk", grad_mixed, value_heads, preferred_element_type=jnp.float32
    )
    centre_term = jnp.sum(grad_attention * attention, axis=-1, keepdims=True)
    grad_scores = (attention * (grad_attention - centre_term)).astype(jnp.bfloat16)
    score_scale = HEAD_DIM ** (-0.5)
    grad_query = (
        jnp.einsum("hqk,khd->qhd", grad_scores, key_heads, preferred_element_type=jnp.float32)
        * score_scale
    )
    attention_low = attention.astype(jnp.bfloat16)
    grad_value_all = jnp.einsum(
        "hqk,qhd->khd", attention_low, grad_mixed, preferred_element_type=jnp.float32
    )
    grad_key_all = (
        jnp.einsum("hqk,qhd->khd", grad_scores, query_rot, preferred_element_type=jnp.float32)
        * score_scale
    )
    grad_key, grad_value = (
        lax.psum_scatter(
            grad_key_all.reshape(key_count, model_width).astype(jnp.bfloat16),
            "fsdp",
            scatter_dimension=0,
            tiled=True,
        ).astype(jnp.float32),
        lax.psum_scatter(
            grad_value_all.reshape(key_count, model_width).astype(jnp.bfloat16),
            "fsdp",
            scatter_dimension=0,
            tiled=True,
        ).astype(jnp.float32),
    )
    grad_joined = jnp.concatenate(
        [
            rotate_back(grad_query, cosine_table, sine_table).reshape(row_count, model_width),
            rotate_back(grad_key.reshape(head_shape), cosine_table, sine_table).reshape(
                row_count, model_width
            ),
            grad_value,
        ],
        axis=1,
    ).astype(jnp.bfloat16)
    grad_w_qkv = jnp.einsum(
        "rd,re->de", inputs_low, grad_joined, preferred_element_type=jnp.float32
    )
    grad_inputs = grad_first + jnp.einsum(
        "re,de->rd", grad_joined, w_qkv, preferred_element_type=jnp.float32
    )
    weight_grads = (
        grad_w_qkv,
        grad_w_out,
        grad_gain_one,
        grad_offset_one,
        grad_w_gate,
        grad_w_up,
        grad_w_down,
        grad_gain_two,
        grad_offset_two,
    )
    return (grad_inputs, weight_grads)


def shards(
    tokens,
    lengths,
    cotangent,
    w_qkv,
    w_out,
    norm1_gain,
    norm1_bias,
    w_gate,
    w_up,
    w_down,
    norm2_gain,
    norm2_bias,
):
    section_index = lax.axis_index("section")
    fsdp_index = lax.axis_index("fsdp")
    is_first = section_index == 0
    row_count = tokens.shape[2]
    model_width = tokens.shape[3]
    slot_count = row_count * lax.axis_size("fsdp")
    micro_count = lengths.shape[0]
    weights = (
        lax.all_gather(w_qkv[0], "fsdp", axis=0, tiled=True),
        lax.all_gather(w_out[0], "fsdp", axis=0, tiled=True),
        lax.all_gather(norm1_gain[0], "fsdp", axis=0, tiled=True),
        lax.all_gather(norm1_bias[0], "fsdp", axis=0, tiled=True),
        lax.all_gather(w_gate[0], "fsdp", axis=0, tiled=True),
        lax.all_gather(w_up[0], "fsdp", axis=0, tiled=True),
        lax.all_gather(w_down[0], "fsdp", axis=0, tiled=True),
        lax.all_gather(norm2_gain[0], "fsdp", axis=0, tiled=True),
        lax.all_gather(norm2_bias[0], "fsdp", axis=0, tiled=True),
    )
    own_tokens = tokens[0, 0]
    own_cotangent = cotangent[0, 0]
    arrived = partner(jnp.where(is_first, own_cotangent, own_tokens), "section", 0)
    batch_tokens = [
        jnp.where(is_first, own_tokens, arrived),
        jnp.where(is_first, arrived, own_tokens),
    ]
    batch_cotangents = [
        jnp.where(is_first, own_cotangent, arrived),
        jnp.where(is_first, arrived, own_cotangent),
    ]
    cosine_table, sine_table = rotary_tables(fsdp_index * row_count, row_count)
    row_slots = fsdp_index * row_count + jnp.arange(row_count)
    key_slots = jnp.arange(slot_count)
    length_column = lengths[:, 0]
    empty_rows = jnp.zeros((row_count, model_width), jnp.bfloat16)
    carried = empty_rows
    kept_list = []
    layer_outputs = []
    for tick_index in range(micro_count + 1):
        length_now = batch_length(length_column, tick_index - section_index)
        fresh_rows = batch_tokens[tick_index] if tick_index < micro_count else empty_rows
        inputs = jnp.where(is_first, fresh_rows, carried).astype(jnp.float32)
        result, kept_state = layer_forward(
            inputs, weights, key_slots < length_now, cosine_table, sine_table
        )
        result_low = result.astype(jnp.bfloat16)
        kept_list.append(kept_state)
        layer_outputs.append(result_low)
        if tick_index < micro_count:
            carried = shifted(result_low, "section", 1)
    arriving = empty_rows
    totals = None
    owned_total = None
    input_grads = []
    for tick_index in range(micro_count + 1):
        batch_now = tick_index - 1 + section_index
        length_now = batch_length(length_column, batch_now)
        is_valid = (batch_now >= 0) & (batch_now < micro_count)
        seed_rows = batch_cotangents[tick_index] if tick_index < micro_count else empty_rows
        seed_grad = (
            seed_rows.astype(jnp.float32) * (row_slots < length_now).astype(jnp.float32)[:, None]
        )
        grad_out = jnp.where(
            is_valid, jnp.where(is_first, arriving.astype(jnp.float32), seed_grad), 0.0
        )
        earlier_state = kept_list[max(tick_index - 1, 0)]
        later_state = kept_list[min(tick_index + 1, micro_count)]
        kept_state = jax.tree.map(
            lambda first_arr, second_arr: jnp.where(is_first, first_arr, second_arr),
            earlier_state,
            later_state,
        )
        grad_inputs, weight_grads = layer_backward(
            grad_out, kept_state, weights, key_slots < length_now, cosine_table, sine_table
        )
        grad_low = grad_inputs.astype(jnp.bfloat16)
        input_grads.append(grad_low)
        if tick_index < micro_count:
            arriving = shifted(grad_low, "section", -1)
        totals = weight_grads if totals is None else jax.tree.map(jnp.add, totals, weight_grads)
    shares = (
        lax.psum_scatter(
            totals[0].astype(jnp.bfloat16), "fsdp", scatter_dimension=0, tiled=True
        ).astype(jnp.float32),
        lax.psum_scatter(
            totals[1].astype(jnp.bfloat16), "fsdp", scatter_dimension=0, tiled=True
        ).astype(jnp.float32),
        lax.psum_scatter(
            totals[2].astype(jnp.bfloat16), "fsdp", scatter_dimension=0, tiled=True
        ).astype(jnp.float32),
        lax.psum_scatter(
            totals[3].astype(jnp.bfloat16), "fsdp", scatter_dimension=0, tiled=True
        ).astype(jnp.float32),
        lax.psum_scatter(
            totals[4].astype(jnp.bfloat16), "fsdp", scatter_dimension=0, tiled=True
        ).astype(jnp.float32),
        lax.psum_scatter(
            totals[5].astype(jnp.bfloat16), "fsdp", scatter_dimension=0, tiled=True
        ).astype(jnp.float32),
        lax.psum_scatter(
            totals[6].astype(jnp.bfloat16), "fsdp", scatter_dimension=0, tiled=True
        ).astype(jnp.float32),
        lax.psum_scatter(
            totals[7].astype(jnp.bfloat16), "fsdp", scatter_dimension=0, tiled=True
        ).astype(jnp.float32),
        lax.psum_scatter(
            totals[8].astype(jnp.bfloat16), "fsdp", scatter_dimension=0, tiled=True
        ).astype(jnp.float32),
    )
    owned_total = (
        lax.psum(shares[0].astype(jnp.bfloat16), "rep").astype(jnp.float32),
        lax.psum(shares[1].astype(jnp.bfloat16), "rep").astype(jnp.float32),
        lax.psum(shares[2].astype(jnp.bfloat16), "rep").astype(jnp.float32),
        lax.psum(shares[3].astype(jnp.bfloat16), "rep").astype(jnp.float32),
        lax.psum(shares[4].astype(jnp.bfloat16), "rep").astype(jnp.float32),
        lax.psum(shares[5].astype(jnp.bfloat16), "rep").astype(jnp.float32),
        lax.psum(shares[6].astype(jnp.bfloat16), "rep").astype(jnp.float32),
        lax.psum(shares[7].astype(jnp.bfloat16), "rep").astype(jnp.float32),
        lax.psum(shares[8].astype(jnp.bfloat16), "rep").astype(jnp.float32),
    )
    outgoing = jnp.where(is_first, input_grads[2], layer_outputs[1])
    returned = partner(outgoing, "section", 0)
    output_rows = jnp.where(is_first, returned, layer_outputs[2])
    grad_rows = jnp.where(is_first, input_grads[1], returned)
    return (
        output_rows[None, None],
        grad_rows[None, None],
        owned_total[0][None],
        owned_total[1][None],
        owned_total[2][None],
        owned_total[3][None],
        owned_total[4][None],
        owned_total[5][None],
        owned_total[6][None],
        owned_total[7][None],
        owned_total[8][None],
    )


MESH = pl.DeviceIdType.MESH
BLOCK = 128
LANES = 128
QKV_PAD = 640
NORM_ROW = 64


def dot(left, right):
    return jnp.dot(left, right, preferred_element_type=jnp.float32)


def dot_rows(left, right):
    return lax.dot_general(left, right, (((1,), (1,)), ((), ())), preferred_element_type=jnp.float32)


def dot_cols(left, right):
    return lax.dot_general(left, right, (((0,), (0,)), ((), ())), preferred_element_type=jnp.float32)


def low(value):
    return value.astype(jnp.bfloat16)


def wide(value):
    return value.astype(jnp.float32)


def wait_for(ref, sem):
    pltpu.make_async_copy(ref, ref, sem).wait()


def turned(values):
    lane = lax.broadcasted_iota(jnp.int32, values.shape, 1)
    ahead = pltpu.roll(values, LANES - HEAD_DIM // 2, 1)
    behind = pltpu.roll(values, HEAD_DIM // 2, 1)
    return jnp.where(lane % HEAD_DIM < HEAD_DIM // 2, ahead, behind)


def relay_scratch(width, hidden):
    vm = pltpu.VMEM
    bf, f32 = jnp.bfloat16, jnp.float32
    slots = 4 * BLOCK
    own = 2 * BLOCK
    dma = pltpu.SemaphoreType.DMA
    part = width // 4
    share = part // 4
    fpart = hidden // 4
    fshare = fpart // 4
    return dict(
        wq=vm((2, width, QKV_PAD), bf), wo=vm((2, 256, width), bf), wgu=vm((2, width, 2 * fpart), bf),
        wd=vm((2, fpart, width), bf),
        x=vm((2, slots, width), bf), hid=vm((2, slots, width), bf), dfed=vm((2, slots, width), bf),
        datt=vm((2, slots, width), bf),
        q=vm((2, 3, slots, LANES), bf), k=vm((2, 3, slots, LANES), bf), v=vm((2, slots, 256), bf),
        pr=vm((2, 3, slots, slots), bf), mix=vm((2, slots, 256), bf), gu=vm((2, slots, 2 * fpart), bf),
        act=vm((2, slots, fpart), bf),
        n1=vm((2, own, width), f32), n2=vm((2, own, width), f32),
        i1=vm((2, own, LANES), f32), i2=vm((2, own, LANES), f32),
        dgu=vm((slots, 2 * fpart), bf), dmix=vm((slots, 256), bf), dqkv=vm((slots, QKV_PAD), bf),
        ds=vm((slots, slots), bf), dq=vm((slots, LANES), f32),
        hidf=vm((own, width), f32), dres=vm((own, width), f32), dy=vm((own, width), f32),
        part=vm((2, own, width), f32), cot=vm((own, width), bf), outb=vm((own, width), bf), tgb=vm((own, width), bf),
        sa=vm((2, 2, BLOCK, width), bf), ra=vm((2, 2, BLOCK, width), bf),
        sb=vm((2, 2, BLOCK, width), bf), rb=vm((2, 2, BLOCK, width), bf),
        par=vm((2, LANES, width), f32), ng=vm((2, LANES, width), f32),
        r1q=vm((2, 3, part, QKV_PAD), bf), r1g=vm((2, 3, part, 2 * fpart), bf),
        r1o=vm((2, 3, share, width), bf), r1d=vm((2, 3, fshare, width), bf),
        s2q=vm((2, part, QKV_PAD), bf), s2g=vm((2, part, 2 * fpart), bf),
        s2o=vm((2, share, width), bf), s2d=vm((2, fshare, width), bf),
        r2q=vm((8, share, QKV_PAD), bf), r2g=vm((8, share, 2 * fpart), bf),
        r2o=vm((2, share, width), bf), r2d=vm((2, fshare, width), bf),
        qraw=vm((part, 3 * width), bf), qpk=vm((4, part, QKV_PAD), bf), aux=vm((LANES, part), f32), raw=dma,
        s3q=vm((share, 3 * width + LANES), bf), s3g=vm((share, 2 * hidden), bf),
        cos=vm((slots, LANES), f32), sin=vm((slots, LANES), f32),
        s3o=vm((share, width), bf), s3d=vm((fshare, width), bf),
        tok_s=dma((1,)), tok_r=dma, cot_s=dma((1,)), cot_r=dma, xc_s=dma((2,)), xc_r=dma((2,)), tz_s=dma((2,)), tz_r=dma((2,)),
        wz=dma((2, 4, 4)), wss=dma((2, 2)), wso=dma((2, 2, 2)), wfs=dma((2, 4)), wrs=dma((2, 4)), wpx=dma((2, 4, 3)), wpy=dma((2, 4, 3)), wpd=dma((2, 4)),
        a_s=dma((2, 2)), a_r=dma((2, 2)), b_s=dma((2, 2)), b_r=dma((2, 2)), c_s=dma((8, 2)), c_r=dma((8, 2)),
        s1s=dma((2, 4)), s1a=dma((2, 4)), s1b=dma((2, 4)), s1t=dma((2, 4)), s1r=dma((2, 4)),
        s2s=dma((2, 4)), s2r=dma((4,)),
        s3s=dma((4, 2)), s3x=dma((4,)), s3y=dma((4,)), s3l=dma((4,)), s3t=dma((4,)), s3e=dma((4,)),
        o_s=dma((2,)), o_r=dma((2,)),
    )


def relay_kernel(names, length_ref, g1_ref, b1_ref, g2_ref, b2_ref, tok_ref, cot_ref, wq_ref, wo_ref, wg_ref, wu_ref, wd_ref,
                 out_ref, tg_ref, oq_ref, oo_ref, og_ref, od_ref, *scratch):
    m = types.SimpleNamespace(**dict(zip(names, scratch)))
    width = tok_ref.shape[3]
    slots = 4 * BLOCK
    part = width // 4
    share = part // 4
    fpart = wd_ref.shape[1]
    fshare = fpart // 4
    s, z, r = lax.axis_index("section"), lax.axis_index("fsdp"), lax.axis_index("rep")
    zp, zh = z % 2, z // 2
    r0, r1 = r % 2, r // 2
    t = 2 * zp + s
    other = 1 - s

    def mixed(low_bit, high_bit, k):
        a = 1 - low_bit if k & 1 else low_bit
        b = 1 - high_bit if k & 2 else high_bit
        return a + 2 * b

    z_of = [mixed(zp, zh, k) for k in range(4)]
    r_of = [mixed(r0, r1, k) for k in range(4)]
    zp_of = [zp, 1 - zp, zp, 1 - zp]
    across = (other, z, r)
    along = (s, z_of[1], r)

    def remote(src, dst, send, recv, device):
        return pltpu.make_async_remote_copy(
            src_ref=src, dst_ref=dst, send_sem=send, recv_sem=recv, device_id=device, device_id_type=MESH)

    def rows(start, size):
        return pl.ds(pl.multiple_of(start, 16), size)

    barrier = pltpu.get_barrier_semaphore()
    greeted = [(other, z_of[0], r)] + [(c, z_of[k], r) for k in (1, 2, 3) for c in (0, 1)]
    greeted += [(s, z, r_of[k]) for k in (1, 2, 3)]
    for device in greeted:
        pl.semaphore_signal(barrier, inc=1, device_id=device, device_id_type=MESH)
    pl.semaphore_wait(barrier, len(greeted))

    home = (zp, 2 * s + zh, r)
    at_home = (zp == s) & (2 * s + zh == z)

    def scatter_rows(src, dst, send, recv, step):
        @pl.when(at_home)
        def _():
            if step == "start":
                pltpu.make_async_copy(src, dst, recv).start()

        @pl.when(jnp.logical_not(at_home))
        def _():
            copy = remote(src, dst, send.at[0], recv, home)
            if step == "start":
                copy.start()
            else:
                copy.wait_send()

    near_block, far_block = rows(t * BLOCK, BLOCK), rows((2 * (1 - zp) + s) * BLOCK, BLOCK)
    tok_args = (tok_ref.at[0, 0], m.x.at[0, rows(z * BLOCK, BLOCK)], m.tok_s, m.tok_r)
    cot_args = (cot_ref.at[0, 0], m.cot.at[rows(zh * BLOCK, BLOCK)], m.cot_s, m.cot_r)

    Q, G, O, D = range(4)
    weight = [m.wq, m.wgu, m.wo, m.wd]
    count = [share, share, share, fshare]
    pieces = 3

    def source_fan(l, kind):
        for k in range(4):
            size = part if k == 0 else share
            start = 0 if k == 0 else r * share
            here = rows(z * part + start, size)
            for c in range(2):
                target = 2 * zp_of[k] + c
                device = (c, z_of[k], r)
                if kind == Q:
                    pairs = [(m.qpk.at[target, rows(start, size)], m.wq.at[l, here])]
                else:
                    cols = pl.ds(pl.multiple_of(target * fpart, LANES), fpart)
                    pairs = [
                        (wg_ref.at[0, rows(start, size), cols], m.wgu.at[l, here, pl.ds(0, fpart)]),
                        (wu_ref.at[0, rows(start, size), cols], m.wgu.at[l, here, pl.ds(fpart, fpart)]),
                    ]
                for src, dst in pairs:
                    if k == 0 and c == l:
                        pltpu.make_async_copy(src, dst, m.wz.at[l, kind, k]).start()
                    else:
                        remote(src, dst, m.wss.at[l, kind], m.wz.at[l, kind, k], device).start()

    def blocks_in(kind):
        return pieces if kind == D else 1

    def piece_rows(kind, b, rep):
        n = count[kind]
        size = n // blocks_in(kind)
        return rows(rep * n + b * size, size)

    def source_own(l, kind, step):
        ref = wo_ref if kind == O else wd_ref
        n = count[kind]
        for i in range(2):
            target = zh + 2 * i
            own = target == z

            def send(src, dst):
                copy = remote(src, dst, m.wso.at[l, kind - O, i], m.wz.at[l, kind, 3], (zp, target, r))
                if step == "start":
                    copy.start()
                else:
                    copy.wait_send()

            @pl.when(own & (zp == l))
            def _():
                if step == "start":
                    pltpu.make_async_copy(
                        ref.at[0], weight[kind].at[l, pl.ds(0, 4 * n)], m.wz.at[l, kind, 3]).start()

            @pl.when(own & (zp != l))
            def _():
                send(ref.at[0], weight[kind].at[l, pl.ds(0, 4 * n)])

            @pl.when(jnp.logical_not(own))
            def _():
                if step == "start":
                    for b in range(blocks_in(kind)):
                        part_rows = piece_rows(kind, b, r)
                        remote(
                            ref.at[0, part_rows], weight[kind].at[l, part_rows], m.wso.at[l, kind - O, i],
                            m.wz.at[l, kind, b], (zp, target, r)).start()
                else:
                    wait_for(weight[kind].at[l, pl.ds(0, n)], m.wso.at[l, kind - O, i])

    def source(l, kinds):
        @pl.when(s == l)
        def _():
            for kind in kinds:
                if kind in (Q, G):
                    source_fan(l, kind)
                else:
                    source_own(l, kind, "start")

    def source_done(l):
        @pl.when(s == l)
        def _():
            size = 6 * share + part
            wait_for(m.wq.at[l, pl.ds(0, size)], m.wss.at[l, Q])
            wait_for(m.wgu.at[l, pl.ds(0, size)], m.wss.at[l, G])
            source_own(l, O, "wait")
            source_own(l, D, "wait")

    xn, yn = (s, z, r_of[1]), (s, z, r_of[2])
    cut = [3 * LANES, fpart, width // 2, width // 2]

    def halves_of(kind, lanes):
        return pl.ds(0, cut[kind]), pl.ds(cut[kind], lanes - cut[kind])

    def block_rows(kind, k, rep):
        if kind in (Q, G):
            return rows(z_of[k] * part + rep * share, share)
        return piece_rows(kind, k - 1, rep)

    def pass_on(l, kind, k):
        block = weight[kind].at[l, block_rows(kind, k, r)]
        wait_for(block, m.wz.at[l, kind, k if kind in (Q, G) else k - 1])
        remote(block, block, m.wfs.at[l, kind], m.wpx.at[l, kind, k - 1], xn).start()
        remote(block, block, m.wfs.at[l, kind], m.wpy.at[l, kind, k - 1], yn).start()

    def pass_half(l, kind, k):
        first, second = halves_of(kind, weight[kind].shape[2])
        here = block_rows(kind, k, r_of[1])
        wait_for(weight[kind].at[l, here], m.wpx.at[l, kind, k - 1])
        half = weight[kind].at[l, here, first]
        remote(half, half, m.wrs.at[l, kind], m.wpd.at[l, kind], yn).start()
        here = block_rows(kind, k, r_of[2])
        wait_for(weight[kind].at[l, here], m.wpy.at[l, kind, k - 1])
        half = weight[kind].at[l, here, second]
        remote(half, half, m.wrs.at[l, kind], m.wpd.at[l, kind], xn).start()

    def need(l, kind):
        n = count[kind]
        if kind in (Q, G):
            wait_for(weight[kind].at[l, rows(z * part, part)], m.wz.at[l, kind, 0])
            wait_for(weight[kind].at[l, pl.ds(0, 3 * n)], m.wpd.at[l, kind])
        else:
            @pl.when(t != z)
            def _():
                wait_for(weight[kind].at[l, pl.ds(0, n)], m.wpd.at[l, kind])

            @pl.when(t == z)
            def _():
                wait_for(weight[kind].at[l, pl.ds(0, 4 * n)], m.wz.at[l, kind, 3])

    def forward_done(l, kind):
        n = count[kind]

        def wait(blocks):
            wait_for(weight[kind].at[l, pl.ds(0, 2 * blocks * n)], m.wfs.at[l, kind])
            wait_for(weight[kind].at[l, pl.ds(0, blocks * n)], m.wrs.at[l, kind])

        if kind in (Q, G):
            wait(3)
        else:
            pl.when(t != z)(lambda: wait(1))

    def own_rows(j):
        return rows((2 * j + s) * BLOCK, BLOCK)

    def chunk(j):
        return pl.ds(2 * j * BLOCK, 2 * BLOCK)

    def kept(j):
        return pl.ds(j * BLOCK, BLOCK)

    def send_partial(e, j, left, right, multiply):
        p = e % 2
        m.part[j] = multiply(left[chunk(j)], right)
        m.sa[p, j] = low(m.part[j, rows(other * BLOCK, BLOCK)])
        copy = remote(m.sa.at[p, j], m.ra.at[p, j], m.a_s.at[p, j], m.a_r.at[p, j], across)
        copy.start()
        return copy

    def send_sum(e, j, copy):
        p = e % 2
        copy.wait()
        m.sb[p, j] = low(m.part[j, rows(s * BLOCK, BLOCK)] + wide(m.ra[p, j]))
        copy = remote(m.sb.at[p, j], m.rb.at[p, j], m.b_s.at[p, j], m.b_r.at[p, j], along)
        copy.start()
        return copy

    def summed(e, j, copy):
        p = e % 2
        copy.wait()
        return wide(m.sb[p, j]) + wide(m.rb[p, j])

    def share_rows(e, j, ref):
        block = ref.at[own_rows(j)]
        copy = remote(block, block, m.c_s.at[e, j], m.c_r.at[e, j], across)
        copy.start()
        return copy

    def lanes_of(size, width):
        return lax.broadcasted_iota(jnp.int32, (size, width), 1)

    pairs = 2 * BLOCK
    length = jnp.where(zh == 0, length_ref[0:1, 0:1], length_ref[1:2, 0:1])
    cos_ref, sin_ref = m.cos, m.sin
    live_keys = lanes_of(pairs, slots) < length
    scale = HEAD_DIM ** (-0.5)

    def make_tables():
        lane = lanes_of(slots, LANES) % (HEAD_DIM // 2)
        freq = jnp.exp(wide(lane) * (-2.0 / HEAD_DIM * math.log(1000.0)))
        angle = wide(lax.broadcasted_iota(jnp.int32, (slots, LANES), 0)) * freq
        sine = jnp.sin(angle)
        m.cos[...] = jnp.cos(angle)
        m.sin[...] = jnp.where(lanes_of(slots, LANES) % HEAD_DIM < HEAD_DIM // 2, -sine, sine)

    def param(l, i):
        return m.par[l, pl.ds(NORM_ROW + i, 1), :]

    def read_params(l):
        for i in range(width // LANES):
            cols = pl.ds(i * LANES, LANES)
            m.par[l, :, cols] = jnp.transpose(wide(m.wq[l, cols, pl.ds(QKV_PAD - LANES, LANES)]))

    def project(l, j):
        here = chunk(j)
        joined = dot(m.x[l, here], m.wq[l])
        cosine, sine = cos_ref[here], sin_ref[here]
        for h in range(3):
            values = joined[:, h * LANES:(h + 1) * LANES]
            values = values * cosine + turned(values) * sine
            m.q[l, h, here] = low(jnp.where(lanes_of(pairs, LANES) < HEAD_DIM, values, 0.0))
            m.k[l, h, here] = low(pltpu.roll(values, HEAD_DIM, 1))
        m.v[l, here] = low(jnp.where(lanes_of(pairs, 256) < 3 * HEAD_DIM, joined[:, 3 * LANES:], 0.0))

    def attend(l, j):
        here = chunk(j)
        total = jnp.zeros((pairs, 256), jnp.float32)
        for h in range(3):
            scores = dot_rows(m.q[l, h, here], m.k[l, h]) * scale
            scores = jnp.where(live_keys, scores, masked_score)
            top = jnp.max(scores, axis=-1, keepdims=True)
            weights = jnp.exp(scores - top)
            weights = low(weights / jnp.sum(weights, axis=-1, keepdims=True))
            m.pr[l, h, here] = weights
            inside = lanes_of(pairs, 256) // HEAD_DIM == h
            total = jnp.where(inside, dot(weights, m.v[l]), total)
        m.mix[l, here] = low(total)

    def normed(values):
        centre = values - jnp.mean(values, axis=-1, keepdims=True)
        inverse = lax.rsqrt(jnp.mean(centre * centre, axis=-1, keepdims=True) + norm_eps)
        return centre * inverse, inverse

    def finish_attention(e, l, j, copy):
        values = wide(m.x[l, own_rows(j)]) + summed(e, j, copy)
        norm, inverse = normed(values)
        m.n1[l, kept(j)] = norm
        m.i1[l, kept(j)] = jnp.broadcast_to(inverse, (BLOCK, LANES))
        hidden = norm * param(l, 0) + param(l, 1)
        m.hidf[kept(j)] = hidden
        m.hid[l, own_rows(j)] = low(hidden)
        return share_rows(l, j, m.hid.at[l])

    def feed(l, j):
        here = chunk(j)
        rows_in = m.hid[l, here]
        gate = dot(rows_in, m.wgu[l, :, pl.ds(0, fpart)])
        up = dot(rows_in, m.wgu[l, :, pl.ds(fpart, fpart)])
        m.gu[l, here, pl.ds(0, fpart)] = low(gate)
        m.gu[l, here, pl.ds(fpart, fpart)] = low(up)
        m.act[l, here] = low(gate * jax.nn.sigmoid(gate) * up)

    def finish_feed(e, l, j, copy):
        values = m.hidf[kept(j)] + summed(e, j, copy)
        norm, inverse = normed(values)
        m.n2[l, kept(j)] = norm
        m.i2[l, kept(j)] = jnp.broadcast_to(inverse, (BLOCK, LANES))
        result = low(norm * param(l, 2) + param(l, 3))
        if l == 0:
            m.x[1, own_rows(j)] = result
            return share_rows(2, j, m.x.at[1])
        m.outb[kept(j)] = result
        return None

    counts = jnp.where(zp == 0, 1.0, 0.0)

    def add_norm_grads(l, i, dy, norm):
        for k, value in enumerate((dy * norm, dy)):
            at = pl.ds(NORM_ROW + i + k, 1)
            m.ng[l, at, :] += jnp.sum(value, axis=0, keepdims=True) * counts

    def norm_grad(dy, norm, inverse, gain):
        scaled = dy * gain
        return inverse * (
            scaled - jnp.mean(scaled, axis=-1, keepdims=True)
            - norm * jnp.mean(scaled * norm, axis=-1, keepdims=True))

    def back_second(l, j):
        dy = m.dy[kept(j)]
        norm = m.n2[l, kept(j)]
        add_norm_grads(l, 2, dy, norm)
        grad = norm_grad(dy, norm, m.i2[l, kept(j), pl.ds(0, 1)], param(l, 2))
        m.dres[kept(j)] = grad
        m.dfed[l, own_rows(j)] = low(grad)
        return share_rows(3 + l, j, m.dfed.at[l])

    def back_feed(l, j):
        here = chunk(j)
        dact = dot_rows(m.dfed[l, here], m.wd[l])
        gate = wide(m.gu[l, here, pl.ds(0, fpart)])
        up = wide(m.gu[l, here, pl.ds(fpart, fpart)])
        sig = jax.nn.sigmoid(gate)
        m.dgu[here, pl.ds(0, fpart)] = low(dact * up * sig * (1.0 + gate * (1.0 - sig)))
        m.dgu[here, pl.ds(fpart, fpart)] = low(dact * gate * sig)

    def back_first(e, l, j, copy):
        dhidden = m.dres[kept(j)] + summed(e, j, copy)
        norm = m.n1[l, kept(j)]
        add_norm_grads(l, 0, dhidden, norm)
        grad = norm_grad(dhidden, norm, m.i1[l, kept(j), pl.ds(0, 1)], param(l, 0))
        m.dres[kept(j)] = grad
        m.datt[l, own_rows(j)] = low(grad)
        return share_rows(5 + l, j, m.datt.at[l])

    def back_mix(l, j):
        m.dmix[chunk(j)] = low(dot_rows(m.datt[l, chunk(j)], m.wo[l]))

    def back_attend(l, h):
        @pl.loop(0, 2)
        def _(i):
            here = rows(i * pairs, pairs)
            grad = m.dmix[here]
            grad = jnp.where(lanes_of(pairs, 256) // HEAD_DIM == h, grad, jnp.zeros_like(grad))
            dprobs = dot_rows(grad, m.v[l])
            probs = wide(m.pr[l, h, here])
            centre = jnp.sum(dprobs * probs, axis=-1, keepdims=True)
            dscores = low(probs * (dprobs - centre))
            m.ds[here] = dscores
            m.dq[here] = dot(dscores, m.k[l, h]) * scale

        dkey = dot_cols(m.ds[...], m.q[l, h]) * scale
        values = jnp.where(lanes_of(slots, LANES) < HEAD_DIM, m.dq[...], pltpu.roll(dkey, HEAD_DIM, 1))
        values = values * cos_ref[...] - turned(values) * sin_ref[...]
        m.dqkv[:, pl.ds(h * LANES, LANES)] = low(values)
        dvalue = low(dot_cols(m.pr[l, h], m.dmix[...]))
        before = jnp.zeros_like(dvalue) if h == 0 else m.dqkv[:, pl.ds(3 * LANES, 256)]
        inside = lanes_of(slots, 256) // HEAD_DIM == h
        m.dqkv[:, pl.ds(3 * LANES, 256)] = jnp.where(inside, dvalue, before)

    def weight_grad(l, kind):
        left, right = (
            (m.x.at[l], m.dqkv), (m.hid.at[l], m.dgu), (m.mix.at[l], m.datt.at[l]),
            (m.act.at[l], m.dfed.at[l]),
        )[kind]

        @pl.loop(0, left.shape[1] // pairs)
        def _(i):
            cols = pl.ds(pl.multiple_of(i * pairs, pairs), pairs)
            grad = dot_cols(left[:, cols], right[...])
            if kind == Q:
                tail = grad[:, QKV_PAD - LANES:] + jnp.transpose(m.ng[l, :, cols])
                weight[kind][l, cols, pl.ds(0, QKV_PAD - LANES)] = low(grad[:, :QKV_PAD - LANES])
                weight[kind][l, cols, pl.ds(QKV_PAD - LANES, LANES)] = low(tail)
            else:
                weight[kind][l, cols] = low(grad)

    first_in = [m.r1q, m.r1g, m.r1o, m.r1d]
    second_out = [m.s2q, m.s2g, m.s2o, m.s2d]
    second_in = [m.r2q, m.r2g, m.r2o, m.r2d]
    third_out = [m.s3q, m.s3g, m.s3o, m.s3d]
    final = [oq_ref, og_ref, oo_ref, od_ref]

    def blocks_of(kind):
        return range(4 if kind in (Q, G) else 1)

    def grad_rows(kind, b, rep):
        n = count[kind]
        return rows((b * part if kind in (Q, G) else 0) + rep * n, n)

    def plane_first(l, kind):
        n = count[kind]
        first, second = halves_of(kind, weight[kind].shape[2])
        for b in blocks_of(kind):
            for slot, rep in ((1, r_of[3]), (0, None)):
                for lanes, device, near, sem in ((first, xn, r_of[1], m.s1a), (second, yn, r_of[2], m.s1b)):
                    block = grad_rows(kind, b, near if rep is None else rep)
                    remote(
                        weight[kind].at[l, block, lanes], first_in[kind].at[l, slot, pl.ds(b * n, n), lanes],
                        m.s1s.at[l, kind], sem.at[l, kind], device).start()

    def plane_second(l, kind):
        n = count[kind]
        first, second = halves_of(kind, weight[kind].shape[2])
        for lanes, device, rep, sem in ((first, yn, r_of[2], m.s1a), (second, xn, r_of[1], m.s1b)):
            wait_for(first_in[kind].at[l, pl.ds(0, 2), :, lanes], sem.at[l, kind])
            for b in blocks_of(kind):
                block = grad_rows(kind, b, rep)
                here = pl.ds(b * n, n)
                weight[kind][l, block, lanes] = low(
                    wide(weight[kind][l, block, lanes]) + wide(first_in[kind][l, 1, here, lanes]))
                remote(
                    weight[kind].at[l, block, lanes], first_in[kind].at[l, 2, here, lanes],
                    m.s1t.at[l, kind], m.s1r.at[l, kind], device).start()

    def spread_line(l, kind):
        n = count[kind]
        wait_for(first_in[kind].at[l, 2], m.s1r.at[l, kind])
        for b in blocks_of(kind):
            here = pl.ds(b * n, n)
            total = wide(weight[kind][l, grad_rows(kind, b, r)])
            total += wide(first_in[kind][l, 0, here]) + wide(first_in[kind][l, 2, here])
            second_out[kind][l, here] = low(total)
        if kind in (Q, G):
            slot = 2 * z + s
            for k in range(4):
                src = second_out[kind].at[l, rows(z_of[k] * n, n)]
                dst = second_in[kind].at[slot]
                if k == 0:
                    @pl.when(s == l)
                    def _():
                        pltpu.make_async_copy(src, dst, m.s2r.at[kind]).start()

                    @pl.when(s != l)
                    def _():
                        remote(src, dst, m.s2s.at[l, kind], m.s2r.at[kind], across).start()
                else:
                    remote(src, dst, m.s2s.at[l, kind], m.s2r.at[kind], (l, z_of[k], r)).start()
        else:
            src, dst = second_out[kind].at[l], second_in[kind].at[zh]
            is_self = (t == z) & (s == l)

            @pl.when(is_self)
            def _():
                pltpu.make_async_copy(src, dst, m.s2r.at[kind]).start()

            @pl.when(jnp.logical_not(is_self))
            def _():
                remote(src, dst, m.s2s.at[l, kind], m.s2r.at[kind], (l, t, r)).start()

    def line_done(l, kind):
        wait_for(first_in[kind].at[l, pl.ds(0, 2)], m.s1s.at[l, kind])
        wait_for(first_in[kind].at[l, 2], m.s1t.at[l, kind])
        n = count[kind]
        if kind in (Q, G):
            @pl.when(s == l)
            def _():
                wait_for(second_out[kind].at[l, pl.ds(0, 3 * n)], m.s2s.at[l, kind])

            @pl.when(s != l)
            def _():
                wait_for(second_out[kind].at[l], m.s2s.at[l, kind])
        else:
            @pl.when(jnp.logical_not((t == z) & (s == l)))
            def _():
                wait_for(second_out[kind].at[l], m.s2s.at[l, kind])

    def in_order(parts):
        low_half = lax.broadcasted_iota(jnp.int32, (share, LANES), 1) < HEAD_DIM

        def swapped(values):
            return pltpu.roll(values, HEAD_DIM, 1)

        def pair(head):
            return parts[head // 3][:, head % 3 * LANES:(head % 3 + 1) * LANES]

        def value(head, at_low):
            h = head % 3
            start = 3 * LANES + h // 2 * LANES
            values = parts[head // 3][:, start:start + LANES]
            return values if (h != 1) == at_low else swapped(values)

        for c in range(HEADS // 2):
            even, odd = pair(2 * c), pair(2 * c + 1)
            for i, values in enumerate((
                jnp.where(low_half, even, swapped(odd)), jnp.where(low_half, swapped(even), odd),
                jnp.where(low_half, value(2 * c, True), value(2 * c + 1, False)),
            )):
                m.s3q[:, pl.ds(i * width + c * LANES, LANES)] = low(values)
        norms = sum(values[:, QKV_PAD - LANES:] for values in parts)
        m.s3q[:, pl.ds(3 * width, LANES)] = low(norms)

    def out_cut(kind):
        lanes = third_out[kind].shape[1]
        middle = lanes // 2 // LANES * LANES
        return pl.ds(0, middle), pl.ds(middle, lanes - middle)

    def finish(kind):
        wait_for(second_in[kind], m.s2r.at[kind])
        if kind in (Q, G):
            parts = []
            for b in range(4):
                near = 2 * (b // 2) + b % 2
                parts.append(wide(second_in[kind][near]) + wide(second_in[kind][near + 4]))
                if kind == G:
                    for i in range(2):
                        m.s3g[:, pl.ds((4 * i + b) * fpart, fpart)] = low(parts[b][:, i * fpart:(i + 1) * fpart])
            if kind == Q:
                in_order(parts)
        else:
            third_out[kind][...] = low(wide(second_in[kind][0]) + wide(second_in[kind][1]))
        dst = final[kind].at[rows(r * count[kind], count[kind])]
        remote(third_out[kind], dst, m.s3s.at[kind, 0], m.s3x.at[kind], xn).start()
        remote(third_out[kind], dst, m.s3s.at[kind, 1], m.s3y.at[kind], yn).start()
        pltpu.make_async_copy(third_out[kind], dst, m.s3l.at[kind]).start()

    def finish_half(kind):
        n = count[kind]
        for lanes, rep, device, sem in zip(out_cut(kind), r_of[1:3], (yn, xn), (m.s3x, m.s3y)):
            wait_for(final[kind].at[rows(rep * n, n)], sem.at[kind])
            half = final[kind].at[rows(rep * n, n), lanes]
            remote(half, half, m.s3t.at[kind], m.s3e.at[kind], device).start()

    def finish_done(kind):
        block = final[kind].at[pl.ds(0, count[kind])]
        wait_for(block, m.s3l.at[kind])
        wait_for(block, m.s3e.at[kind])
        wait_for(third_out[kind], m.s3s.at[kind, 0])
        wait_for(third_out[kind], m.s3s.at[kind, 1])
        wait_for(block, m.s3t.at[kind])

    def send_rows(i, src, dst, step):
        block = src.at[rows(zp * BLOCK, BLOCK)]
        is_self = (zh == s) & (t == z)

        @pl.when(is_self)
        def _():
            if step == "start":
                pltpu.make_async_copy(block, dst, m.o_r.at[i]).start()

        @pl.when(jnp.logical_not(is_self))
        def _():
            copy = remote(block, dst, m.o_s.at[i], m.o_r.at[i], (zh, t, r))
            if step == "start":
                copy.start()
            else:
                copy.wait_send()

        if step == "wait":
            wait_for(dst, m.o_r.at[i])

    raw_copy = pltpu.make_async_copy(wq_ref.at[0], m.qraw, m.raw)

    def pack_weights():
        raw_copy.wait()
        low_half = lanes_of(part, LANES) < HEAD_DIM

        def column(i, head, at_low):
            values = wide(m.qraw[:, pl.ds(i * width + head // 2 * LANES, LANES)])
            return values if (head % 2 == 0) == at_low else pltpu.roll(values, HEAD_DIM, 1)

        m.aux[...] = jnp.zeros(m.aux.shape, jnp.float32)
        for i, ref in enumerate((g1_ref, b1_ref, g2_ref, b2_ref)):
            m.aux[pl.ds(NORM_ROW + i, 1)] = wide(ref[...])
        norms = jnp.transpose(m.aux[...])
        for c in range(4):
            heads = [3 * c + h for h in range(3)]
            for h, head in enumerate(heads):
                m.qpk[c, :, pl.ds(h * LANES, LANES)] = low(
                    jnp.where(low_half, column(0, head, True), column(1, head, False)))
            m.qpk[c, :, pl.ds(3 * LANES, LANES)] = low(
                jnp.where(low_half, column(2, heads[0], True), column(2, heads[1], False)))
            m.qpk[c, :, pl.ds(4 * LANES, LANES)] = low(jnp.where(low_half, column(2, heads[2], True), norms))

    def where_moved(kind, step):
        if kind in (Q, G):
            step()
        else:
            pl.when(t != z)(step)

    def on(l, kind, k):
        where_moved(kind, lambda: pass_on(l, kind, k))

    def half(l, kind, k):
        where_moved(kind, lambda: pass_half(l, kind, k))

    near, far = m.x.at[0, near_block], m.x.at[0, far_block]
    near_along = remote(near, near, m.tz_s.at[0], m.tz_r.at[0], along)
    near_across = remote(near, near, m.xc_s.at[0], m.xc_r.at[0], across)
    far_across = remote(far, far, m.xc_s.at[1], m.xc_r.at[1], across)
    cot_block = m.cot.at[rows(zp * BLOCK, BLOCK)]
    cot_along = remote(cot_block, cot_block, m.tz_s.at[1], m.tz_r.at[1], along)

    def share_tokens_near():
        wait_for(near, m.tok_r)
        near_along.start()
        near_across.start()

    def share_tokens_far():
        near_along.wait_send()
        wait_for(far, m.tz_r.at[0])
        far_across.start()

    def tokens_shared():
        near_across.wait()
        far_across.wait()

    def cotangent_along():
        wait_for(cot_block, m.cot_r)
        cot_along.start()

    def forward_end():
        send_rows(0, m.outb, out_ref.at[0, 0], "start")
        for l in range(2):
            source_done(l)
            for kind in (Q, O, G, D):
                forward_done(l, kind)
        cot_along.wait_send()
        wait_for(m.cot.at[rows((1 - zp) * BLOCK, BLOCK)], m.tz_r.at[1])
        for j in range(2):
            slot = (2 * j + s) * BLOCK + lax.broadcasted_iota(jnp.int32, (BLOCK, width), 0)
            m.dy[kept(j)] = jnp.where(slot < length, wide(m.cot[kept(j)]), 0.0)

    def layer_done(l, j, copy):
        result = low(m.dres[kept(j)] + summed(5 if l == 1 else 7, j, copy))
        if l == 1:
            m.dy[kept(j)] = wide(result)
        else:
            m.tgb[kept(j)] = result

    def finish_on(l, kind):
        pl.when(s == l)(lambda: finish(kind))

    def half_on(l, kind):
        pl.when(s == l)(lambda: finish_half(kind))

    def all_done():
        for kind in (D, G, O, Q):
            finish_done(kind)
            for l in (1, 0):
                line_done(l, kind)
        scatter_rows(*tok_args, "wait")
        scatter_rows(*cot_args, "wait")
        send_rows(0, m.outb, out_ref.at[0, 0], "wait")
        send_rows(1, m.tgb, tg_ref.at[0, 0], "wait")

    raw_copy.start()
    scatter_rows(*tok_args, "start")
    source(0, (O,))
    pack_weights()
    source(0, (Q,))
    on(0, Q, 1)
    for l in range(2):
        m.wo[l, pl.ds(part, 256 - part)] = jnp.zeros((256 - part, width), jnp.bfloat16)
        m.ng[l] = jnp.zeros((LANES, width), jnp.float32)
    half(0, Q, 1)
    make_tables()
    share_tokens_near()
    source(0, (G, D))
    on(0, Q, 2)
    on(0, O, 1)
    on(0, Q, 3)
    half(0, Q, 3)
    half(0, Q, 2)
    share_tokens_far()
    on(0, G, 1)
    half(0, O, 1)
    need(0, Q)
    read_params(0)
    tokens_shared()
    project(0, 0)
    project(0, 1)
    attend(0, 0)
    on(0, G, 2)
    half(0, G, 1)
    need(0, O)
    a0 = send_partial(0, 0, m.mix.at[0], m.wo[0], dot)
    attend(0, 1)
    b0 = send_sum(0, 0, a0)
    a1 = send_partial(0, 1, m.mix.at[0], m.wo[0], dot)
    b1 = send_sum(0, 1, a1)
    source(1, (Q, O, G))
    on(0, G, 3)
    half(0, G, 3)
    on(0, D, 2)
    half(0, D, 2)
    half(0, G, 2)
    on(0, D, 3)
    c0 = finish_attention(0, 0, 0, b0)
    need(0, G)
    on(0, D, 1)
    half(0, D, 1)
    c0.wait()
    half(0, D, 3)
    on(1, Q, 3)
    on(1, Q, 1)
    on(1, G, 1)
    feed(0, 0)
    c1 = finish_attention(0, 0, 1, b1)
    on(1, Q, 2)
    half(1, Q, 3)
    need(0, D)
    a0 = send_partial(1, 0, m.act.at[0], m.wd[0], dot)
    c1.wait()
    on(1, O, 1)
    b0 = send_sum(1, 0, a0)
    feed(0, 1)
    a1 = send_partial(1, 1, m.act.at[0], m.wd[0], dot)
    half(1, Q, 1)
    half(1, Q, 2)
    b1 = send_sum(1, 1, a1)
    source(1, (D,))
    on(1, G, 2)
    need(1, Q)
    half(1, G, 1)
    read_params(1)
    half(1, O, 1)
    on(1, G, 3)
    c0 = finish_feed(1, 0, 0, b0)
    c1 = finish_feed(1, 0, 1, b1)
    c0.wait()
    project(1, 0)
    half(1, G, 2)
    scatter_rows(*cot_args, "start")
    c1.wait()
    project(1, 1)
    attend(1, 0)
    need(1, O)
    on(1, D, 1)
    a0 = send_partial(2, 0, m.mix.at[1], m.wo[1], dot)
    attend(1, 1)
    b0 = send_sum(2, 0, a0)
    half(1, G, 3)
    on(1, D, 2)
    on(1, D, 3)
    a1 = send_partial(2, 1, m.mix.at[1], m.wo[1], dot)
    b1 = send_sum(2, 1, a1)
    cotangent_along()
    c0 = finish_attention(2, 1, 0, b0)
    half(1, D, 2)
    half(1, D, 1)
    half(1, D, 3)
    need(1, G)
    c0.wait()
    feed(1, 0)
    c1 = finish_attention(2, 1, 1, b1)
    need(1, D)
    a0 = send_partial(3, 0, m.act.at[1], m.wd[1], dot)
    c1.wait()
    b0 = send_sum(3, 0, a0)
    feed(1, 1)
    a1 = send_partial(3, 1, m.act.at[1], m.wd[1], dot)
    b1 = send_sum(3, 1, a1)
    finish_feed(3, 1, 0, b0)
    finish_feed(3, 1, 1, b1)
    forward_end()
    c0 = back_second(1, 0)
    c1 = back_second(1, 1)
    c0.wait()
    back_feed(1, 0)
    a0 = send_partial(4, 0, m.dgu, m.wgu[1], dot_rows)
    c1.wait()
    back_feed(1, 1)
    b0 = send_sum(4, 0, a0)
    a1 = send_partial(4, 1, m.dgu, m.wgu[1], dot_rows)
    weight_grad(1, D)
    plane_first(1, D)
    b1 = send_sum(4, 1, a1)
    weight_grad(1, G)
    plane_first(1, G)
    c0 = back_first(4, 1, 0, b0)
    c1 = back_first(4, 1, 1, b1)
    c0.wait()
    back_mix(1, 0)
    plane_second(1, D)
    c1.wait()
    back_mix(1, 1)
    back_attend(1, 0)
    back_attend(1, 1)
    back_attend(1, 2)
    a0 = send_partial(5, 0, m.dqkv, m.wq[1], dot_rows)
    a1 = send_partial(5, 1, m.dqkv, m.wq[1], dot_rows)
    b0 = send_sum(5, 0, a0)
    weight_grad(1, O)
    plane_first(1, O)
    b1 = send_sum(5, 1, a1)
    weight_grad(1, Q)
    plane_first(1, Q)
    plane_second(1, G)
    layer_done(1, 0, b0)
    layer_done(1, 1, b1)
    c0 = back_second(0, 0)
    c1 = back_second(0, 1)
    c0.wait()
    back_feed(0, 0)
    a0 = send_partial(6, 0, m.dgu, m.wgu[0], dot_rows)
    c1.wait()
    back_feed(0, 1)
    b0 = send_sum(6, 0, a0)
    spread_line(1, D)
    a1 = send_partial(6, 1, m.dgu, m.wgu[0], dot_rows)
    weight_grad(0, D)
    plane_first(0, D)
    b1 = send_sum(6, 1, a1)
    weight_grad(0, G)
    plane_second(1, Q)
    spread_line(1, G)
    plane_first(0, G)
    c0 = back_first(6, 0, 0, b0)
    c1 = back_first(6, 0, 1, b1)
    c0.wait()
    back_mix(0, 0)
    c1.wait()
    plane_second(1, O)
    back_mix(0, 1)
    back_attend(0, 0)
    plane_second(0, D)
    back_attend(0, 1)
    back_attend(0, 2)
    a0 = send_partial(7, 0, m.dqkv, m.wq[0], dot_rows)
    a1 = send_partial(7, 1, m.dqkv, m.wq[0], dot_rows)
    b0 = send_sum(7, 0, a0)
    weight_grad(0, O)
    plane_first(0, O)
    b1 = send_sum(7, 1, a1)
    spread_line(1, O)
    weight_grad(0, Q)
    plane_first(0, Q)
    plane_second(0, G)
    finish_on(1, G)
    layer_done(0, 0, b0)
    spread_line(1, Q)
    layer_done(0, 1, b1)
    plane_second(0, O)
    send_rows(1, m.tgb, tg_ref.at[0, 0], "start")
    spread_line(0, D)
    spread_line(0, G)
    plane_second(0, Q)
    finish_on(1, D)
    finish_on(1, O)
    finish_on(0, G)
    finish_on(1, Q)
    finish_on(0, D)
    spread_line(0, Q)
    half_on(1, O)
    half_on(1, G)
    spread_line(0, O)
    finish_on(0, O)
    finish_on(0, Q)
    half_on(0, D)
    half_on(0, G)
    half_on(1, D)
    half_on(0, O)
    half_on(0, Q)
    half_on(1, Q)
    all_done()


def relay(tokens, lengths, cotangent, w_qkv, w_out, norm1_gain, norm1_bias, w_gate, w_up, w_down, norm2_gain, norm2_bias):
    bf = jnp.bfloat16
    part, width = w_qkv.shape[1], tokens.shape[3]
    hidden = w_gate.shape[2]
    scratch = relay_scratch(width, hidden)
    any_space = pl.BlockSpec(memory_space=pl.ANY)
    fpart = hidden // 4
    outs = pl.pallas_call(
        functools.partial(relay_kernel, tuple(scratch)),
        out_shape=(
            jax.ShapeDtypeStruct(tokens.shape, bf), jax.ShapeDtypeStruct(tokens.shape, bf),
            jax.ShapeDtypeStruct((part, 3 * width + LANES), bf), jax.ShapeDtypeStruct((part, width), bf),
            jax.ShapeDtypeStruct((part, 2 * hidden), bf), jax.ShapeDtypeStruct((fpart, width), bf),
        ),
        in_specs=[pl.BlockSpec(memory_space=pltpu.VMEM)] * 5 + [any_space] * 7,
        out_specs=[any_space] * 6,
        scratch_shapes=list(scratch.values()),
        compiler_params=pltpu.CompilerParams(
            collective_id=1, has_side_effects=True, vmem_limit_bytes=VMEM_LIMIT),
    )(lengths, norm1_gain, norm1_bias, norm2_gain, norm2_bias, tokens, cotangent, w_qkv, w_out, w_gate, w_up, w_down)
    output, token_grad, grad_q, grad_out, grad_gu, grad_down = outs
    grad_q, grad_out, grad_gu, grad_down = (grad.astype(jnp.float32) for grad in (grad_q, grad_out, grad_gu, grad_down))
    norms = grad_q[:, 3 * width + NORM_ROW:3 * width + NORM_ROW + 4]
    return (
        output, token_grad, grad_q[None, :, :3 * width], grad_out[None], norms[:, 0][None], norms[:, 1][None],
        grad_gu[None, :, :hidden], grad_gu[None, :, hidden:], grad_down[None], norms[:, 2][None], norms[:, 3][None],
    )


def fits_relay(args):
    tokens, lengths, w_qkv, w_gate, w_down = args[0], args[1], args[3], args[7], args[9]
    axes = tuple(lax.axis_size(axis) for axis in ("section", "fsdp", "rep"))
    return (
        axes == (2, 4, 4)
        and tokens.shape == (1, 1, BLOCK, 768)
        and lengths.shape == (2, 1)
        and w_qkv.shape == (1, 192, 2304)
        and w_gate.shape == (1, 192, 3072)
        and w_down.shape == (1, 768, 768)
    )


def program(*args):
    return relay(*args) if fits_relay(args) else shards(*args)


def solution(mesh):
    return jax.shard_map(
        program,
        mesh=mesh,
        in_specs=(
            P("section", "rep", "fsdp", None),
            P(None, "rep"),
            P("section", "rep", "fsdp", None),
            P("section", "fsdp", None),
            P("section", "fsdp", None),
            P("section", "fsdp"),
            P("section", "fsdp"),
            P("section", "fsdp", None),
            P("section", "fsdp", None),
            P("section", "fsdp", None),
            P("section", "fsdp"),
            P("section", "fsdp"),
        ),
        out_specs=(
            P("section", "rep", "fsdp", None),
            P("section", "rep", "fsdp", None),
            P("section", "fsdp", None),
            P("section", "fsdp", None),
            P("section", "fsdp"),
            P("section", "fsdp"),
            P("section", "fsdp", None),
            P("section", "fsdp", None),
            P("section", "fsdp", None),
            P("section", "fsdp"),
            P("section", "fsdp"),
        ),
        check_vma=False,
    )
```

```python
import functools
import math
import types

import jax
import jax.numpy as jnp
from jax import lax
from jax.experimental import pallas as pl
from jax.experimental.pallas import tpu as pltpu
from jax.sharding import PartitionSpec as P

HEADS = 12
HEAD_DIM = 64


norm_eps = 1e-05
masked_score = -1000000000.0
VMEM_LIMIT = 62 * 2**20


def partner(block, axis, distance):
    count = lax.axis_size(axis)
    route = []
    for low in range(count):
        high = low | 1 << distance
        if high != low and high < count:
            route += [(low, high), (high, low)]
    return lax.ppermute(block, axis, route)


def shifted(value, axis, steps):
    count = lax.axis_size(axis)
    initial, last = (max(0, -steps), min(count, count - steps))
    return lax.ppermute(value, axis, [(source, source + steps) for source in range(initial, last)])


def norm_rows(values, norm_gain, offset):
    centre = values - jnp.mean(values, axis=-1, keepdims=True)
    inverse = lax.rsqrt(jnp.mean(centre * centre, axis=-1, keepdims=True) + norm_eps)
    normed = centre * inverse
    return (normed * norm_gain + offset, normed, inverse)


def norm_back(grad_out, normed, inverse, norm_gain):
    scaled = grad_out * norm_gain
    return inverse * (
        scaled
        - jnp.mean(scaled, axis=-1, keepdims=True)
        - normed * jnp.mean(scaled * normed, axis=-1, keepdims=True)
    )


def rotary_tables(first_slot, row_count):
    half_dim = HEAD_DIM // 2
    inverse_freq = 1000.0 ** (-2.0 * jnp.arange(half_dim, dtype=jnp.float32) / HEAD_DIM)
    places = (first_slot + jnp.arange(row_count)).astype(jnp.float32)
    angles = places[:, None] * inverse_freq[None, :]
    angles = jnp.concatenate([angles, angles], axis=-1)[:, None, :]
    return (jnp.cos(angles), jnp.sin(angles))


def turn_half(values):
    half_dim = values.shape[-1] // 2
    return jnp.concatenate([-values[..., half_dim:], values[..., :half_dim]], axis=-1)


def rotate(values, cosine_table, sine_table):
    return values * cosine_table + turn_half(values) * sine_table


def rotate_back(values, cosine_table, sine_table):
    return values * cosine_table - turn_half(values) * sine_table


def masked_scores(query_rot, key_all, live_keys):
    key_heads = key_all.reshape(key_all.shape[0], HEADS, HEAD_DIM)
    scores = jnp.einsum(
        "qhd,khd->hqk", query_rot, key_heads, preferred_element_type=jnp.float32
    ) * HEAD_DIM ** (-0.5)
    return jnp.where(live_keys[None, None, :], scores, masked_score)


def batch_length(length_column, batch_now):
    picked = jnp.clip(batch_now, 0, length_column.shape[0] - 1)
    return lax.dynamic_index_in_dim(length_column, picked, 0, keepdims=False)


def layer_forward(inputs, weights, live_keys, cosine_table, sine_table):
    w_qkv, w_out, gain_one, offset_one, w_gate, w_up, w_down, gain_two, offset_two = weights
    row_count, model_width = inputs.shape
    head_shape = (row_count, HEADS, HEAD_DIM)
    inputs_low = inputs.astype(jnp.bfloat16)
    joined = jnp.dot(inputs_low, w_qkv, preferred_element_type=jnp.float32)
    query_rot = rotate(
        joined[:, :model_width].reshape(head_shape), cosine_table, sine_table
    ).astype(jnp.bfloat16)
    key_own = (
        rotate(
            joined[:, model_width : 2 * model_width].reshape(head_shape), cosine_table, sine_table
        )
        .reshape(row_count, model_width)
        .astype(jnp.bfloat16)
    )
    value_own = joined[:, 2 * model_width :].astype(jnp.bfloat16)
    key_all, value_all = (
        lax.all_gather(key_own, "fsdp", axis=0, tiled=True),
        lax.all_gather(value_own, "fsdp", axis=0, tiled=True),
    )
    scores = masked_scores(query_rot, key_all, live_keys)
    highest = jnp.max(scores, axis=-1, keepdims=True)
    log_total = highest + jnp.log(jnp.sum(jnp.exp(scores - highest), axis=-1, keepdims=True))
    softmax_weights = jnp.exp(scores - log_total).astype(jnp.bfloat16)
    value_heads = value_all.reshape(value_all.shape[0], HEADS, HEAD_DIM)
    mixed_heads = jnp.einsum(
        "hqk,khd->qhd", softmax_weights, value_heads, preferred_element_type=jnp.float32
    )
    mixed_heads = mixed_heads.reshape(row_count, model_width).astype(jnp.bfloat16)
    attended = jnp.dot(mixed_heads, w_out, preferred_element_type=jnp.float32)
    hidden, normed_one, inverse_one = norm_rows(inputs + attended, gain_one, offset_one)
    hidden_low = hidden.astype(jnp.bfloat16)
    gate_proj = jnp.dot(hidden_low, w_gate, preferred_element_type=jnp.float32)
    upward = jnp.dot(hidden_low, w_up, preferred_element_type=jnp.float32)
    product = (jax.nn.silu(gate_proj) * upward).astype(jnp.bfloat16)
    mlp_out = jnp.dot(product, w_down, preferred_element_type=jnp.float32)
    result, normed_two, inverse_two = norm_rows(hidden + mlp_out, gain_two, offset_two)
    key_saved, value_saved = (key_all, value_all)
    kept_state = (
        inputs_low,
        query_rot,
        key_saved,
        value_saved,
        log_total,
        mixed_heads,
        normed_one,
        inverse_one,
        hidden_low,
        gate_proj,
        upward,
        product,
        normed_two,
        inverse_two,
    )
    return (result, kept_state)


def layer_backward(grad_out, kept_state, weights, live_keys, cosine_table, sine_table):
    w_qkv, w_out, gain_one, offset_one, w_gate, w_up, w_down, gain_two, offset_two = weights
    (
        inputs_low,
        query_rot,
        key_saved,
        value_saved,
        log_total,
        mixed_heads,
        normed_one,
        inverse_one,
        hidden_low,
        gate_proj,
        upward,
        product,
        normed_two,
        inverse_two,
    ) = kept_state
    row_count, model_width = inputs_low.shape
    head_shape = (row_count, HEADS, HEAD_DIM)
    key_all, value_all = (key_saved, value_saved)
    grad_gain_two = jnp.sum(grad_out * normed_two, axis=0)
    grad_offset_two = jnp.sum(grad_out, axis=0)
    grad_second = norm_back(grad_out, normed_two, inverse_two, gain_two)
    grad_fed = grad_second.astype(jnp.bfloat16)
    grad_product = jnp.einsum("rd,fd->rf", grad_fed, w_down, preferred_element_type=jnp.float32)
    grad_w_down = jnp.einsum("rf,rd->fd", product, grad_fed, preferred_element_type=jnp.float32)
    sigmoid_gate = jax.nn.sigmoid(gate_proj)
    silu_gate = gate_proj * sigmoid_gate
    grad_gate = (
        grad_product * upward * sigmoid_gate * (1.0 + gate_proj * (1.0 - sigmoid_gate))
    ).astype(jnp.bfloat16)
    grad_upward = (grad_product * silu_gate).astype(jnp.bfloat16)
    grad_hidden = grad_second + jnp.einsum(
        "rf,df->rd", grad_gate, w_gate, preferred_element_type=jnp.float32
    )
    grad_hidden = grad_hidden + jnp.einsum(
        "rf,df->rd", grad_upward, w_up, preferred_element_type=jnp.float32
    )
    grad_w_gate = jnp.einsum("rd,rf->df", hidden_low, grad_gate, preferred_element_type=jnp.float32)
    grad_w_up = jnp.einsum("rd,rf->df", hidden_low, grad_upward, preferred_element_type=jnp.float32)
    grad_gain_one = jnp.sum(grad_hidden * normed_one, axis=0)
    grad_offset_one = jnp.sum(grad_hidden, axis=0)
    grad_first = norm_back(grad_hidden, normed_one, inverse_one, gain_one)
    grad_attended = grad_first.astype(jnp.bfloat16)
    grad_w_out = jnp.einsum(
        "rd,re->de", mixed_heads, grad_attended, preferred_element_type=jnp.float32
    )
    grad_mixed = (
        jnp.einsum("re,de->rd", grad_attended, w_out, preferred_element_type=jnp.float32)
        .astype(jnp.bfloat16)
        .reshape(head_shape)
    )
    scores = masked_scores(query_rot, key_all, live_keys)
    attention = jnp.exp(scores - log_total)
    key_count = key_all.shape[0]
    key_heads = key_all.reshape(key_count, HEADS, HEAD_DIM)
    value_heads = value_all.reshape(key_count, HEADS, HEAD_DIM)
    grad_attention = jnp.einsum(
        "qhd,khd->hqk", grad_mixed, value_heads, preferred_element_type=jnp.float32
    )
    centre_term = jnp.sum(grad_attention * attention, axis=-1, keepdims=True)
    grad_scores = (attention * (grad_attention - centre_term)).astype(jnp.bfloat16)
    score_scale = HEAD_DIM ** (-0.5)
    grad_query = (
        jnp.einsum("hqk,khd->qhd", grad_scores, key_heads, preferred_element_type=jnp.float32)
        * score_scale
    )
    attention_low = attention.astype(jnp.bfloat16)
    grad_value_all = jnp.einsum(
        "hqk,qhd->khd", attention_low, grad_mixed, preferred_element_type=jnp.float32
    )
    grad_key_all = (
        jnp.einsum("hqk,qhd->khd", grad_scores, query_rot, preferred_element_type=jnp.float32)
        * score_scale
    )
    grad_key, grad_value = (
        lax.psum_scatter(
            grad_key_all.reshape(key_count, model_width).astype(jnp.bfloat16),
            "fsdp",
            scatter_dimension=0,
            tiled=True,
        ).astype(jnp.float32),
        lax.psum_scatter(
            grad_value_all.reshape(key_count, model_width).astype(jnp.bfloat16),
            "fsdp",
            scatter_dimension=0,
            tiled=True,
        ).astype(jnp.float32),
    )
    grad_joined = jnp.concatenate(
        [
            rotate_back(grad_query, cosine_table, sine_table).reshape(row_count, model_width),
            rotate_back(grad_key.reshape(head_shape), cosine_table, sine_table).reshape(
                row_count, model_width
            ),
            grad_value,
        ],
        axis=1,
    ).astype(jnp.bfloat16)
    grad_w_qkv = jnp.einsum(
        "rd,re->de", inputs_low, grad_joined, preferred_element_type=jnp.float32
    )
    grad_inputs = grad_first + jnp.einsum(
        "re,de->rd", grad_joined, w_qkv, preferred_element_type=jnp.float32
    )
    weight_grads = (
        grad_w_qkv,
        grad_w_out,
        grad_gain_one,
        grad_offset_one,
        grad_w_gate,
        grad_w_up,
        grad_w_down,
        grad_gain_two,
        grad_offset_two,
    )
    return (grad_inputs, weight_grads)


def shards(
    tokens,
    lengths,
    cotangent,
    w_qkv,
    w_out,
    norm1_gain,
    norm1_bias,
    w_gate,
    w_up,
    w_down,
    norm2_gain,
    norm2_bias,
):
    section_index = lax.axis_index("section")
    fsdp_index = lax.axis_index("fsdp")
    is_first = section_index == 0
    row_count = tokens.shape[2]
    model_width = tokens.shape[3]
    slot_count = row_count * lax.axis_size("fsdp")
    micro_count = lengths.shape[0]
    weights = (
        lax.all_gather(w_qkv[0], "fsdp", axis=0, tiled=True),
        lax.all_gather(w_out[0], "fsdp", axis=0, tiled=True),
        lax.all_gather(norm1_gain[0], "fsdp", axis=0, tiled=True),
        lax.all_gather(norm1_bias[0], "fsdp", axis=0, tiled=True),
        lax.all_gather(w_gate[0], "fsdp", axis=0, tiled=True),
        lax.all_gather(w_up[0], "fsdp", axis=0, tiled=True),
        lax.all_gather(w_down[0], "fsdp", axis=0, tiled=True),
        lax.all_gather(norm2_gain[0], "fsdp", axis=0, tiled=True),
        lax.all_gather(norm2_bias[0], "fsdp", axis=0, tiled=True),
    )
    own_tokens = tokens[0, 0]
    own_cotangent = cotangent[0, 0]
    arrived = partner(jnp.where(is_first, own_cotangent, own_tokens), "section", 0)
    batch_tokens = [
        jnp.where(is_first, own_tokens, arrived),
        jnp.where(is_first, arrived, own_tokens),
    ]
    batch_cotangents = [
        jnp.where(is_first, own_cotangent, arrived),
        jnp.where(is_first, arrived, own_cotangent),
    ]
    cosine_table, sine_table = rotary_tables(fsdp_index * row_count, row_count)
    row_slots = fsdp_index * row_count + jnp.arange(row_count)
    key_slots = jnp.arange(slot_count)
    length_column = lengths[:, 0]
    empty_rows = jnp.zeros((row_count, model_width), jnp.bfloat16)
    carried = empty_rows
    kept_list = []
    layer_outputs = []
    for tick_index in range(micro_count + 1):
        length_now = batch_length(length_column, tick_index - section_index)
        fresh_rows = batch_tokens[tick_index] if tick_index < micro_count else empty_rows
        inputs = jnp.where(is_first, fresh_rows, carried).astype(jnp.float32)
        result, kept_state = layer_forward(
            inputs, weights, key_slots < length_now, cosine_table, sine_table
        )
        result_low = result.astype(jnp.bfloat16)
        kept_list.append(kept_state)
        layer_outputs.append(result_low)
        if tick_index < micro_count:
            carried = shifted(result_low, "section", 1)
    arriving = empty_rows
    totals = None
    owned_total = None
    input_grads = []
    for tick_index in range(micro_count + 1):
        batch_now = tick_index - 1 + section_index
        length_now = batch_length(length_column, batch_now)
        is_valid = (batch_now >= 0) & (batch_now < micro_count)
        seed_rows = batch_cotangents[tick_index] if tick_index < micro_count else empty_rows
        seed_grad = (
            seed_rows.astype(jnp.float32) * (row_slots < length_now).astype(jnp.float32)[:, None]
        )
        grad_out = jnp.where(
            is_valid, jnp.where(is_first, arriving.astype(jnp.float32), seed_grad), 0.0
        )
        earlier_state = kept_list[max(tick_index - 1, 0)]
        later_state = kept_list[min(tick_index + 1, micro_count)]
        kept_state = jax.tree.map(
            lambda first_arr, second_arr: jnp.where(is_first, first_arr, second_arr),
            earlier_state,
            later_state,
        )
        grad_inputs, weight_grads = layer_backward(
            grad_out, kept_state, weights, key_slots < length_now, cosine_table, sine_table
        )
        grad_low = grad_inputs.astype(jnp.bfloat16)
        input_grads.append(grad_low)
        if tick_index < micro_count:
            arriving = shifted(grad_low, "section", -1)
        totals = weight_grads if totals is None else jax.tree.map(jnp.add, totals, weight_grads)
    shares = (
        lax.psum_scatter(
            totals[0].astype(jnp.bfloat16), "fsdp", scatter_dimension=0, tiled=True
        ).astype(jnp.float32),
        lax.psum_scatter(
            totals[1].astype(jnp.bfloat16), "fsdp", scatter_dimension=0, tiled=True
        ).astype(jnp.float32),
        lax.psum_scatter(
            totals[2].astype(jnp.bfloat16), "fsdp", scatter_dimension=0, tiled=True
        ).astype(jnp.float32),
        lax.psum_scatter(
            totals[3].astype(jnp.bfloat16), "fsdp", scatter_dimension=0, tiled=True
        ).astype(jnp.float32),
        lax.psum_scatter(
            totals[4].astype(jnp.bfloat16), "fsdp", scatter_dimension=0, tiled=True
        ).astype(jnp.float32),
        lax.psum_scatter(
            totals[5].astype(jnp.bfloat16), "fsdp", scatter_dimension=0, tiled=True
        ).astype(jnp.float32),
        lax.psum_scatter(
            totals[6].astype(jnp.bfloat16), "fsdp", scatter_dimension=0, tiled=True
        ).astype(jnp.float32),
        lax.psum_scatter(
            totals[7].astype(jnp.bfloat16), "fsdp", scatter_dimension=0, tiled=True
        ).astype(jnp.float32),
        lax.psum_scatter(
            totals[8].astype(jnp.bfloat16), "fsdp", scatter_dimension=0, tiled=True
        ).astype(jnp.float32),
    )
    owned_total = (
        lax.psum(shares[0].astype(jnp.bfloat16), "rep").astype(jnp.float32),
        lax.psum(shares[1].astype(jnp.bfloat16), "rep").astype(jnp.float32),
        lax.psum(shares[2].astype(jnp.bfloat16), "rep").astype(jnp.float32),
        lax.psum(shares[3].astype(jnp.bfloat16), "rep").astype(jnp.float32),
        lax.psum(shares[4].astype(jnp.bfloat16), "rep").astype(jnp.float32),
        lax.psum(shares[5].astype(jnp.bfloat16), "rep").astype(jnp.float32),
        lax.psum(shares[6].astype(jnp.bfloat16), "rep").astype(jnp.float32),
        lax.psum(shares[7].astype(jnp.bfloat16), "rep").astype(jnp.float32),
        lax.psum(shares[8].astype(jnp.bfloat16), "rep").astype(jnp.float32),
    )
    outgoing = jnp.where(is_first, input_grads[2], layer_outputs[1])
    returned = partner(outgoing, "section", 0)
    output_rows = jnp.where(is_first, returned, layer_outputs[2])
    grad_rows = jnp.where(is_first, input_grads[1], returned)
    return (
        output_rows[None, None],
        grad_rows[None, None],
        owned_total[0][None],
        owned_total[1][None],
        owned_total[2][None],
        owned_total[3][None],
        owned_total[4][None],
        owned_total[5][None],
        owned_total[6][None],
        owned_total[7][None],
        owned_total[8][None],
    )


MESH = pl.DeviceIdType.MESH
BLOCK = 128
LANES = 128
QKV_PAD = 640
NORM_ROW = 64


def dot(left, right):
    return jnp.dot(left, right, preferred_element_type=jnp.float32)


def dot_rows(left, right):
    return lax.dot_general(left, right, (((1,), (1,)), ((), ())), preferred_element_type=jnp.float32)


def dot_cols(left, right):
    return lax.dot_general(left, right, (((0,), (0,)), ((), ())), preferred_element_type=jnp.float32)


def low(value):
    return value.astype(jnp.bfloat16)


def wide(value):
    return value.astype(jnp.float32)


def wait_for(ref, sem):
    pltpu.make_async_copy(ref, ref, sem).wait()


def turned(values):
    lane = lax.broadcasted_iota(jnp.int32, values.shape, 1)
    ahead = pltpu.roll(values, LANES - HEAD_DIM // 2, 1)
    behind = pltpu.roll(values, HEAD_DIM // 2, 1)
    return jnp.where(lane % HEAD_DIM < HEAD_DIM // 2, ahead, behind)


def relay_scratch(width, hidden):
    vm = pltpu.VMEM
    bf, f32 = jnp.bfloat16, jnp.float32
    slots = 4 * BLOCK
    own = 2 * BLOCK
    dma = pltpu.SemaphoreType.DMA
    part = width // 4
    share = part // 4
    fpart = hidden // 4
    fshare = fpart // 4
    return dict(
        wq=vm((2, width, QKV_PAD), bf), wo=vm((2, 256, width), bf), wgu=vm((2, width, 2 * fpart), bf),
        wd=vm((2, fpart, width), bf),
        x=vm((2, slots, width), bf), hid=vm((2, slots, width), bf), dfed=vm((2, slots, width), bf),
        datt=vm((2, slots, width), bf),
        q=vm((2, 3, slots, LANES), bf), k=vm((2, 3, slots, LANES), bf), v=vm((2, slots, 256), bf),
        pr=vm((2, 3, slots, slots), bf), mix=vm((2, slots, 256), bf), gu=vm((2, slots, 2 * fpart), bf),
        act=vm((2, slots, fpart), bf),
        n1=vm((2, own, width), f32), n2=vm((2, own, width), f32),
        i1=vm((2, own, LANES), f32), i2=vm((2, own, LANES), f32),
        dgu=vm((slots, 2 * fpart), bf), dmix=vm((slots, 256), bf), dqkv=vm((slots, QKV_PAD), bf),
        ds=vm((slots, slots), bf), dq=vm((slots, LANES), f32),
        hidf=vm((own, width), f32), dres=vm((own, width), f32), dy=vm((own, width), f32),
        part=vm((2, own, width), f32), cot=vm((own, width), bf), outb=vm((own, width), bf), tgb=vm((own, width), bf),
        sa=vm((2, 2, BLOCK, width), bf), ra=vm((2, 2, BLOCK, width), bf),
        sb=vm((2, 2, BLOCK, width), bf), rb=vm((2, 2, BLOCK, width), bf),
        par=vm((2, LANES, width), f32), ng=vm((2, LANES, width), f32),
        r1q=vm((2, 3, part, QKV_PAD), bf), r1g=vm((2, 3, part, 2 * fpart), bf),
        r1o=vm((2, 3, share, width), bf), r1d=vm((2, 3, fshare, width), bf),
        s2q=vm((2, part, QKV_PAD), bf), s2g=vm((2, part, 2 * fpart), bf),
        s2o=vm((2, share, width), bf), s2d=vm((2, fshare, width), bf),
        r2q=vm((8, share, QKV_PAD), bf), r2g=vm((8, share, 2 * fpart), bf),
        r2o=vm((2, share, width), bf), r2d=vm((2, fshare, width), bf),
        qraw=vm((part, 3 * width), bf), qpk=vm((4, part, QKV_PAD), bf), aux=vm((LANES, part), f32), raw=dma,
        s3q=vm((share, 3 * width + LANES), bf), s3g=vm((share, 2 * hidden), bf),
        cos=vm((slots, LANES), f32), sin=vm((slots, LANES), f32),
        s3o=vm((share, width), bf), s3d=vm((fshare, width), bf),
        tok_s=dma((1,)), tok_r=dma, cot_s=dma((1,)), cot_r=dma, xc_s=dma((2,)), xc_r=dma((2,)), tz_s=dma((2,)), tz_r=dma((2,)),
        wz=dma((2, 4, 4)), wss=dma((2, 2)), wso=dma((2, 2, 2)), wfs=dma((2, 4)), wrs=dma((2, 4)), wpx=dma((2, 4, 3)), wpy=dma((2, 4, 3)), wpd=dma((2, 4)),
        a_s=dma((2, 2)), a_r=dma((2, 2)), b_s=dma((2, 2)), b_r=dma((2, 2)), c_s=dma((8, 2)), c_r=dma((8, 2)),
        s1s=dma((2, 4)), s1a=dma((2, 4)), s1b=dma((2, 4)), s1t=dma((2, 4)), s1r=dma((2, 4)),
        s2s=dma((2, 4)), s2r=dma((4,)),
        s3s=dma((4, 2)), s3x=dma((4,)), s3y=dma((4,)), s3l=dma((4,)), s3t=dma((4,)), s3e=dma((4,)),
        o_s=dma((2,)), o_r=dma((2,)),
    )


def relay_kernel(names, length_ref, g1_ref, b1_ref, g2_ref, b2_ref, tok_ref, cot_ref, wq_ref, wo_ref, wg_ref, wu_ref, wd_ref,
                 out_ref, tg_ref, oq_ref, on_ref, oo_ref, og_ref, ou_ref, od_ref, *scratch):
    m = types.SimpleNamespace(**dict(zip(names, scratch)))
    width = tok_ref.shape[3]
    slots = 4 * BLOCK
    part = width // 4
    share = part // 4
    fpart = wd_ref.shape[1]
    fshare = fpart // 4
    s, z, r = lax.axis_index("section"), lax.axis_index("fsdp"), lax.axis_index("rep")
    zp, zh = z % 2, z // 2
    r0, r1 = r % 2, r // 2
    t = 2 * zp + s
    other = 1 - s

    def mixed(low_bit, high_bit, k):
        a = 1 - low_bit if k & 1 else low_bit
        b = 1 - high_bit if k & 2 else high_bit
        return a + 2 * b

    z_of = [mixed(zp, zh, k) for k in range(4)]
    r_of = [mixed(r0, r1, k) for k in range(4)]
    zp_of = [zp, 1 - zp, zp, 1 - zp]
    across = (other, z, r)
    along = (s, z_of[1], r)

    def remote(src, dst, send, recv, device):
        return pltpu.make_async_remote_copy(
            src_ref=src, dst_ref=dst, send_sem=send, recv_sem=recv, device_id=device, device_id_type=MESH)

    def rows(start, size):
        return pl.ds(pl.multiple_of(start, 16), size)

    barrier = pltpu.get_barrier_semaphore()
    greeted = [(other, z_of[0], r)] + [(c, z_of[k], r) for k in (1, 2, 3) for c in (0, 1)]
    greeted += [(s, z, r_of[k]) for k in (1, 2, 3)]
    for device in greeted:
        pl.semaphore_signal(barrier, inc=1, device_id=device, device_id_type=MESH)
    pl.semaphore_wait(barrier, len(greeted))

    home = (zp, 2 * s + zh, r)
    at_home = (zp == s) & (2 * s + zh == z)

    def scatter_rows(src, dst, send, recv, step):
        @pl.when(at_home)
        def _():
            if step == "start":
                pltpu.make_async_copy(src, dst, recv).start()

        @pl.when(jnp.logical_not(at_home))
        def _():
            copy = remote(src, dst, send.at[0], recv, home)
            if step == "start":
                copy.start()
            else:
                copy.wait_send()

    near_block, far_block = rows(t * BLOCK, BLOCK), rows((2 * (1 - zp) + s) * BLOCK, BLOCK)
    tok_args = (tok_ref.at[0, 0], m.x.at[0, rows(z * BLOCK, BLOCK)], m.tok_s, m.tok_r)
    cot_args = (cot_ref.at[0, 0], m.cot.at[rows(zh * BLOCK, BLOCK)], m.cot_s, m.cot_r)

    Q, G, O, D = range(4)
    weight = [m.wq, m.wgu, m.wo, m.wd]
    count = [share, share, share, fshare]
    pieces = 3

    def source_fan(l, kind):
        for k in range(4):
            size = part if k == 0 else share
            start = 0 if k == 0 else r * share
            here = rows(z * part + start, size)
            for c in range(2):
                target = 2 * zp_of[k] + c
                device = (c, z_of[k], r)
                if kind == Q:
                    pairs = [(m.qpk.at[target, rows(start, size)], m.wq.at[l, here])]
                else:
                    cols = pl.ds(pl.multiple_of(target * fpart, LANES), fpart)
                    pairs = [
                        (wg_ref.at[0, rows(start, size), cols], m.wgu.at[l, here, pl.ds(0, fpart)]),
                        (wu_ref.at[0, rows(start, size), cols], m.wgu.at[l, here, pl.ds(fpart, fpart)]),
                    ]
                for src, dst in pairs:
                    if k == 0 and c == l:
                        pltpu.make_async_copy(src, dst, m.wz.at[l, kind, k]).start()
                    else:
                        remote(src, dst, m.wss.at[l, kind], m.wz.at[l, kind, k], device).start()

    def blocks_in(kind):
        return pieces if kind == D else 1

    def piece_rows(kind, b, rep):
        n = count[kind]
        size = n // blocks_in(kind)
        return rows(rep * n + b * size, size)

    def source_own(l, kind, step):
        ref = wo_ref if kind == O else wd_ref
        n = count[kind]
        for i in range(2):
            target = zh + 2 * i
            own = target == z

            def send(src, dst):
                copy = remote(src, dst, m.wso.at[l, kind - O, i], m.wz.at[l, kind, 3], (zp, target, r))
                if step == "start":
                    copy.start()
                else:
                    copy.wait_send()

            @pl.when(own & (zp == l))
            def _():
                if step == "start":
                    pltpu.make_async_copy(
                        ref.at[0], weight[kind].at[l, pl.ds(0, 4 * n)], m.wz.at[l, kind, 3]).start()

            @pl.when(own & (zp != l))
            def _():
                send(ref.at[0], weight[kind].at[l, pl.ds(0, 4 * n)])

            @pl.when(jnp.logical_not(own))
            def _():
                if step == "start":
                    for b in range(blocks_in(kind)):
                        part_rows = piece_rows(kind, b, r)
                        remote(
                            ref.at[0, part_rows], weight[kind].at[l, part_rows], m.wso.at[l, kind - O, i],
                            m.wz.at[l, kind, b], (zp, target, r)).start()
                else:
                    wait_for(weight[kind].at[l, pl.ds(0, n)], m.wso.at[l, kind - O, i])

    def source(l, kinds):
        @pl.when(s == l)
        def _():
            for kind in kinds:
                if kind in (Q, G):
                    source_fan(l, kind)
                else:
                    source_own(l, kind, "start")

    def source_done(l):
        @pl.when(s == l)
        def _():
            size = 6 * share + part
            wait_for(m.wq.at[l, pl.ds(0, size)], m.wss.at[l, Q])
            wait_for(m.wgu.at[l, pl.ds(0, size)], m.wss.at[l, G])
            source_own(l, O, "wait")
            source_own(l, D, "wait")

    xn, yn = (s, z, r_of[1]), (s, z, r_of[2])
    cut = [3 * LANES, fpart, width // 2, width // 2]

    def halves_of(kind, lanes):
        return pl.ds(0, cut[kind]), pl.ds(cut[kind], lanes - cut[kind])

    def block_rows(kind, k, rep):
        if kind in (Q, G):
            return rows(z_of[k] * part + rep * share, share)
        return piece_rows(kind, k - 1, rep)

    def pass_on(l, kind, k):
        block = weight[kind].at[l, block_rows(kind, k, r)]
        wait_for(block, m.wz.at[l, kind, k if kind in (Q, G) else k - 1])
        remote(block, block, m.wfs.at[l, kind], m.wpx.at[l, kind, k - 1], xn).start()
        remote(block, block, m.wfs.at[l, kind], m.wpy.at[l, kind, k - 1], yn).start()

    def pass_half(l, kind, k):
        first, second = halves_of(kind, weight[kind].shape[2])
        here = block_rows(kind, k, r_of[1])
        wait_for(weight[kind].at[l, here], m.wpx.at[l, kind, k - 1])
        half = weight[kind].at[l, here, first]
        remote(half, half, m.wrs.at[l, kind], m.wpd.at[l, kind], yn).start()
        here = block_rows(kind, k, r_of[2])
        wait_for(weight[kind].at[l, here], m.wpy.at[l, kind, k - 1])
        half = weight[kind].at[l, here, second]
        remote(half, half, m.wrs.at[l, kind], m.wpd.at[l, kind], xn).start()

    def need(l, kind):
        n = count[kind]
        if kind in (Q, G):
            wait_for(weight[kind].at[l, rows(z * part, part)], m.wz.at[l, kind, 0])
            wait_for(weight[kind].at[l, pl.ds(0, 3 * n)], m.wpd.at[l, kind])
        else:
            @pl.when(t != z)
            def _():
                wait_for(weight[kind].at[l, pl.ds(0, n)], m.wpd.at[l, kind])

            @pl.when(t == z)
            def _():
                wait_for(weight[kind].at[l, pl.ds(0, 4 * n)], m.wz.at[l, kind, 3])

    def forward_done(l, kind):
        n = count[kind]

        def wait(blocks):
            wait_for(weight[kind].at[l, pl.ds(0, 2 * blocks * n)], m.wfs.at[l, kind])
            wait_for(weight[kind].at[l, pl.ds(0, blocks * n)], m.wrs.at[l, kind])

        if kind in (Q, G):
            wait(3)
        else:
            pl.when(t != z)(lambda: wait(1))

    def own_rows(j):
        return rows((2 * j + s) * BLOCK, BLOCK)

    def chunk(j):
        return pl.ds(2 * j * BLOCK, 2 * BLOCK)

    def kept(j):
        return pl.ds(j * BLOCK, BLOCK)

    def send_partial(e, j, left, right, multiply):
        p = e % 2
        m.part[j] = multiply(left[chunk(j)], right)
        m.sa[p, j] = low(m.part[j, rows(other * BLOCK, BLOCK)])
        copy = remote(m.sa.at[p, j], m.ra.at[p, j], m.a_s.at[p, j], m.a_r.at[p, j], across)
        copy.start()
        return copy

    def send_sum(e, j, copy):
        p = e % 2
        copy.wait()
        m.sb[p, j] = low(m.part[j, rows(s * BLOCK, BLOCK)] + wide(m.ra[p, j]))
        copy = remote(m.sb.at[p, j], m.rb.at[p, j], m.b_s.at[p, j], m.b_r.at[p, j], along)
        copy.start()
        return copy

    def summed(e, j, copy):
        p = e % 2
        copy.wait()
        return wide(m.sb[p, j]) + wide(m.rb[p, j])

    def share_rows(e, j, ref):
        block = ref.at[own_rows(j)]
        copy = remote(block, block, m.c_s.at[e, j], m.c_r.at[e, j], across)
        copy.start()
        return copy

    def lanes_of(size, width):
        return lax.broadcasted_iota(jnp.int32, (size, width), 1)

    pairs = 2 * BLOCK
    length = jnp.where(zh == 0, length_ref[0:1, 0:1], length_ref[1:2, 0:1])
    cos_ref, sin_ref = m.cos, m.sin
    live_keys = lanes_of(pairs, slots) < length
    scale = HEAD_DIM ** (-0.5)

    def make_tables():
        lane = lanes_of(slots, LANES) % (HEAD_DIM // 2)
        freq = jnp.exp(wide(lane) * (-2.0 / HEAD_DIM * math.log(1000.0)))
        angle = wide(lax.broadcasted_iota(jnp.int32, (slots, LANES), 0)) * freq
        sine = jnp.sin(angle)
        m.cos[...] = jnp.cos(angle)
        m.sin[...] = jnp.where(lanes_of(slots, LANES) % HEAD_DIM < HEAD_DIM // 2, -sine, sine)

    def param(l, i):
        return m.par[l, pl.ds(NORM_ROW + i, 1), :]

    def read_params(l):
        for i in range(width // LANES):
            cols = pl.ds(i * LANES, LANES)
            m.par[l, :, cols] = jnp.transpose(wide(m.wq[l, cols, pl.ds(QKV_PAD - LANES, LANES)]))

    def project(l, j):
        here = chunk(j)
        joined = dot(m.x[l, here], m.wq[l])
        cosine, sine = cos_ref[here], sin_ref[here]
        for h in range(3):
            values = joined[:, h * LANES:(h + 1) * LANES]
            values = values * cosine + turned(values) * sine
            m.q[l, h, here] = low(jnp.where(lanes_of(pairs, LANES) < HEAD_DIM, values, 0.0))
            m.k[l, h, here] = low(pltpu.roll(values, HEAD_DIM, 1))
        m.v[l, here] = low(jnp.where(lanes_of(pairs, 256) < 3 * HEAD_DIM, joined[:, 3 * LANES:], 0.0))

    def attend(l, j):
        here = chunk(j)
        total = jnp.zeros((pairs, 256), jnp.float32)
        for h in range(3):
            scores = dot_rows(m.q[l, h, here], m.k[l, h]) * scale
            scores = jnp.where(live_keys, scores, masked_score)
            top = jnp.max(scores, axis=-1, keepdims=True)
            weights = jnp.exp(scores - top)
            weights = low(weights / jnp.sum(weights, axis=-1, keepdims=True))
            m.pr[l, h, here] = weights
            inside = lanes_of(pairs, 256) // HEAD_DIM == h
            total = jnp.where(inside, dot(weights, m.v[l]), total)
        m.mix[l, here] = low(total)

    def normed(values):
        centre = values - jnp.mean(values, axis=-1, keepdims=True)
        inverse = lax.rsqrt(jnp.mean(centre * centre, axis=-1, keepdims=True) + norm_eps)
        return centre * inverse, inverse

    def finish_attention(e, l, j, copy):
        values = wide(m.x[l, own_rows(j)]) + summed(e, j, copy)
        norm, inverse = normed(values)
        m.n1[l, kept(j)] = norm
        m.i1[l, kept(j)] = jnp.broadcast_to(inverse, (BLOCK, LANES))
        hidden = norm * param(l, 0) + param(l, 1)
        m.hidf[kept(j)] = hidden
        m.hid[l, own_rows(j)] = low(hidden)
        return share_rows(l, j, m.hid.at[l])

    def feed(l, j):
        here = chunk(j)
        rows_in = m.hid[l, here]
        gate = dot(rows_in, m.wgu[l, :, pl.ds(0, fpart)])
        up = dot(rows_in, m.wgu[l, :, pl.ds(fpart, fpart)])
        m.gu[l, here, pl.ds(0, fpart)] = low(gate)
        m.gu[l, here, pl.ds(fpart, fpart)] = low(up)
        m.act[l, here] = low(gate * jax.nn.sigmoid(gate) * up)

    def finish_feed(e, l, j, copy):
        values = m.hidf[kept(j)] + summed(e, j, copy)
        norm, inverse = normed(values)
        m.n2[l, kept(j)] = norm
        m.i2[l, kept(j)] = jnp.broadcast_to(inverse, (BLOCK, LANES))
        result = low(norm * param(l, 2) + param(l, 3))
        if l == 0:
            m.x[1, own_rows(j)] = result
            return share_rows(2, j, m.x.at[1])
        m.outb[kept(j)] = result
        return None

    counts = jnp.where(zp == 0, 1.0, 0.0)

    def add_norm_grads(l, i, dy, norm):
        for k, value in enumerate((dy * norm, dy)):
            at = pl.ds(NORM_ROW + i + k, 1)
            m.ng[l, at, :] += jnp.sum(value, axis=0, keepdims=True) * counts

    def norm_grad(dy, norm, inverse, gain):
        scaled = dy * gain
        return inverse * (
            scaled - jnp.mean(scaled, axis=-1, keepdims=True)
            - norm * jnp.mean(scaled * norm, axis=-1, keepdims=True))

    def back_second(l, j):
        dy = m.dy[kept(j)]
        norm = m.n2[l, kept(j)]
        add_norm_grads(l, 2, dy, norm)
        grad = norm_grad(dy, norm, m.i2[l, kept(j), pl.ds(0, 1)], param(l, 2))
        m.dres[kept(j)] = grad
        m.dfed[l, own_rows(j)] = low(grad)
        return share_rows(3 + l, j, m.dfed.at[l])

    def back_feed(l, j):
        here = chunk(j)
        dact = dot_rows(m.dfed[l, here], m.wd[l])
        gate = wide(m.gu[l, here, pl.ds(0, fpart)])
        up = wide(m.gu[l, here, pl.ds(fpart, fpart)])
        sig = jax.nn.sigmoid(gate)
        m.dgu[here, pl.ds(0, fpart)] = low(dact * up * sig * (1.0 + gate * (1.0 - sig)))
        m.dgu[here, pl.ds(fpart, fpart)] = low(dact * gate * sig)

    def back_first(e, l, j, copy):
        dhidden = m.dres[kept(j)] + summed(e, j, copy)
        norm = m.n1[l, kept(j)]
        add_norm_grads(l, 0, dhidden, norm)
        grad = norm_grad(dhidden, norm, m.i1[l, kept(j), pl.ds(0, 1)], param(l, 0))
        m.dres[kept(j)] = grad
        m.datt[l, own_rows(j)] = low(grad)
        return share_rows(5 + l, j, m.datt.at[l])

    def back_mix(l, j):
        m.dmix[chunk(j)] = low(dot_rows(m.datt[l, chunk(j)], m.wo[l]))

    def back_attend(l, h):
        @pl.loop(0, 2)
        def _(i):
            here = rows(i * pairs, pairs)
            grad = m.dmix[here]
            grad = jnp.where(lanes_of(pairs, 256) // HEAD_DIM == h, grad, jnp.zeros_like(grad))
            dprobs = dot_rows(grad, m.v[l])
            probs = wide(m.pr[l, h, here])
            centre = jnp.sum(dprobs * probs, axis=-1, keepdims=True)
            dscores = low(probs * (dprobs - centre))
            m.ds[here] = dscores
            m.dq[here] = dot(dscores, m.k[l, h]) * scale

        dkey = dot_cols(m.ds[...], m.q[l, h]) * scale
        values = jnp.where(lanes_of(slots, LANES) < HEAD_DIM, m.dq[...], pltpu.roll(dkey, HEAD_DIM, 1))
        values = values * cos_ref[...] - turned(values) * sin_ref[...]
        m.dqkv[:, pl.ds(h * LANES, LANES)] = low(values)
        dvalue = low(dot_cols(m.pr[l, h], m.dmix[...]))
        before = jnp.zeros_like(dvalue) if h == 0 else m.dqkv[:, pl.ds(3 * LANES, 256)]
        inside = lanes_of(slots, 256) // HEAD_DIM == h
        m.dqkv[:, pl.ds(3 * LANES, 256)] = jnp.where(inside, dvalue, before)

    def weight_grad(l, kind):
        left, right = (
            (m.x.at[l], m.dqkv), (m.hid.at[l], m.dgu), (m.mix.at[l], m.datt.at[l]),
            (m.act.at[l], m.dfed.at[l]),
        )[kind]

        @pl.loop(0, left.shape[1] // pairs)
        def _(i):
            cols = pl.ds(pl.multiple_of(i * pairs, pairs), pairs)
            grad = dot_cols(left[:, cols], right[...])
            if kind == Q:
                tail = grad[:, QKV_PAD - LANES:] + jnp.transpose(m.ng[l, :, cols])
                weight[kind][l, cols, pl.ds(0, QKV_PAD - LANES)] = low(grad[:, :QKV_PAD - LANES])
                weight[kind][l, cols, pl.ds(QKV_PAD - LANES, LANES)] = low(tail)
            else:
                weight[kind][l, cols] = low(grad)

    first_in = [m.r1q, m.r1g, m.r1o, m.r1d]
    second_out = [m.s2q, m.s2g, m.s2o, m.s2d]
    second_in = [m.r2q, m.r2g, m.r2o, m.r2d]
    third_out = [m.s3q, m.s3g, m.s3o, m.s3d]
    final = [(oq_ref, on_ref), (og_ref, ou_ref), (oo_ref,), (od_ref,)]

    def blocks_of(kind):
        return range(4 if kind in (Q, G) else 1)

    def grad_rows(kind, b, rep):
        n = count[kind]
        return rows((b * part if kind in (Q, G) else 0) + rep * n, n)

    def plane_first(l, kind):
        n = count[kind]
        first, second = halves_of(kind, weight[kind].shape[2])
        for b in blocks_of(kind):
            for slot, rep in ((1, r_of[3]), (0, None)):
                for lanes, device, near, sem in ((first, xn, r_of[1], m.s1a), (second, yn, r_of[2], m.s1b)):
                    block = grad_rows(kind, b, near if rep is None else rep)
                    remote(
                        weight[kind].at[l, block, lanes], first_in[kind].at[l, slot, pl.ds(b * n, n), lanes],
                        m.s1s.at[l, kind], sem.at[l, kind], device).start()

    def plane_second(l, kind):
        n = count[kind]
        first, second = halves_of(kind, weight[kind].shape[2])
        for lanes, device, rep, sem in ((first, yn, r_of[2], m.s1a), (second, xn, r_of[1], m.s1b)):
            wait_for(first_in[kind].at[l, pl.ds(0, 2), :, lanes], sem.at[l, kind])
            for b in blocks_of(kind):
                block = grad_rows(kind, b, rep)
                here = pl.ds(b * n, n)
                weight[kind][l, block, lanes] = low(
                    wide(weight[kind][l, block, lanes]) + wide(first_in[kind][l, 1, here, lanes]))
                remote(
                    weight[kind].at[l, block, lanes], first_in[kind].at[l, 2, here, lanes],
                    m.s1t.at[l, kind], m.s1r.at[l, kind], device).start()

    def spread_line(l, kind):
        n = count[kind]
        wait_for(first_in[kind].at[l, 2], m.s1r.at[l, kind])
        for b in blocks_of(kind):
            here = pl.ds(b * n, n)
            total = wide(weight[kind][l, grad_rows(kind, b, r)])
            total += wide(first_in[kind][l, 0, here]) + wide(first_in[kind][l, 2, here])
            second_out[kind][l, here] = low(total)
        if kind in (Q, G):
            slot = 2 * z + s
            for k in range(4):
                src = second_out[kind].at[l, rows(z_of[k] * n, n)]
                dst = second_in[kind].at[slot]
                if k == 0:
                    @pl.when(s == l)
                    def _():
                        pltpu.make_async_copy(src, dst, m.s2r.at[kind]).start()

                    @pl.when(s != l)
                    def _():
                        remote(src, dst, m.s2s.at[l, kind], m.s2r.at[kind], across).start()
                else:
                    remote(src, dst, m.s2s.at[l, kind], m.s2r.at[kind], (l, z_of[k], r)).start()
        else:
            src, dst = second_out[kind].at[l], second_in[kind].at[zh]
            is_self = (t == z) & (s == l)

            @pl.when(is_self)
            def _():
                pltpu.make_async_copy(src, dst, m.s2r.at[kind]).start()

            @pl.when(jnp.logical_not(is_self))
            def _():
                remote(src, dst, m.s2s.at[l, kind], m.s2r.at[kind], (l, t, r)).start()

    def line_done(l, kind):
        wait_for(first_in[kind].at[l, pl.ds(0, 2)], m.s1s.at[l, kind])
        wait_for(first_in[kind].at[l, 2], m.s1t.at[l, kind])
        n = count[kind]
        if kind in (Q, G):
            @pl.when(s == l)
            def _():
                wait_for(second_out[kind].at[l, pl.ds(0, 3 * n)], m.s2s.at[l, kind])

            @pl.when(s != l)
            def _():
                wait_for(second_out[kind].at[l], m.s2s.at[l, kind])
        else:
            @pl.when(jnp.logical_not((t == z) & (s == l)))
            def _():
                wait_for(second_out[kind].at[l], m.s2s.at[l, kind])

    def in_order(parts):
        low_half = lax.broadcasted_iota(jnp.int32, (share, LANES), 1) < HEAD_DIM

        def swapped(values):
            return pltpu.roll(values, HEAD_DIM, 1)

        def pair(head):
            return parts[head // 3][:, head % 3 * LANES:(head % 3 + 1) * LANES]

        def value(head, at_low):
            h = head % 3
            start = 3 * LANES + h // 2 * LANES
            values = parts[head // 3][:, start:start + LANES]
            return values if (h != 1) == at_low else swapped(values)

        for c in range(HEADS // 2):
            even, odd = pair(2 * c), pair(2 * c + 1)
            for i, values in enumerate((
                jnp.where(low_half, even, swapped(odd)), jnp.where(low_half, swapped(even), odd),
                jnp.where(low_half, value(2 * c, True), value(2 * c + 1, False)),
            )):
                m.s3q[:, pl.ds(i * width + c * LANES, LANES)] = low(values)
        norms = sum(values[:, QKV_PAD - LANES:] for values in parts)
        m.s3q[:, pl.ds(3 * width, LANES)] = low(norms)

    def out_halves(kind):
        if kind == G:
            return [(og_ref, pl.ds(0, og_ref.shape[1]))], [(ou_ref, pl.ds(0, ou_ref.shape[1]))]
        ref = final[kind][0]
        middle = ref.shape[1] // 2
        first, second = [(ref, pl.ds(0, middle))], [(ref, pl.ds(middle, middle))]
        return first, second + [(on_ref, pl.ds(0, LANES))] if kind == Q else second

    def finish(kind):
        wait_for(second_in[kind], m.s2r.at[kind])
        if kind in (Q, G):
            parts = []
            for b in range(4):
                near = 2 * (b // 2) + b % 2
                parts.append(wide(second_in[kind][near]) + wide(second_in[kind][near + 4]))
                if kind == G:
                    for i in range(2):
                        m.s3g[:, pl.ds((4 * i + b) * fpart, fpart)] = low(parts[b][:, i * fpart:(i + 1) * fpart])
            if kind == Q:
                in_order(parts)
        else:
            third_out[kind][...] = low(wide(second_in[kind][0]) + wide(second_in[kind][1]))
        here = rows(r * count[kind], count[kind])
        start = 0
        for ref in final[kind]:
            src, dst = third_out[kind].at[:, pl.ds(start, ref.shape[1])], ref.at[here]
            start += ref.shape[1]
            remote(src, dst, m.s3s.at[kind, 0], m.s3x.at[kind], xn).start()
            remote(src, dst, m.s3s.at[kind, 1], m.s3y.at[kind], yn).start()
            pltpu.make_async_copy(src, dst, m.s3l.at[kind]).start()

    def finish_half(kind):
        n = count[kind]
        for parts, rep, device, sem in zip(out_halves(kind), r_of[1:3], (yn, xn), (m.s3x, m.s3y)):
            wait_for(third_out[kind], sem.at[kind])
            for ref, lanes in parts:
                half = ref.at[rows(rep * n, n), lanes]
                remote(half, half, m.s3t.at[kind], m.s3e.at[kind], device).start()

    def finish_done(kind):
        block = third_out[kind]
        wait_for(block, m.s3l.at[kind])
        wait_for(block, m.s3e.at[kind])
        wait_for(third_out[kind], m.s3s.at[kind, 0])
        wait_for(third_out[kind], m.s3s.at[kind, 1])
        wait_for(block, m.s3t.at[kind])

    def send_rows(i, src, dst, step):
        block = src.at[rows(zp * BLOCK, BLOCK)]
        is_self = (zh == s) & (t == z)

        @pl.when(is_self)
        def _():
            if step == "start":
                pltpu.make_async_copy(block, dst, m.o_r.at[i]).start()

        @pl.when(jnp.logical_not(is_self))
        def _():
            copy = remote(block, dst, m.o_s.at[i], m.o_r.at[i], (zh, t, r))
            if step == "start":
                copy.start()
            else:
                copy.wait_send()

        if step == "wait":
            wait_for(dst, m.o_r.at[i])

    raw_copy = pltpu.make_async_copy(wq_ref.at[0], m.qraw, m.raw)

    def pack_weights():
        raw_copy.wait()
        low_half = lanes_of(part, LANES) < HEAD_DIM

        def column(i, head, at_low):
            values = wide(m.qraw[:, pl.ds(i * width + head // 2 * LANES, LANES)])
            return values if (head % 2 == 0) == at_low else pltpu.roll(values, HEAD_DIM, 1)

        m.aux[...] = jnp.zeros(m.aux.shape, jnp.float32)
        for i, ref in enumerate((g1_ref, b1_ref, g2_ref, b2_ref)):
            m.aux[pl.ds(NORM_ROW + i, 1)] = wide(ref[...])
        norms = jnp.transpose(m.aux[...])
        for c in range(4):
            heads = [3 * c + h for h in range(3)]
            for h, head in enumerate(heads):
                m.qpk[c, :, pl.ds(h * LANES, LANES)] = low(
                    jnp.where(low_half, column(0, head, True), column(1, head, False)))
            m.qpk[c, :, pl.ds(3 * LANES, LANES)] = low(
                jnp.where(low_half, column(2, heads[0], True), column(2, heads[1], False)))
            m.qpk[c, :, pl.ds(4 * LANES, LANES)] = low(jnp.where(low_half, column(2, heads[2], True), norms))

    def where_moved(kind, step):
        if kind in (Q, G):
            step()
        else:
            pl.when(t != z)(step)

    def on(l, kind, k):
        where_moved(kind, lambda: pass_on(l, kind, k))

    def half(l, kind, k):
        where_moved(kind, lambda: pass_half(l, kind, k))

    near, far = m.x.at[0, near_block], m.x.at[0, far_block]
    near_along = remote(near, near, m.tz_s.at[0], m.tz_r.at[0], along)
    near_across = remote(near, near, m.xc_s.at[0], m.xc_r.at[0], across)
    far_across = remote(far, far, m.xc_s.at[1], m.xc_r.at[1], across)
    cot_block = m.cot.at[rows(zp * BLOCK, BLOCK)]
    cot_along = remote(cot_block, cot_block, m.tz_s.at[1], m.tz_r.at[1], along)

    def share_tokens_near():
        wait_for(near, m.tok_r)
        near_along.start()
        near_across.start()

    def share_tokens_far():
        near_along.wait_send()
        wait_for(far, m.tz_r.at[0])
        far_across.start()

    def tokens_shared():
        near_across.wait()
        far_across.wait()

    def cotangent_along():
        wait_for(cot_block, m.cot_r)
        cot_along.start()

    def forward_end():
        send_rows(0, m.outb, out_ref.at[0, 0], "start")
        for l in range(2):
            source_done(l)
            for kind in (Q, O, G, D):
                forward_done(l, kind)
        cot_along.wait_send()
        wait_for(m.cot.at[rows((1 - zp) * BLOCK, BLOCK)], m.tz_r.at[1])
        for j in range(2):
            slot = (2 * j + s) * BLOCK + lax.broadcasted_iota(jnp.int32, (BLOCK, width), 0)
            m.dy[kept(j)] = jnp.where(slot < length, wide(m.cot[kept(j)]), 0.0)

    def layer_done(l, j, copy):
        result = low(m.dres[kept(j)] + summed(5 if l == 1 else 7, j, copy))
        if l == 1:
            m.dy[kept(j)] = wide(result)
        else:
            m.tgb[kept(j)] = result

    def finish_on(l, kind):
        pl.when(s == l)(lambda: finish(kind))

    def half_on(l, kind):
        pl.when(s == l)(lambda: finish_half(kind))

    def all_done():
        for kind in (D, G, O, Q):
            finish_done(kind)
            for l in (1, 0):
                line_done(l, kind)
        scatter_rows(*tok_args, "wait")
        scatter_rows(*cot_args, "wait")
        send_rows(0, m.outb, out_ref.at[0, 0], "wait")
        send_rows(1, m.tgb, tg_ref.at[0, 0], "wait")

    raw_copy.start()
    scatter_rows(*tok_args, "start")
    source(0, (O,))
    pack_weights()
    source(0, (Q,))
    for l in range(2):
        m.wo[l, pl.ds(part, 256 - part)] = jnp.zeros((256 - part, width), jnp.bfloat16)
        m.ng[l] = jnp.zeros((LANES, width), jnp.float32)
    on(0, Q, 1)
    half(0, Q, 1)
    make_tables()
    on(0, O, 1)
    share_tokens_near()
    source(0, (G,))
    on(0, Q, 2)
    on(0, Q, 3)
    half(0, O, 1)
    half(0, Q, 3)
    half(0, Q, 2)
    share_tokens_far()
    on(0, G, 1)
    need(0, Q)
    source(0, (D,))
    read_params(0)
    tokens_shared()
    project(0, 0)
    project(0, 1)
    attend(0, 0)
    on(0, G, 2)
    need(0, O)
    a0 = send_partial(0, 0, m.mix.at[0], m.wo[0], dot)
    attend(0, 1)
    b0 = send_sum(0, 0, a0)
    a1 = send_partial(0, 1, m.mix.at[0], m.wo[0], dot)
    b1 = send_sum(0, 1, a1)
    on(0, G, 3)
    half(0, G, 1)
    source(1, (O,))
    source(1, (Q,))
    source(1, (G,))
    half(0, G, 2)
    half(0, G, 3)
    on(0, D, 2)
    on(0, D, 3)
    c0 = finish_attention(0, 0, 0, b0)
    need(0, G)
    on(0, D, 1)
    half(0, D, 3)
    half(0, D, 1)
    on(1, Q, 1)
    c0.wait()
    on(1, Q, 3)
    feed(0, 0)
    half(0, D, 2)
    c1 = finish_attention(0, 0, 1, b1)
    on(1, Q, 2)
    need(0, D)
    a0 = send_partial(1, 0, m.act.at[0], m.wd[0], dot)
    on(1, G, 1)
    c1.wait()
    on(1, O, 1)
    half(1, Q, 1)
    b0 = send_sum(1, 0, a0)
    feed(0, 1)
    half(1, Q, 2)
    a1 = send_partial(1, 1, m.act.at[0], m.wd[0], dot)
    half(1, G, 1)
    b1 = send_sum(1, 1, a1)
    source(1, (D,))
    half(1, Q, 3)
    half(1, O, 1)
    on(1, G, 2)
    need(1, Q)
    on(1, G, 3)
    read_params(1)
    c0 = finish_feed(1, 0, 0, b0)
    c1 = finish_feed(1, 0, 1, b1)
    c0.wait()
    project(1, 0)
    half(1, G, 2)
    scatter_rows(*cot_args, "start")
    c1.wait()
    on(1, D, 1)
    project(1, 1)
    attend(1, 0)
    need(1, O)
    a0 = send_partial(2, 0, m.mix.at[1], m.wo[1], dot)
    attend(1, 1)
    on(1, D, 2)
    b0 = send_sum(2, 0, a0)
    half(1, G, 3)
    a1 = send_partial(2, 1, m.mix.at[1], m.wo[1], dot)
    b1 = send_sum(2, 1, a1)
    on(1, D, 3)
    half(1, D, 1)
    cotangent_along()
    half(1, D, 2)
    c0 = finish_attention(2, 1, 0, b0)
    half(1, D, 3)
    need(1, G)
    c0.wait()
    feed(1, 0)
    c1 = finish_attention(2, 1, 1, b1)
    need(1, D)
    a0 = send_partial(3, 0, m.act.at[1], m.wd[1], dot)
    c1.wait()
    b0 = send_sum(3, 0, a0)
    feed(1, 1)
    a1 = send_partial(3, 1, m.act.at[1], m.wd[1], dot)
    b1 = send_sum(3, 1, a1)
    finish_feed(3, 1, 0, b0)
    finish_feed(3, 1, 1, b1)
    forward_end()
    c0 = back_second(1, 0)
    c1 = back_second(1, 1)
    c0.wait()
    back_feed(1, 0)
    a0 = send_partial(4, 0, m.dgu, m.wgu[1], dot_rows)
    c1.wait()
    back_feed(1, 1)
    b0 = send_sum(4, 0, a0)
    a1 = send_partial(4, 1, m.dgu, m.wgu[1], dot_rows)
    weight_grad(1, D)
    plane_first(1, D)
    b1 = send_sum(4, 1, a1)
    weight_grad(1, G)
    plane_first(1, G)
    c0 = back_first(4, 1, 0, b0)
    c1 = back_first(4, 1, 1, b1)
    c0.wait()
    back_mix(1, 0)
    c1.wait()
    back_mix(1, 1)
    back_attend(1, 0)
    back_attend(1, 1)
    back_attend(1, 2)
    a0 = send_partial(5, 0, m.dqkv, m.wq[1], dot_rows)
    a1 = send_partial(5, 1, m.dqkv, m.wq[1], dot_rows)
    b0 = send_sum(5, 0, a0)
    weight_grad(1, O)
    plane_first(1, O)
    plane_second(1, D)
    b1 = send_sum(5, 1, a1)
    weight_grad(1, Q)
    plane_first(1, Q)
    spread_line(1, D)
    layer_done(1, 0, b0)
    plane_second(1, G)
    layer_done(1, 1, b1)
    c0 = back_second(0, 0)
    c1 = back_second(0, 1)
    c0.wait()
    back_feed(0, 0)
    a0 = send_partial(6, 0, m.dgu, m.wgu[0], dot_rows)
    c1.wait()
    back_feed(0, 1)
    b0 = send_sum(6, 0, a0)
    a1 = send_partial(6, 1, m.dgu, m.wgu[0], dot_rows)
    weight_grad(0, D)
    plane_first(0, D)
    b1 = send_sum(6, 1, a1)
    weight_grad(0, G)
    spread_line(1, G)
    plane_first(0, G)
    c0 = back_first(6, 0, 0, b0)
    plane_second(1, O)
    plane_second(0, D)
    c1 = back_first(6, 0, 1, b1)
    c0.wait()
    back_mix(0, 0)
    c1.wait()
    back_mix(0, 1)
    back_attend(0, 0)
    back_attend(0, 1)
    back_attend(0, 2)
    a0 = send_partial(7, 0, m.dqkv, m.wq[0], dot_rows)
    plane_second(1, Q)
    a1 = send_partial(7, 1, m.dqkv, m.wq[0], dot_rows)
    b0 = send_sum(7, 0, a0)
    weight_grad(0, O)
    plane_first(0, O)
    b1 = send_sum(7, 1, a1)
    spread_line(1, O)
    finish_on(1, O)
    weight_grad(0, Q)
    plane_first(0, Q)
    spread_line(0, D)
    plane_second(0, G)
    finish_on(1, G)
    layer_done(0, 0, b0)
    spread_line(1, Q)
    layer_done(0, 1, b1)
    plane_second(0, Q)
    spread_line(0, G)
    plane_second(0, O)
    finish_on(1, D)
    send_rows(1, m.tgb, tg_ref.at[0, 0], "start")
    finish_on(0, G)
    finish_on(0, D)
    spread_line(0, O)
    spread_line(0, Q)
    finish_on(0, O)
    finish_on(1, Q)
    half_on(1, D)
    finish_on(0, Q)
    half_on(1, O)
    half_on(1, G)
    half_on(1, Q)
    half_on(0, G)
    half_on(0, O)
    half_on(0, D)
    half_on(0, Q)
    all_done()


def relay(tokens, lengths, cotangent, w_qkv, w_out, norm1_gain, norm1_bias, w_gate, w_up, w_down, norm2_gain, norm2_bias):
    bf = jnp.bfloat16
    part, width = w_qkv.shape[1], tokens.shape[3]
    hidden = w_gate.shape[2]
    scratch = relay_scratch(width, hidden)
    any_space = pl.BlockSpec(memory_space=pl.ANY)
    fpart = hidden // 4
    outs = pl.pallas_call(
        functools.partial(relay_kernel, tuple(scratch)),
        out_shape=(
            jax.ShapeDtypeStruct(tokens.shape, bf), jax.ShapeDtypeStruct(tokens.shape, bf),
            jax.ShapeDtypeStruct((part, 3 * width), bf), jax.ShapeDtypeStruct((part, LANES), bf),
            jax.ShapeDtypeStruct((part, width), bf),
            jax.ShapeDtypeStruct((part, hidden), bf), jax.ShapeDtypeStruct((part, hidden), bf),
            jax.ShapeDtypeStruct((fpart, width), bf),
        ),
        in_specs=[pl.BlockSpec(memory_space=pltpu.VMEM)] * 5 + [any_space] * 7,
        out_specs=[any_space] * 8,
        scratch_shapes=list(scratch.values()),
        compiler_params=pltpu.CompilerParams(
            collective_id=1, has_side_effects=True, vmem_limit_bytes=VMEM_LIMIT),
    )(lengths, norm1_gain, norm1_bias, norm2_gain, norm2_bias, tokens, cotangent, w_qkv, w_out, w_gate, w_up, w_down)
    output, token_grad, *grads = outs
    grad_q, norms, grad_out, grad_gate, grad_up, grad_down = (grad.astype(jnp.float32)[None] for grad in grads)
    norms = norms[:, :, NORM_ROW:NORM_ROW + 4]
    return (
        output, token_grad, grad_q, grad_out, norms[:, :, 0], norms[:, :, 1],
        grad_gate, grad_up, grad_down, norms[:, :, 2], norms[:, :, 3],
    )


def fits_relay(args):
    tokens, lengths, w_qkv, w_gate, w_down = args[0], args[1], args[3], args[7], args[9]
    axes = tuple(lax.axis_size(axis) for axis in ("section", "fsdp", "rep"))
    return (
        axes == (2, 4, 4)
        and tokens.shape == (1, 1, BLOCK, 768)
        and lengths.shape == (2, 1)
        and w_qkv.shape == (1, 192, 2304)
        and w_gate.shape == (1, 192, 3072)
        and w_down.shape == (1, 768, 768)
    )


def program(*args):
    return relay(*args) if fits_relay(args) else shards(*args)


def solution(mesh):
    return jax.shard_map(
        program,
        mesh=mesh,
        in_specs=(
            P("section", "rep", "fsdp", None),
            P(None, "rep"),
            P("section", "rep", "fsdp", None),
            P("section", "fsdp", None),
            P("section", "fsdp", None),
            P("section", "fsdp"),
            P("section", "fsdp"),
            P("section", "fsdp", None),
            P("section", "fsdp", None),
            P("section", "fsdp", None),
            P("section", "fsdp"),
            P("section", "fsdp"),
        ),
        out_specs=(
            P("section", "rep", "fsdp", None),
            P("section", "rep", "fsdp", None),
            P("section", "fsdp", None),
            P("section", "fsdp", None),
            P("section", "fsdp"),
            P("section", "fsdp"),
            P("section", "fsdp", None),
            P("section", "fsdp", None),
            P("section", "fsdp", None),
            P("section", "fsdp"),
            P("section", "fsdp"),
        ),
        check_vma=False,
    )
```

```python
import functools
import math
import types

import jax
import jax.numpy as jnp
from jax import lax
from jax.experimental import pallas as pl
from jax.experimental.pallas import tpu as pltpu
from jax.sharding import PartitionSpec as P

HEADS = 12
HEAD_DIM = 64


norm_eps = 1e-05
masked_score = -1000000000.0
VMEM_LIMIT = 62 * 2**20


def partner(block, axis, distance):
    count = lax.axis_size(axis)
    route = []
    for low in range(count):
        high = low | 1 << distance
        if high != low and high < count:
            route += [(low, high), (high, low)]
    return lax.ppermute(block, axis, route)


def shifted(value, axis, steps):
    count = lax.axis_size(axis)
    initial, last = (max(0, -steps), min(count, count - steps))
    return lax.ppermute(value, axis, [(source, source + steps) for source in range(initial, last)])


def norm_rows(values, norm_gain, offset):
    centre = values - jnp.mean(values, axis=-1, keepdims=True)
    inverse = lax.rsqrt(jnp.mean(centre * centre, axis=-1, keepdims=True) + norm_eps)
    normed = centre * inverse
    return (normed * norm_gain + offset, normed, inverse)


def norm_back(grad_out, normed, inverse, norm_gain):
    scaled = grad_out * norm_gain
    return inverse * (
        scaled
        - jnp.mean(scaled, axis=-1, keepdims=True)
        - normed * jnp.mean(scaled * normed, axis=-1, keepdims=True)
    )


def rotary_tables(first_slot, row_count):
    half_dim = HEAD_DIM // 2
    inverse_freq = 1000.0 ** (-2.0 * jnp.arange(half_dim, dtype=jnp.float32) / HEAD_DIM)
    places = (first_slot + jnp.arange(row_count)).astype(jnp.float32)
    angles = places[:, None] * inverse_freq[None, :]
    angles = jnp.concatenate([angles, angles], axis=-1)[:, None, :]
    return (jnp.cos(angles), jnp.sin(angles))


def turn_half(values):
    half_dim = values.shape[-1] // 2
    return jnp.concatenate([-values[..., half_dim:], values[..., :half_dim]], axis=-1)


def rotate(values, cosine_table, sine_table):
    return values * cosine_table + turn_half(values) * sine_table


def rotate_back(values, cosine_table, sine_table):
    return values * cosine_table - turn_half(values) * sine_table


def masked_scores(query_rot, key_all, live_keys):
    key_heads = key_all.reshape(key_all.shape[0], HEADS, HEAD_DIM)
    scores = jnp.einsum(
        "qhd,khd->hqk", query_rot, key_heads, preferred_element_type=jnp.float32
    ) * HEAD_DIM ** (-0.5)
    return jnp.where(live_keys[None, None, :], scores, masked_score)


def batch_length(length_column, batch_now):
    picked = jnp.clip(batch_now, 0, length_column.shape[0] - 1)
    return lax.dynamic_index_in_dim(length_column, picked, 0, keepdims=False)


def layer_forward(inputs, weights, live_keys, cosine_table, sine_table):
    w_qkv, w_out, gain_one, offset_one, w_gate, w_up, w_down, gain_two, offset_two = weights
    row_count, model_width = inputs.shape
    head_shape = (row_count, HEADS, HEAD_DIM)
    inputs_low = inputs.astype(jnp.bfloat16)
    joined = jnp.dot(inputs_low, w_qkv, preferred_element_type=jnp.float32)
    query_rot = rotate(
        joined[:, :model_width].reshape(head_shape), cosine_table, sine_table
    ).astype(jnp.bfloat16)
    key_own = (
        rotate(
            joined[:, model_width : 2 * model_width].reshape(head_shape), cosine_table, sine_table
        )
        .reshape(row_count, model_width)
        .astype(jnp.bfloat16)
    )
    value_own = joined[:, 2 * model_width :].astype(jnp.bfloat16)
    key_all, value_all = (
        lax.all_gather(key_own, "fsdp", axis=0, tiled=True),
        lax.all_gather(value_own, "fsdp", axis=0, tiled=True),
    )
    scores = masked_scores(query_rot, key_all, live_keys)
    highest = jnp.max(scores, axis=-1, keepdims=True)
    log_total = highest + jnp.log(jnp.sum(jnp.exp(scores - highest), axis=-1, keepdims=True))
    softmax_weights = jnp.exp(scores - log_total).astype(jnp.bfloat16)
    value_heads = value_all.reshape(value_all.shape[0], HEADS, HEAD_DIM)
    mixed_heads = jnp.einsum(
        "hqk,khd->qhd", softmax_weights, value_heads, preferred_element_type=jnp.float32
    )
    mixed_heads = mixed_heads.reshape(row_count, model_width).astype(jnp.bfloat16)
    attended = jnp.dot(mixed_heads, w_out, preferred_element_type=jnp.float32)
    hidden, normed_one, inverse_one = norm_rows(inputs + attended, gain_one, offset_one)
    hidden_low = hidden.astype(jnp.bfloat16)
    gate_proj = jnp.dot(hidden_low, w_gate, preferred_element_type=jnp.float32)
    upward = jnp.dot(hidden_low, w_up, preferred_element_type=jnp.float32)
    product = (jax.nn.silu(gate_proj) * upward).astype(jnp.bfloat16)
    mlp_out = jnp.dot(product, w_down, preferred_element_type=jnp.float32)
    result, normed_two, inverse_two = norm_rows(hidden + mlp_out, gain_two, offset_two)
    key_saved, value_saved = (key_all, value_all)
    kept_state = (
        inputs_low,
        query_rot,
        key_saved,
        value_saved,
        log_total,
        mixed_heads,
        normed_one,
        inverse_one,
        hidden_low,
        gate_proj,
        upward,
        product,
        normed_two,
        inverse_two,
    )
    return (result, kept_state)


def layer_backward(grad_out, kept_state, weights, live_keys, cosine_table, sine_table):
    w_qkv, w_out, gain_one, offset_one, w_gate, w_up, w_down, gain_two, offset_two = weights
    (
        inputs_low,
        query_rot,
        key_saved,
        value_saved,
        log_total,
        mixed_heads,
        normed_one,
        inverse_one,
        hidden_low,
        gate_proj,
        upward,
        product,
        normed_two,
        inverse_two,
    ) = kept_state
    row_count, model_width = inputs_low.shape
    head_shape = (row_count, HEADS, HEAD_DIM)
    key_all, value_all = (key_saved, value_saved)
    grad_gain_two = jnp.sum(grad_out * normed_two, axis=0)
    grad_offset_two = jnp.sum(grad_out, axis=0)
    grad_second = norm_back(grad_out, normed_two, inverse_two, gain_two)
    grad_fed = grad_second.astype(jnp.bfloat16)
    grad_product = jnp.einsum("rd,fd->rf", grad_fed, w_down, preferred_element_type=jnp.float32)
    grad_w_down = jnp.einsum("rf,rd->fd", product, grad_fed, preferred_element_type=jnp.float32)
    sigmoid_gate = jax.nn.sigmoid(gate_proj)
    silu_gate = gate_proj * sigmoid_gate
    grad_gate = (
        grad_product * upward * sigmoid_gate * (1.0 + gate_proj * (1.0 - sigmoid_gate))
    ).astype(jnp.bfloat16)
    grad_upward = (grad_product * silu_gate).astype(jnp.bfloat16)
    grad_hidden = grad_second + jnp.einsum(
        "rf,df->rd", grad_gate, w_gate, preferred_element_type=jnp.float32
    )
    grad_hidden = grad_hidden + jnp.einsum(
        "rf,df->rd", grad_upward, w_up, preferred_element_type=jnp.float32
    )
    grad_w_gate = jnp.einsum("rd,rf->df", hidden_low, grad_gate, preferred_element_type=jnp.float32)
    grad_w_up = jnp.einsum("rd,rf->df", hidden_low, grad_upward, preferred_element_type=jnp.float32)
    grad_gain_one = jnp.sum(grad_hidden * normed_one, axis=0)
    grad_offset_one = jnp.sum(grad_hidden, axis=0)
    grad_first = norm_back(grad_hidden, normed_one, inverse_one, gain_one)
    grad_attended = grad_first.astype(jnp.bfloat16)
    grad_w_out = jnp.einsum(
        "rd,re->de", mixed_heads, grad_attended, preferred_element_type=jnp.float32
    )
    grad_mixed = (
        jnp.einsum("re,de->rd", grad_attended, w_out, preferred_element_type=jnp.float32)
        .astype(jnp.bfloat16)
        .reshape(head_shape)
    )
    scores = masked_scores(query_rot, key_all, live_keys)
    attention = jnp.exp(scores - log_total)
    key_count = key_all.shape[0]
    key_heads = key_all.reshape(key_count, HEADS, HEAD_DIM)
    value_heads = value_all.reshape(key_count, HEADS, HEAD_DIM)
    grad_attention = jnp.einsum(
        "qhd,khd->hqk", grad_mixed, value_heads, preferred_element_type=jnp.float32
    )
    centre_term = jnp.sum(grad_attention * attention, axis=-1, keepdims=True)
    grad_scores = (attention * (grad_attention - centre_term)).astype(jnp.bfloat16)
    score_scale = HEAD_DIM ** (-0.5)
    grad_query = (
        jnp.einsum("hqk,khd->qhd", grad_scores, key_heads, preferred_element_type=jnp.float32)
        * score_scale
    )
    attention_low = attention.astype(jnp.bfloat16)
    grad_value_all = jnp.einsum(
        "hqk,qhd->khd", attention_low, grad_mixed, preferred_element_type=jnp.float32
    )
    grad_key_all = (
        jnp.einsum("hqk,qhd->khd", grad_scores, query_rot, preferred_element_type=jnp.float32)
        * score_scale
    )
    grad_key, grad_value = (
        lax.psum_scatter(
            grad_key_all.reshape(key_count, model_width).astype(jnp.bfloat16),
            "fsdp",
            scatter_dimension=0,
            tiled=True,
        ).astype(jnp.float32),
        lax.psum_scatter(
            grad_value_all.reshape(key_count, model_width).astype(jnp.bfloat16),
            "fsdp",
            scatter_dimension=0,
            tiled=True,
        ).astype(jnp.float32),
    )
    grad_joined = jnp.concatenate(
        [
            rotate_back(grad_query, cosine_table, sine_table).reshape(row_count, model_width),
            rotate_back(grad_key.reshape(head_shape), cosine_table, sine_table).reshape(
                row_count, model_width
            ),
            grad_value,
        ],
        axis=1,
    ).astype(jnp.bfloat16)
    grad_w_qkv = jnp.einsum(
        "rd,re->de", inputs_low, grad_joined, preferred_element_type=jnp.float32
    )
    grad_inputs = grad_first + jnp.einsum(
        "re,de->rd", grad_joined, w_qkv, preferred_element_type=jnp.float32
    )
    weight_grads = (
        grad_w_qkv,
        grad_w_out,
        grad_gain_one,
        grad_offset_one,
        grad_w_gate,
        grad_w_up,
        grad_w_down,
        grad_gain_two,
        grad_offset_two,
    )
    return (grad_inputs, weight_grads)


def shards(
    tokens,
    lengths,
    cotangent,
    w_qkv,
    w_out,
    norm1_gain,
    norm1_bias,
    w_gate,
    w_up,
    w_down,
    norm2_gain,
    norm2_bias,
):
    section_index = lax.axis_index("section")
    fsdp_index = lax.axis_index("fsdp")
    is_first = section_index == 0
    row_count = tokens.shape[2]
    model_width = tokens.shape[3]
    slot_count = row_count * lax.axis_size("fsdp")
    micro_count = lengths.shape[0]
    weights = (
        lax.all_gather(w_qkv[0], "fsdp", axis=0, tiled=True),
        lax.all_gather(w_out[0], "fsdp", axis=0, tiled=True),
        lax.all_gather(norm1_gain[0], "fsdp", axis=0, tiled=True),
        lax.all_gather(norm1_bias[0], "fsdp", axis=0, tiled=True),
        lax.all_gather(w_gate[0], "fsdp", axis=0, tiled=True),
        lax.all_gather(w_up[0], "fsdp", axis=0, tiled=True),
        lax.all_gather(w_down[0], "fsdp", axis=0, tiled=True),
        lax.all_gather(norm2_gain[0], "fsdp", axis=0, tiled=True),
        lax.all_gather(norm2_bias[0], "fsdp", axis=0, tiled=True),
    )
    own_tokens = tokens[0, 0]
    own_cotangent = cotangent[0, 0]
    arrived = partner(jnp.where(is_first, own_cotangent, own_tokens), "section", 0)
    batch_tokens = [
        jnp.where(is_first, own_tokens, arrived),
        jnp.where(is_first, arrived, own_tokens),
    ]
    batch_cotangents = [
        jnp.where(is_first, own_cotangent, arrived),
        jnp.where(is_first, arrived, own_cotangent),
    ]
    cosine_table, sine_table = rotary_tables(fsdp_index * row_count, row_count)
    row_slots = fsdp_index * row_count + jnp.arange(row_count)
    key_slots = jnp.arange(slot_count)
    length_column = lengths[:, 0]
    empty_rows = jnp.zeros((row_count, model_width), jnp.bfloat16)
    carried = empty_rows
    kept_list = []
    layer_outputs = []
    for tick_index in range(micro_count + 1):
        length_now = batch_length(length_column, tick_index - section_index)
        fresh_rows = batch_tokens[tick_index] if tick_index < micro_count else empty_rows
        inputs = jnp.where(is_first, fresh_rows, carried).astype(jnp.float32)
        result, kept_state = layer_forward(
            inputs, weights, key_slots < length_now, cosine_table, sine_table
        )
        result_low = result.astype(jnp.bfloat16)
        kept_list.append(kept_state)
        layer_outputs.append(result_low)
        if tick_index < micro_count:
            carried = shifted(result_low, "section", 1)
    arriving = empty_rows
    totals = None
    owned_total = None
    input_grads = []
    for tick_index in range(micro_count + 1):
        batch_now = tick_index - 1 + section_index
        length_now = batch_length(length_column, batch_now)
        is_valid = (batch_now >= 0) & (batch_now < micro_count)
        seed_rows = batch_cotangents[tick_index] if tick_index < micro_count else empty_rows
        seed_grad = (
            seed_rows.astype(jnp.float32) * (row_slots < length_now).astype(jnp.float32)[:, None]
        )
        grad_out = jnp.where(
            is_valid, jnp.where(is_first, arriving.astype(jnp.float32), seed_grad), 0.0
        )
        earlier_state = kept_list[max(tick_index - 1, 0)]
        later_state = kept_list[min(tick_index + 1, micro_count)]
        kept_state = jax.tree.map(
            lambda first_arr, second_arr: jnp.where(is_first, first_arr, second_arr),
            earlier_state,
            later_state,
        )
        grad_inputs, weight_grads = layer_backward(
            grad_out, kept_state, weights, key_slots < length_now, cosine_table, sine_table
        )
        grad_low = grad_inputs.astype(jnp.bfloat16)
        input_grads.append(grad_low)
        if tick_index < micro_count:
            arriving = shifted(grad_low, "section", -1)
        totals = weight_grads if totals is None else jax.tree.map(jnp.add, totals, weight_grads)
    shares = (
        lax.psum_scatter(
            totals[0].astype(jnp.bfloat16), "fsdp", scatter_dimension=0, tiled=True
        ).astype(jnp.float32),
        lax.psum_scatter(
            totals[1].astype(jnp.bfloat16), "fsdp", scatter_dimension=0, tiled=True
        ).astype(jnp.float32),
        lax.psum_scatter(
            totals[2].astype(jnp.bfloat16), "fsdp", scatter_dimension=0, tiled=True
        ).astype(jnp.float32),
        lax.psum_scatter(
            totals[3].astype(jnp.bfloat16), "fsdp", scatter_dimension=0, tiled=True
        ).astype(jnp.float32),
        lax.psum_scatter(
            totals[4].astype(jnp.bfloat16), "fsdp", scatter_dimension=0, tiled=True
        ).astype(jnp.float32),
        lax.psum_scatter(
            totals[5].astype(jnp.bfloat16), "fsdp", scatter_dimension=0, tiled=True
        ).astype(jnp.float32),
        lax.psum_scatter(
            totals[6].astype(jnp.bfloat16), "fsdp", scatter_dimension=0, tiled=True
        ).astype(jnp.float32),
        lax.psum_scatter(
            totals[7].astype(jnp.bfloat16), "fsdp", scatter_dimension=0, tiled=True
        ).astype(jnp.float32),
        lax.psum_scatter(
            totals[8].astype(jnp.bfloat16), "fsdp", scatter_dimension=0, tiled=True
        ).astype(jnp.float32),
    )
    owned_total = (
        lax.psum(shares[0].astype(jnp.bfloat16), "rep").astype(jnp.float32),
        lax.psum(shares[1].astype(jnp.bfloat16), "rep").astype(jnp.float32),
        lax.psum(shares[2].astype(jnp.bfloat16), "rep").astype(jnp.float32),
        lax.psum(shares[3].astype(jnp.bfloat16), "rep").astype(jnp.float32),
        lax.psum(shares[4].astype(jnp.bfloat16), "rep").astype(jnp.float32),
        lax.psum(shares[5].astype(jnp.bfloat16), "rep").astype(jnp.float32),
        lax.psum(shares[6].astype(jnp.bfloat16), "rep").astype(jnp.float32),
        lax.psum(shares[7].astype(jnp.bfloat16), "rep").astype(jnp.float32),
        lax.psum(shares[8].astype(jnp.bfloat16), "rep").astype(jnp.float32),
    )
    outgoing = jnp.where(is_first, input_grads[2], layer_outputs[1])
    returned = partner(outgoing, "section", 0)
    output_rows = jnp.where(is_first, returned, layer_outputs[2])
    grad_rows = jnp.where(is_first, input_grads[1], returned)
    return (
        output_rows[None, None],
        grad_rows[None, None],
        owned_total[0][None],
        owned_total[1][None],
        owned_total[2][None],
        owned_total[3][None],
        owned_total[4][None],
        owned_total[5][None],
        owned_total[6][None],
        owned_total[7][None],
        owned_total[8][None],
    )


MESH = pl.DeviceIdType.MESH
BLOCK = 128
LANES = 128
QKV_PAD = 640
NORM_ROW = 64


def dot(left, right):
    return jnp.dot(left, right, preferred_element_type=jnp.float32)


def dot_rows(left, right):
    return lax.dot_general(left, right, (((1,), (1,)), ((), ())), preferred_element_type=jnp.float32)


def dot_cols(left, right):
    return lax.dot_general(left, right, (((0,), (0,)), ((), ())), preferred_element_type=jnp.float32)


def low(value):
    return value.astype(jnp.bfloat16)


def wide(value):
    return value.astype(jnp.float32)


def wait_for(ref, sem):
    pltpu.make_async_copy(ref, ref, sem).wait()


def turned(values):
    lane = lax.broadcasted_iota(jnp.int32, values.shape, 1)
    ahead = pltpu.roll(values, LANES - HEAD_DIM // 2, 1)
    behind = pltpu.roll(values, HEAD_DIM // 2, 1)
    return jnp.where(lane % HEAD_DIM < HEAD_DIM // 2, ahead, behind)


def relay_scratch(width, hidden):
    vm = pltpu.VMEM
    bf, f32 = jnp.bfloat16, jnp.float32
    slots = 4 * BLOCK
    own = 2 * BLOCK
    dma = pltpu.SemaphoreType.DMA
    part = width // 4
    share = part // 4
    fpart = hidden // 4
    fshare = fpart // 4
    return dict(
        wq=vm((2, width, QKV_PAD), bf), wo=vm((2, 256, width), bf), wgu=vm((2, width, 2 * fpart), bf),
        wd=vm((2, fpart, width), bf),
        x=vm((2, slots, width), bf), hid=vm((2, slots, width), bf), dfed=vm((2, slots, width), bf),
        datt=vm((2, slots, width), bf),
        q=vm((2, 3, slots, LANES), bf), k=vm((2, 3, slots, LANES), bf), v=vm((2, slots, 256), bf),
        pr=vm((2, 3, slots, slots), bf), mix=vm((2, slots, 256), bf), gu=vm((2, slots, 2 * fpart), bf),
        act=vm((2, slots, fpart), bf),
        n1=vm((2, own, width), f32), n2=vm((2, own, width), f32),
        i1=vm((2, own, LANES), f32), i2=vm((2, own, LANES), f32),
        dgu=vm((slots, 2 * fpart), bf), dmix=vm((slots, 256), bf), dqkv=vm((slots, QKV_PAD), bf),
        ds=vm((slots, slots), bf), dq=vm((slots, LANES), f32),
        hidf=vm((own, width), f32), dres=vm((own, width), f32), dy=vm((own, width), f32),
        part=vm((2, own, width), f32), cot=vm((own, width), bf), outb=vm((own, width), bf), tgb=vm((own, width), bf),
        sa=vm((2, 2, BLOCK, width), bf), ra=vm((2, 2, BLOCK, width), bf),
        sb=vm((2, 2, BLOCK, width), bf), rb=vm((2, 2, BLOCK, width), bf),
        par=vm((2, LANES, width), f32), ng=vm((2, LANES, width), f32),
        r1q=vm((2, 3, part, QKV_PAD), bf), r1g=vm((2, 3, part, 2 * fpart), bf),
        r1o=vm((2, 3, share, width), bf), r1d=vm((2, 3, fshare, width), bf),
        s2q=vm((2, part, QKV_PAD), bf), s2g=vm((2, part, 2 * fpart), bf),
        s2o=vm((2, share, width), bf), s2d=vm((2, fshare, width), bf),
        r2q=vm((8, share, QKV_PAD), bf), r2g=vm((8, share, 2 * fpart), bf),
        r2o=vm((2, share, width), bf), r2d=vm((2, fshare, width), bf),
        qraw=vm((part, 3 * width), bf), qpk=vm((4, part, QKV_PAD), bf), aux=vm((LANES, part), f32), raw=dma,
        s3q=vm((share, 3 * width + LANES), bf), s3g=vm((share, 2 * hidden), bf),
        cos=vm((slots, LANES), f32), sin=vm((slots, LANES), f32),
        s3o=vm((share, width), bf), s3d=vm((fshare, width), bf),
        tok_s=dma((1,)), tok_r=dma, cot_s=dma((1,)), cot_r=dma, xc_s=dma((2,)), xc_r=dma((2,)), tz_s=dma((2,)), tz_r=dma((2,)),
        wz=dma((2, 4, 4)), wss=dma((2, 2)), wso=dma((2, 2, 2)), wfs=dma((2, 4)), wrs=dma((2, 4)), wpx=dma((2, 4, 3)), wpy=dma((2, 4, 3)), wpd=dma((2, 4)),
        a_s=dma((2, 2)), a_r=dma((2, 2)), b_s=dma((2, 2)), b_r=dma((2, 2)), c_s=dma((8, 2)), c_r=dma((8, 2)),
        s1s=dma((2, 4)), s1a=dma((2, 4)), s1b=dma((2, 4)), s1t=dma((2, 4)), s1r=dma((2, 4)),
        s2s=dma((2, 4)), s2r=dma((4,)),
        s3s=dma((4, 2)), s3x=dma((4,)), s3y=dma((4,)), s3l=dma((4,)), s3t=dma((4,)), s3e=dma((4,)),
        o_s=dma((2,)), o_r=dma((2,)),
    )


def relay_kernel(names, length_ref, g1_ref, b1_ref, g2_ref, b2_ref, tok_ref, cot_ref, wq_ref, wo_ref, wg_ref, wu_ref, wd_ref,
                 out_ref, tg_ref, oq_ref, on_ref, oo_ref, og_ref, ou_ref, od_ref, *scratch):
    m = types.SimpleNamespace(**dict(zip(names, scratch)))
    width = tok_ref.shape[3]
    slots = 4 * BLOCK
    part = width // 4
    share = part // 4
    fpart = wd_ref.shape[1]
    fshare = fpart // 4
    s, z, r = lax.axis_index("section"), lax.axis_index("fsdp"), lax.axis_index("rep")
    zp, zh = z % 2, z // 2
    r0, r1 = r % 2, r // 2
    t = 2 * zp + s
    other = 1 - s

    def mixed(low_bit, high_bit, k):
        a = 1 - low_bit if k & 1 else low_bit
        b = 1 - high_bit if k & 2 else high_bit
        return a + 2 * b

    z_of = [mixed(zp, zh, k) for k in range(4)]
    r_of = [mixed(r0, r1, k) for k in range(4)]
    zp_of = [zp, 1 - zp, zp, 1 - zp]
    across = (other, z, r)
    along = (s, z_of[1], r)

    def remote(src, dst, send, recv, device):
        return pltpu.make_async_remote_copy(
            src_ref=src, dst_ref=dst, send_sem=send, recv_sem=recv, device_id=device, device_id_type=MESH)

    def rows(start, size):
        return pl.ds(pl.multiple_of(start, 16), size)

    barrier = pltpu.get_barrier_semaphore()
    greeted = [(other, z_of[0], r)] + [(c, z_of[k], r) for k in (1, 2, 3) for c in (0, 1)]
    greeted += [(s, z, r_of[k]) for k in (1, 2, 3)]
    for device in greeted:
        pl.semaphore_signal(barrier, inc=1, device_id=device, device_id_type=MESH)
    pl.semaphore_wait(barrier, len(greeted))

    home = (zp, 2 * s + zh, r)
    at_home = (zp == s) & (2 * s + zh == z)

    def scatter_rows(src, dst, send, recv, step):
        @pl.when(at_home)
        def _():
            if step == "start":
                pltpu.make_async_copy(src, dst, recv).start()

        @pl.when(jnp.logical_not(at_home))
        def _():
            copy = remote(src, dst, send.at[0], recv, home)
            if step == "start":
                copy.start()
            else:
                copy.wait_send()

    near_block, far_block = rows(t * BLOCK, BLOCK), rows((2 * (1 - zp) + s) * BLOCK, BLOCK)
    tok_args = (tok_ref.at[0, 0], m.x.at[0, rows(z * BLOCK, BLOCK)], m.tok_s, m.tok_r)
    cot_args = (cot_ref.at[0, 0], m.cot.at[rows(zh * BLOCK, BLOCK)], m.cot_s, m.cot_r)

    Q, G, O, D = range(4)
    weight = [m.wq, m.wgu, m.wo, m.wd]
    count = [share, share, share, fshare]
    pieces = 3

    def source_fan(l, kind):
        for k in range(4):
            size = part if k == 0 else share
            start = 0 if k == 0 else r * share
            here = rows(z * part + start, size)
            for c in range(2):
                target = 2 * zp_of[k] + c
                device = (c, z_of[k], r)
                if kind == Q:
                    pairs = [(m.qpk.at[target, rows(start, size)], m.wq.at[l, here])]
                else:
                    cols = pl.ds(pl.multiple_of(target * fpart, LANES), fpart)
                    pairs = [
                        (wg_ref.at[0, rows(start, size), cols], m.wgu.at[l, here, pl.ds(0, fpart)]),
                        (wu_ref.at[0, rows(start, size), cols], m.wgu.at[l, here, pl.ds(fpart, fpart)]),
                    ]
                for src, dst in pairs:
                    if k == 0 and c == l:
                        pltpu.make_async_copy(src, dst, m.wz.at[l, kind, k]).start()
                    else:
                        remote(src, dst, m.wss.at[l, kind], m.wz.at[l, kind, k], device).start()

    def blocks_in(kind):
        return pieces if kind == D else 1

    def piece_rows(kind, b, rep):
        n = count[kind]
        size = n // blocks_in(kind)
        return rows(rep * n + b * size, size)

    def source_own(l, kind, step):
        ref = wo_ref if kind == O else wd_ref
        n = count[kind]
        for i in range(2):
            target = zh + 2 * i
            own = target == z

            def send(src, dst):
                copy = remote(src, dst, m.wso.at[l, kind - O, i], m.wz.at[l, kind, 3], (zp, target, r))
                if step == "start":
                    copy.start()
                else:
                    copy.wait_send()

            @pl.when(own & (zp == l))
            def _():
                if step == "start":
                    pltpu.make_async_copy(
                        ref.at[0], weight[kind].at[l, pl.ds(0, 4 * n)], m.wz.at[l, kind, 3]).start()

            @pl.when(own & (zp != l))
            def _():
                send(ref.at[0], weight[kind].at[l, pl.ds(0, 4 * n)])

            @pl.when(jnp.logical_not(own))
            def _():
                if step == "start":
                    for b in range(blocks_in(kind)):
                        part_rows = piece_rows(kind, b, r)
                        remote(
                            ref.at[0, part_rows], weight[kind].at[l, part_rows], m.wso.at[l, kind - O, i],
                            m.wz.at[l, kind, b], (zp, target, r)).start()
                else:
                    wait_for(weight[kind].at[l, pl.ds(0, n)], m.wso.at[l, kind - O, i])

    def source(l, kinds):
        @pl.when(s == l)
        def _():
            for kind in kinds:
                if kind in (Q, G):
                    source_fan(l, kind)
                else:
                    source_own(l, kind, "start")

    def source_done(l):
        @pl.when(s == l)
        def _():
            size = 6 * share + part
            wait_for(m.wq.at[l, pl.ds(0, size)], m.wss.at[l, Q])
            wait_for(m.wgu.at[l, pl.ds(0, size)], m.wss.at[l, G])
            source_own(l, O, "wait")
            source_own(l, D, "wait")

    xn, yn = (s, z, r_of[1]), (s, z, r_of[2])
    cut = [3 * LANES, fpart, width // 2, width // 2]

    def halves_of(kind, lanes):
        return pl.ds(0, cut[kind]), pl.ds(cut[kind], lanes - cut[kind])

    def block_rows(kind, k, rep):
        if kind in (Q, G):
            return rows(z_of[k] * part + rep * share, share)
        return piece_rows(kind, k - 1, rep)

    def pass_on(l, kind, k):
        block = weight[kind].at[l, block_rows(kind, k, r)]
        wait_for(block, m.wz.at[l, kind, k if kind in (Q, G) else k - 1])
        remote(block, block, m.wfs.at[l, kind], m.wpx.at[l, kind, k - 1], xn).start()
        remote(block, block, m.wfs.at[l, kind], m.wpy.at[l, kind, k - 1], yn).start()

    def pass_half(l, kind, k):
        first, second = halves_of(kind, weight[kind].shape[2])
        here = block_rows(kind, k, r_of[1])
        wait_for(weight[kind].at[l, here], m.wpx.at[l, kind, k - 1])
        half = weight[kind].at[l, here, first]
        remote(half, half, m.wrs.at[l, kind], m.wpd.at[l, kind], yn).start()
        here = block_rows(kind, k, r_of[2])
        wait_for(weight[kind].at[l, here], m.wpy.at[l, kind, k - 1])
        half = weight[kind].at[l, here, second]
        remote(half, half, m.wrs.at[l, kind], m.wpd.at[l, kind], xn).start()

    def need(l, kind):
        n = count[kind]
        if kind in (Q, G):
            wait_for(weight[kind].at[l, rows(z * part, part)], m.wz.at[l, kind, 0])
            wait_for(weight[kind].at[l, pl.ds(0, 3 * n)], m.wpd.at[l, kind])
        else:
            @pl.when(t != z)
            def _():
                wait_for(weight[kind].at[l, pl.ds(0, n)], m.wpd.at[l, kind])

            @pl.when(t == z)
            def _():
                wait_for(weight[kind].at[l, pl.ds(0, 4 * n)], m.wz.at[l, kind, 3])

    def forward_done(l, kind):
        n = count[kind]

        def wait(blocks):
            wait_for(weight[kind].at[l, pl.ds(0, 2 * blocks * n)], m.wfs.at[l, kind])
            wait_for(weight[kind].at[l, pl.ds(0, blocks * n)], m.wrs.at[l, kind])

        if kind in (Q, G):
            wait(3)
        else:
            pl.when(t != z)(lambda: wait(1))

    def own_rows(j):
        return rows((2 * j + s) * BLOCK, BLOCK)

    def chunk(j):
        return pl.ds(2 * j * BLOCK, 2 * BLOCK)

    def kept(j):
        return pl.ds(j * BLOCK, BLOCK)

    def send_partial(e, j, left, right, multiply):
        p = e % 2
        m.part[j] = multiply(left[chunk(j)], right)
        m.sa[p, j] = low(m.part[j, rows(other * BLOCK, BLOCK)])
        copy = remote(m.sa.at[p, j], m.ra.at[p, j], m.a_s.at[p, j], m.a_r.at[p, j], across)
        copy.start()
        return copy

    def send_sum(e, j, copy):
        p = e % 2
        copy.wait()
        m.sb[p, j] = low(m.part[j, rows(s * BLOCK, BLOCK)] + wide(m.ra[p, j]))
        copy = remote(m.sb.at[p, j], m.rb.at[p, j], m.b_s.at[p, j], m.b_r.at[p, j], along)
        copy.start()
        return copy

    def summed(e, j, copy):
        p = e % 2
        copy.wait()
        return wide(m.sb[p, j]) + wide(m.rb[p, j])

    def share_rows(e, j, ref):
        block = ref.at[own_rows(j)]
        copy = remote(block, block, m.c_s.at[e, j], m.c_r.at[e, j], across)
        copy.start()
        return copy

    def lanes_of(size, width):
        return lax.broadcasted_iota(jnp.int32, (size, width), 1)

    pairs = 2 * BLOCK
    length = jnp.where(zh == 0, length_ref[0:1, 0:1], length_ref[1:2, 0:1])
    cos_ref, sin_ref = m.cos, m.sin
    live_keys = lanes_of(pairs, slots) < length
    scale = HEAD_DIM ** (-0.5)

    def make_tables():
        lane = lanes_of(slots, LANES) % (HEAD_DIM // 2)
        freq = jnp.exp(wide(lane) * (-2.0 / HEAD_DIM * math.log(1000.0)))
        angle = wide(lax.broadcasted_iota(jnp.int32, (slots, LANES), 0)) * freq
        sine = jnp.sin(angle)
        m.cos[...] = jnp.cos(angle)
        m.sin[...] = jnp.where(lanes_of(slots, LANES) % HEAD_DIM < HEAD_DIM // 2, -sine, sine)

    def param(l, i):
        return m.par[l, pl.ds(NORM_ROW + i, 1), :]

    def read_params(l):
        for i in range(width // LANES):
            cols = pl.ds(i * LANES, LANES)
            m.par[l, :, cols] = jnp.transpose(wide(m.wq[l, cols, pl.ds(QKV_PAD - LANES, LANES)]))

    def project(l, j):
        here = chunk(j)
        joined = dot(m.x[l, here], m.wq[l])
        cosine, sine = cos_ref[here], sin_ref[here]
        for h in range(3):
            values = joined[:, h * LANES:(h + 1) * LANES]
            values = values * cosine + turned(values) * sine
            m.q[l, h, here] = low(jnp.where(lanes_of(pairs, LANES) < HEAD_DIM, values, 0.0))
            m.k[l, h, here] = low(pltpu.roll(values, HEAD_DIM, 1))
        m.v[l, here] = low(jnp.where(lanes_of(pairs, 256) < 3 * HEAD_DIM, joined[:, 3 * LANES:], 0.0))

    def attend(l, j):
        here = chunk(j)
        total = jnp.zeros((pairs, 256), jnp.float32)
        for h in range(3):
            scores = dot_rows(m.q[l, h, here], m.k[l, h]) * scale
            scores = jnp.where(live_keys, scores, masked_score)
            top = jnp.max(scores, axis=-1, keepdims=True)
            weights = jnp.exp(scores - top)
            weights = low(weights * (1.0 / jnp.sum(weights, axis=-1, keepdims=True)))
            m.pr[l, h, here] = weights
            inside = lanes_of(pairs, 256) // HEAD_DIM == h
            total = jnp.where(inside, dot(weights, m.v[l]), total)
        m.mix[l, here] = low(total)

    def normed(values):
        centre = values - jnp.mean(values, axis=-1, keepdims=True)
        inverse = lax.rsqrt(jnp.mean(centre * centre, axis=-1, keepdims=True) + norm_eps)
        return centre * inverse, inverse

    def finish_attention(e, l, j, copy):
        values = wide(m.x[l, own_rows(j)]) + summed(e, j, copy)
        norm, inverse = normed(values)
        m.n1[l, kept(j)] = norm
        m.i1[l, kept(j)] = jnp.broadcast_to(inverse, (BLOCK, LANES))
        hidden = norm * param(l, 0) + param(l, 1)
        m.hidf[kept(j)] = hidden
        m.hid[l, own_rows(j)] = low(hidden)
        return share_rows(l, j, m.hid.at[l])

    def feed(l, j):
        here = chunk(j)
        rows_in = m.hid[l, here]
        gate = dot(rows_in, m.wgu[l, :, pl.ds(0, fpart)])
        up = dot(rows_in, m.wgu[l, :, pl.ds(fpart, fpart)])
        m.gu[l, here, pl.ds(0, fpart)] = low(gate)
        m.gu[l, here, pl.ds(fpart, fpart)] = low(up)
        m.act[l, here] = low(gate * jax.nn.sigmoid(gate) * up)

    def finish_feed(e, l, j, copy):
        values = m.hidf[kept(j)] + summed(e, j, copy)
        norm, inverse = normed(values)
        m.n2[l, kept(j)] = norm
        m.i2[l, kept(j)] = jnp.broadcast_to(inverse, (BLOCK, LANES))
        result = low(norm * param(l, 2) + param(l, 3))
        if l == 0:
            m.x[1, own_rows(j)] = result
            return share_rows(2, j, m.x.at[1])
        m.outb[kept(j)] = result
        return None

    counts = jnp.where(zp == 0, 1.0, 0.0)

    def add_norm_grads(l, i, dy, norm):
        for k, value in enumerate((dy * norm, dy)):
            at = pl.ds(NORM_ROW + i + k, 1)
            m.ng[l, at, :] += jnp.sum(value, axis=0, keepdims=True) * counts

    def norm_grad(dy, norm, inverse, gain):
        scaled = dy * gain
        return inverse * (
            scaled - jnp.mean(scaled, axis=-1, keepdims=True)
            - norm * jnp.mean(scaled * norm, axis=-1, keepdims=True))

    def back_second(l, j):
        dy = m.dy[kept(j)]
        norm = m.n2[l, kept(j)]
        add_norm_grads(l, 2, dy, norm)
        grad = norm_grad(dy, norm, m.i2[l, kept(j), pl.ds(0, 1)], param(l, 2))
        m.dres[kept(j)] = grad
        m.dfed[l, own_rows(j)] = low(grad)
        return share_rows(3 + l, j, m.dfed.at[l])

    def back_feed(l, j):
        here = chunk(j)
        dact = dot_rows(m.dfed[l, here], m.wd[l])
        gate = wide(m.gu[l, here, pl.ds(0, fpart)])
        up = wide(m.gu[l, here, pl.ds(fpart, fpart)])
        sig = jax.nn.sigmoid(gate)
        m.dgu[here, pl.ds(0, fpart)] = low(dact * up * sig * (1.0 + gate * (1.0 - sig)))
        m.dgu[here, pl.ds(fpart, fpart)] = low(dact * gate * sig)

    def back_first(e, l, j, copy):
        dhidden = m.dres[kept(j)] + summed(e, j, copy)
        norm = m.n1[l, kept(j)]
        add_norm_grads(l, 0, dhidden, norm)
        grad = norm_grad(dhidden, norm, m.i1[l, kept(j), pl.ds(0, 1)], param(l, 0))
        m.dres[kept(j)] = grad
        m.datt[l, own_rows(j)] = low(grad)
        return share_rows(5 + l, j, m.datt.at[l])

    def back_mix(l, j):
        m.dmix[chunk(j)] = low(dot_rows(m.datt[l, chunk(j)], m.wo[l]))

    def back_attend(l, h):
        @pl.loop(0, 2)
        def _(i):
            here = rows(i * pairs, pairs)
            grad = m.dmix[here]
            grad = jnp.where(lanes_of(pairs, 256) // HEAD_DIM == h, grad, jnp.zeros_like(grad))
            dprobs = dot_rows(grad, m.v[l])
            probs = wide(m.pr[l, h, here])
            centre = jnp.sum(dprobs * probs, axis=-1, keepdims=True)
            dscores = low(probs * (dprobs - centre))
            m.ds[here] = dscores
            m.dq[here] = dot(dscores, m.k[l, h]) * scale

        dkey = dot_cols(m.ds[...], m.q[l, h]) * scale
        values = jnp.where(lanes_of(slots, LANES) < HEAD_DIM, m.dq[...], pltpu.roll(dkey, HEAD_DIM, 1))
        values = values * cos_ref[...] - turned(values) * sin_ref[...]
        m.dqkv[:, pl.ds(h * LANES, LANES)] = low(values)
        dvalue = low(dot_cols(m.pr[l, h], m.dmix[...]))
        before = jnp.zeros_like(dvalue) if h == 0 else m.dqkv[:, pl.ds(3 * LANES, 256)]
        inside = lanes_of(slots, 256) // HEAD_DIM == h
        m.dqkv[:, pl.ds(3 * LANES, 256)] = jnp.where(inside, dvalue, before)

    def weight_grad(l, kind):
        left, right = (
            (m.x.at[l], m.dqkv), (m.hid.at[l], m.dgu), (m.mix.at[l], m.datt.at[l]),
            (m.act.at[l], m.dfed.at[l]),
        )[kind]

        @pl.loop(0, left.shape[1] // pairs)
        def _(i):
            cols = pl.ds(pl.multiple_of(i * pairs, pairs), pairs)
            grad = dot_cols(left[:, cols], right[...])
            if kind == Q:
                tail = grad[:, QKV_PAD - LANES:] + jnp.transpose(m.ng[l, :, cols])
                weight[kind][l, cols, pl.ds(0, QKV_PAD - LANES)] = low(grad[:, :QKV_PAD - LANES])
                weight[kind][l, cols, pl.ds(QKV_PAD - LANES, LANES)] = low(tail)
            else:
                weight[kind][l, cols] = low(grad)

    first_in = [m.r1q, m.r1g, m.r1o, m.r1d]
    second_out = [m.s2q, m.s2g, m.s2o, m.s2d]
    second_in = [m.r2q, m.r2g, m.r2o, m.r2d]
    third_out = [m.s3q, m.s3g, m.s3o, m.s3d]
    final = [(oq_ref, on_ref), (og_ref, ou_ref), (oo_ref,), (od_ref,)]

    def blocks_of(kind):
        return range(4 if kind in (Q, G) else 1)

    def grad_rows(kind, b, rep):
        n = count[kind]
        return rows((b * part if kind in (Q, G) else 0) + rep * n, n)

    def plane_first(l, kind):
        n = count[kind]
        first, second = halves_of(kind, weight[kind].shape[2])
        for b in blocks_of(kind):
            for slot, rep in ((1, r_of[3]), (0, None)):
                for lanes, device, near, sem in ((first, xn, r_of[1], m.s1a), (second, yn, r_of[2], m.s1b)):
                    block = grad_rows(kind, b, near if rep is None else rep)
                    remote(
                        weight[kind].at[l, block, lanes], first_in[kind].at[l, slot, pl.ds(b * n, n), lanes],
                        m.s1s.at[l, kind], sem.at[l, kind], device).start()

    def plane_second(l, kind):
        n = count[kind]
        first, second = halves_of(kind, weight[kind].shape[2])
        for lanes, device, rep, sem in ((first, yn, r_of[2], m.s1a), (second, xn, r_of[1], m.s1b)):
            wait_for(first_in[kind].at[l, pl.ds(0, 2), :, lanes], sem.at[l, kind])
            for b in blocks_of(kind):
                block = grad_rows(kind, b, rep)
                here = pl.ds(b * n, n)
                weight[kind][l, block, lanes] = low(
                    wide(weight[kind][l, block, lanes]) + wide(first_in[kind][l, 1, here, lanes]))
                remote(
                    weight[kind].at[l, block, lanes], first_in[kind].at[l, 2, here, lanes],
                    m.s1t.at[l, kind], m.s1r.at[l, kind], device).start()

    def spread_line(l, kind):
        n = count[kind]
        wait_for(first_in[kind].at[l, 2], m.s1r.at[l, kind])
        for b in blocks_of(kind):
            here = pl.ds(b * n, n)
            total = wide(weight[kind][l, grad_rows(kind, b, r)])
            total += wide(first_in[kind][l, 0, here]) + wide(first_in[kind][l, 2, here])
            second_out[kind][l, here] = low(total)
        if kind in (Q, G):
            slot = 2 * z + s
            for k in range(4):
                src = second_out[kind].at[l, rows(z_of[k] * n, n)]
                dst = second_in[kind].at[slot]
                if k == 0:
                    @pl.when(s == l)
                    def _():
                        pltpu.make_async_copy(src, dst, m.s2r.at[kind]).start()

                    @pl.when(s != l)
                    def _():
                        remote(src, dst, m.s2s.at[l, kind], m.s2r.at[kind], across).start()
                else:
                    remote(src, dst, m.s2s.at[l, kind], m.s2r.at[kind], (l, z_of[k], r)).start()
        else:
            src, dst = second_out[kind].at[l], second_in[kind].at[zh]
            is_self = (t == z) & (s == l)

            @pl.when(is_self)
            def _():
                pltpu.make_async_copy(src, dst, m.s2r.at[kind]).start()

            @pl.when(jnp.logical_not(is_self))
            def _():
                remote(src, dst, m.s2s.at[l, kind], m.s2r.at[kind], (l, t, r)).start()

    def line_done(l, kind):
        wait_for(first_in[kind].at[l, pl.ds(0, 2)], m.s1s.at[l, kind])
        wait_for(first_in[kind].at[l, 2], m.s1t.at[l, kind])
        n = count[kind]
        if kind in (Q, G):
            @pl.when(s == l)
            def _():
                wait_for(second_out[kind].at[l, pl.ds(0, 3 * n)], m.s2s.at[l, kind])

            @pl.when(s != l)
            def _():
                wait_for(second_out[kind].at[l], m.s2s.at[l, kind])
        else:
            @pl.when(jnp.logical_not((t == z) & (s == l)))
            def _():
                wait_for(second_out[kind].at[l], m.s2s.at[l, kind])

    def in_order(parts):
        low_half = lax.broadcasted_iota(jnp.int32, (share, LANES), 1) < HEAD_DIM

        def swapped(values):
            return pltpu.roll(values, HEAD_DIM, 1)

        def pair(head):
            return parts[head // 3][:, head % 3 * LANES:(head % 3 + 1) * LANES]

        def value(head, at_low):
            h = head % 3
            start = 3 * LANES + h // 2 * LANES
            values = parts[head // 3][:, start:start + LANES]
            return values if (h != 1) == at_low else swapped(values)

        for c in range(HEADS // 2):
            even, odd = pair(2 * c), pair(2 * c + 1)
            for i, values in enumerate((
                jnp.where(low_half, even, swapped(odd)), jnp.where(low_half, swapped(even), odd),
                jnp.where(low_half, value(2 * c, True), value(2 * c + 1, False)),
            )):
                m.s3q[:, pl.ds(i * width + c * LANES, LANES)] = low(values)
        norms = sum(values[:, QKV_PAD - LANES:] for values in parts)
        m.s3q[:, pl.ds(3 * width, LANES)] = low(norms)

    def out_halves(kind):
        if kind == G:
            return [(og_ref, pl.ds(0, og_ref.shape[1]))], [(ou_ref, pl.ds(0, ou_ref.shape[1]))]
        ref = final[kind][0]
        middle = ref.shape[1] // 2
        first, second = [(ref, pl.ds(0, middle))], [(ref, pl.ds(middle, middle))]
        return first, second + [(on_ref, pl.ds(0, LANES))] if kind == Q else second

    def finish(kind):
        wait_for(second_in[kind], m.s2r.at[kind])
        if kind in (Q, G):
            parts = []
            for b in range(4):
                near = 2 * (b // 2) + b % 2
                parts.append(wide(second_in[kind][near]) + wide(second_in[kind][near + 4]))
                if kind == G:
                    for i in range(2):
                        m.s3g[:, pl.ds((4 * i + b) * fpart, fpart)] = low(parts[b][:, i * fpart:(i + 1) * fpart])
            if kind == Q:
                in_order(parts)
        else:
            third_out[kind][...] = low(wide(second_in[kind][0]) + wide(second_in[kind][1]))
        here = rows(r * count[kind], count[kind])
        start = 0
        for ref in final[kind]:
            src, dst = third_out[kind].at[:, pl.ds(start, ref.shape[1])], ref.at[here]
            start += ref.shape[1]
            remote(src, dst, m.s3s.at[kind, 0], m.s3x.at[kind], xn).start()
            remote(src, dst, m.s3s.at[kind, 1], m.s3y.at[kind], yn).start()
            pltpu.make_async_copy(src, dst, m.s3l.at[kind]).start()

    def finish_half(kind):
        n = count[kind]
        for parts, rep, device, sem in zip(out_halves(kind), r_of[1:3], (yn, xn), (m.s3x, m.s3y)):
            wait_for(third_out[kind], sem.at[kind])
            for ref, lanes in parts:
                half = ref.at[rows(rep * n, n), lanes]
                remote(half, half, m.s3t.at[kind], m.s3e.at[kind], device).start()

    def finish_done(kind):
        block = third_out[kind]
        wait_for(block, m.s3l.at[kind])
        wait_for(block, m.s3e.at[kind])
        wait_for(third_out[kind], m.s3s.at[kind, 0])
        wait_for(third_out[kind], m.s3s.at[kind, 1])
        wait_for(block, m.s3t.at[kind])

    def send_rows(i, src, dst, step):
        block = src.at[rows(zp * BLOCK, BLOCK)]
        is_self = (zh == s) & (t == z)

        @pl.when(is_self)
        def _():
            if step == "start":
                pltpu.make_async_copy(block, dst, m.o_r.at[i]).start()

        @pl.when(jnp.logical_not(is_self))
        def _():
            copy = remote(block, dst, m.o_s.at[i], m.o_r.at[i], (zh, t, r))
            if step == "start":
                copy.start()
            else:
                copy.wait_send()

        if step == "wait":
            wait_for(dst, m.o_r.at[i])

    raw_copy = pltpu.make_async_copy(wq_ref.at[0], m.qraw, m.raw)

    def pack_weights():
        raw_copy.wait()
        low_half = lanes_of(part, LANES) < HEAD_DIM

        def column(i, head, at_low):
            values = wide(m.qraw[:, pl.ds(i * width + head // 2 * LANES, LANES)])
            return values if (head % 2 == 0) == at_low else pltpu.roll(values, HEAD_DIM, 1)

        m.aux[...] = jnp.zeros(m.aux.shape, jnp.float32)
        for i, ref in enumerate((g1_ref, b1_ref, g2_ref, b2_ref)):
            m.aux[pl.ds(NORM_ROW + i, 1)] = wide(ref[...])
        norms = jnp.transpose(m.aux[...])
        for c in range(4):
            heads = [3 * c + h for h in range(3)]
            for h, head in enumerate(heads):
                m.qpk[c, :, pl.ds(h * LANES, LANES)] = low(
                    jnp.where(low_half, column(0, head, True), column(1, head, False)))
            m.qpk[c, :, pl.ds(3 * LANES, LANES)] = low(
                jnp.where(low_half, column(2, heads[0], True), column(2, heads[1], False)))
            m.qpk[c, :, pl.ds(4 * LANES, LANES)] = low(jnp.where(low_half, column(2, heads[2], True), norms))

    def where_moved(kind, step):
        if kind in (Q, G):
            step()
        else:
            pl.when(t != z)(step)

    def on(l, kind, k):
        where_moved(kind, lambda: pass_on(l, kind, k))

    def half(l, kind, k):
        where_moved(kind, lambda: pass_half(l, kind, k))

    near, far = m.x.at[0, near_block], m.x.at[0, far_block]
    near_along = remote(near, near, m.tz_s.at[0], m.tz_r.at[0], along)
    near_across = remote(near, near, m.xc_s.at[0], m.xc_r.at[0], across)
    far_across = remote(far, far, m.xc_s.at[1], m.xc_r.at[1], across)
    cot_block = m.cot.at[rows(zp * BLOCK, BLOCK)]
    cot_along = remote(cot_block, cot_block, m.tz_s.at[1], m.tz_r.at[1], along)

    def share_tokens_near():
        wait_for(near, m.tok_r)
        near_along.start()
        near_across.start()

    def share_tokens_far():
        near_along.wait_send()
        wait_for(far, m.tz_r.at[0])
        far_across.start()

    def tokens_shared():
        near_across.wait()
        far_across.wait()

    def cotangent_along():
        wait_for(cot_block, m.cot_r)
        cot_along.start()

    def forward_end():
        send_rows(0, m.outb, out_ref.at[0, 0], "start")
        for l in range(2):
            source_done(l)
            for kind in (Q, O, G, D):
                forward_done(l, kind)
        cot_along.wait_send()
        wait_for(m.cot.at[rows((1 - zp) * BLOCK, BLOCK)], m.tz_r.at[1])
        for j in range(2):
            slot = (2 * j + s) * BLOCK + lax.broadcasted_iota(jnp.int32, (BLOCK, width), 0)
            m.dy[kept(j)] = jnp.where(slot < length, wide(m.cot[kept(j)]), 0.0)

    def layer_done(l, j, copy):
        result = low(m.dres[kept(j)] + summed(5 if l == 1 else 7, j, copy))
        if l == 1:
            m.dy[kept(j)] = wide(result)
        else:
            m.tgb[kept(j)] = result

    def finish_on(l, kind):
        pl.when(s == l)(lambda: finish(kind))

    def half_on(l, kind):
        pl.when(s == l)(lambda: finish_half(kind))

    def all_done():
        for kind in (D, G, O, Q):
            finish_done(kind)
            for l in (1, 0):
                line_done(l, kind)
        scatter_rows(*tok_args, "wait")
        scatter_rows(*cot_args, "wait")
        send_rows(0, m.outb, out_ref.at[0, 0], "wait")
        send_rows(1, m.tgb, tg_ref.at[0, 0], "wait")

    raw_copy.start()
    scatter_rows(*tok_args, "start")
    source(0, (O,))
    pack_weights()
    source(0, (Q,))
    for l in range(2):
        m.wo[l, pl.ds(part, 256 - part)] = jnp.zeros((256 - part, width), jnp.bfloat16)
        m.ng[l] = jnp.zeros((LANES, width), jnp.float32)
    on(0, Q, 1)
    half(0, Q, 1)
    make_tables()
    on(0, O, 1)
    share_tokens_near()
    source(0, (G,))
    on(0, Q, 2)
    on(0, Q, 3)
    half(0, O, 1)
    half(0, Q, 3)
    half(0, Q, 2)
    share_tokens_far()
    on(0, G, 1)
    need(0, Q)
    source(0, (D,))
    read_params(0)
    tokens_shared()
    project(0, 0)
    project(0, 1)
    attend(0, 0)
    on(0, G, 2)
    need(0, O)
    a0 = send_partial(0, 0, m.mix.at[0], m.wo[0], dot)
    attend(0, 1)
    b0 = send_sum(0, 0, a0)
    a1 = send_partial(0, 1, m.mix.at[0], m.wo[0], dot)
    b1 = send_sum(0, 1, a1)
    on(0, G, 3)
    half(0, G, 1)
    source(1, (O,))
    source(1, (Q,))
    source(1, (G,))
    half(0, G, 2)
    half(0, G, 3)
    on(0, D, 2)
    on(0, D, 3)
    c0 = finish_attention(0, 0, 0, b0)
    need(0, G)
    on(0, D, 1)
    half(0, D, 3)
    half(0, D, 1)
    on(1, Q, 1)
    c0.wait()
    on(1, Q, 3)
    feed(0, 0)
    half(0, D, 2)
    c1 = finish_attention(0, 0, 1, b1)
    on(1, Q, 2)
    need(0, D)
    a0 = send_partial(1, 0, m.act.at[0], m.wd[0], dot)
    on(1, G, 1)
    c1.wait()
    on(1, O, 1)
    half(1, Q, 1)
    b0 = send_sum(1, 0, a0)
    feed(0, 1)
    half(1, Q, 2)
    a1 = send_partial(1, 1, m.act.at[0], m.wd[0], dot)
    half(1, G, 1)
    b1 = send_sum(1, 1, a1)
    source(1, (D,))
    half(1, Q, 3)
    half(1, O, 1)
    on(1, G, 2)
    need(1, Q)
    on(1, G, 3)
    read_params(1)
    c0 = finish_feed(1, 0, 0, b0)
    c1 = finish_feed(1, 0, 1, b1)
    c0.wait()
    project(1, 0)
    half(1, G, 2)
    scatter_rows(*cot_args, "start")
    c1.wait()
    on(1, D, 1)
    project(1, 1)
    attend(1, 0)
    need(1, O)
    a0 = send_partial(2, 0, m.mix.at[1], m.wo[1], dot)
    attend(1, 1)
    on(1, D, 2)
    b0 = send_sum(2, 0, a0)
    half(1, G, 3)
    a1 = send_partial(2, 1, m.mix.at[1], m.wo[1], dot)
    b1 = send_sum(2, 1, a1)
    on(1, D, 3)
    half(1, D, 1)
    cotangent_along()
    half(1, D, 2)
    c0 = finish_attention(2, 1, 0, b0)
    half(1, D, 3)
    need(1, G)
    c0.wait()
    feed(1, 0)
    c1 = finish_attention(2, 1, 1, b1)
    need(1, D)
    a0 = send_partial(3, 0, m.act.at[1], m.wd[1], dot)
    c1.wait()
    b0 = send_sum(3, 0, a0)
    feed(1, 1)
    a1 = send_partial(3, 1, m.act.at[1], m.wd[1], dot)
    b1 = send_sum(3, 1, a1)
    finish_feed(3, 1, 0, b0)
    finish_feed(3, 1, 1, b1)
    forward_end()
    c0 = back_second(1, 0)
    c1 = back_second(1, 1)
    c0.wait()
    back_feed(1, 0)
    a0 = send_partial(4, 0, m.dgu, m.wgu[1], dot_rows)
    c1.wait()
    back_feed(1, 1)
    b0 = send_sum(4, 0, a0)
    a1 = send_partial(4, 1, m.dgu, m.wgu[1], dot_rows)
    weight_grad(1, D)
    plane_first(1, D)
    b1 = send_sum(4, 1, a1)
    weight_grad(1, G)
    plane_first(1, G)
    c0 = back_first(4, 1, 0, b0)
    c1 = back_first(4, 1, 1, b1)
    c0.wait()
    back_mix(1, 0)
    c1.wait()
    back_mix(1, 1)
    back_attend(1, 0)
    back_attend(1, 1)
    back_attend(1, 2)
    a0 = send_partial(5, 0, m.dqkv, m.wq[1], dot_rows)
    a1 = send_partial(5, 1, m.dqkv, m.wq[1], dot_rows)
    b0 = send_sum(5, 0, a0)
    weight_grad(1, O)
    plane_first(1, O)
    plane_second(1, D)
    b1 = send_sum(5, 1, a1)
    weight_grad(1, Q)
    plane_first(1, Q)
    spread_line(1, D)
    layer_done(1, 0, b0)
    plane_second(1, G)
    layer_done(1, 1, b1)
    c0 = back_second(0, 0)
    c1 = back_second(0, 1)
    c0.wait()
    back_feed(0, 0)
    a0 = send_partial(6, 0, m.dgu, m.wgu[0], dot_rows)
    c1.wait()
    back_feed(0, 1)
    b0 = send_sum(6, 0, a0)
    a1 = send_partial(6, 1, m.dgu, m.wgu[0], dot_rows)
    weight_grad(0, D)
    plane_first(0, D)
    b1 = send_sum(6, 1, a1)
    weight_grad(0, G)
    spread_line(1, G)
    plane_first(0, G)
    c0 = back_first(6, 0, 0, b0)
    plane_second(1, O)
    plane_second(0, D)
    c1 = back_first(6, 0, 1, b1)
    c0.wait()
    back_mix(0, 0)
    c1.wait()
    back_mix(0, 1)
    back_attend(0, 0)
    back_attend(0, 1)
    back_attend(0, 2)
    a0 = send_partial(7, 0, m.dqkv, m.wq[0], dot_rows)
    plane_second(1, Q)
    a1 = send_partial(7, 1, m.dqkv, m.wq[0], dot_rows)
    b0 = send_sum(7, 0, a0)
    weight_grad(0, O)
    plane_first(0, O)
    b1 = send_sum(7, 1, a1)
    spread_line(1, O)
    finish_on(1, O)
    weight_grad(0, Q)
    plane_first(0, Q)
    spread_line(0, D)
    plane_second(0, G)
    finish_on(1, G)
    layer_done(0, 0, b0)
    spread_line(1, Q)
    layer_done(0, 1, b1)
    plane_second(0, Q)
    spread_line(0, G)
    plane_second(0, O)
    finish_on(1, D)
    send_rows(1, m.tgb, tg_ref.at[0, 0], "start")
    finish_on(0, G)
    finish_on(0, D)
    spread_line(0, O)
    spread_line(0, Q)
    finish_on(0, O)
    finish_on(1, Q)
    half_on(1, D)
    finish_on(0, Q)
    half_on(1, O)
    half_on(1, G)
    half_on(1, Q)
    half_on(0, G)
    half_on(0, O)
    half_on(0, D)
    half_on(0, Q)
    all_done()


def relay(tokens, lengths, cotangent, w_qkv, w_out, norm1_gain, norm1_bias, w_gate, w_up, w_down, norm2_gain, norm2_bias):
    bf = jnp.bfloat16
    part, width = w_qkv.shape[1], tokens.shape[3]
    hidden = w_gate.shape[2]
    scratch = relay_scratch(width, hidden)
    any_space = pl.BlockSpec(memory_space=pl.ANY)
    fpart = hidden // 4
    outs = pl.pallas_call(
        functools.partial(relay_kernel, tuple(scratch)),
        out_shape=(
            jax.ShapeDtypeStruct(tokens.shape, bf), jax.ShapeDtypeStruct(tokens.shape, bf),
            jax.ShapeDtypeStruct((part, 3 * width), bf), jax.ShapeDtypeStruct((part, LANES), bf),
            jax.ShapeDtypeStruct((part, width), bf),
            jax.ShapeDtypeStruct((part, hidden), bf), jax.ShapeDtypeStruct((part, hidden), bf),
            jax.ShapeDtypeStruct((fpart, width), bf),
        ),
        in_specs=[pl.BlockSpec(memory_space=pltpu.VMEM)] * 5 + [any_space] * 7,
        out_specs=[any_space] * 8,
        scratch_shapes=list(scratch.values()),
        compiler_params=pltpu.CompilerParams(
            collective_id=1, has_side_effects=True, vmem_limit_bytes=VMEM_LIMIT),
    )(lengths, norm1_gain, norm1_bias, norm2_gain, norm2_bias, tokens, cotangent, w_qkv, w_out, w_gate, w_up, w_down)
    output, token_grad, *grads = outs
    grad_q, norms, grad_out, grad_gate, grad_up, grad_down = (grad.astype(jnp.float32)[None] for grad in grads)
    norms = norms[:, :, NORM_ROW:NORM_ROW + 4]
    return (
        output, token_grad, grad_q, grad_out, norms[:, :, 0], norms[:, :, 1],
        grad_gate, grad_up, grad_down, norms[:, :, 2], norms[:, :, 3],
    )


def fits_relay(args):
    tokens, lengths, w_qkv, w_gate, w_down = args[0], args[1], args[3], args[7], args[9]
    axes = tuple(lax.axis_size(axis) for axis in ("section", "fsdp", "rep"))
    return (
        axes == (2, 4, 4)
        and tokens.shape == (1, 1, BLOCK, 768)
        and lengths.shape == (2, 1)
        and w_qkv.shape == (1, 192, 2304)
        and w_gate.shape == (1, 192, 3072)
        and w_down.shape == (1, 768, 768)
    )


def program(*args):
    return relay(*args) if fits_relay(args) else shards(*args)


def solution(mesh):
    return jax.shard_map(
        program,
        mesh=mesh,
        in_specs=(
            P("section", "rep", "fsdp", None),
            P(None, "rep"),
            P("section", "rep", "fsdp", None),
            P("section", "fsdp", None),
            P("section", "fsdp", None),
            P("section", "fsdp"),
            P("section", "fsdp"),
            P("section", "fsdp", None),
            P("section", "fsdp", None),
            P("section", "fsdp", None),
            P("section", "fsdp"),
            P("section", "fsdp"),
        ),
        out_specs=(
            P("section", "rep", "fsdp", None),
            P("section", "rep", "fsdp", None),
            P("section", "fsdp", None),
            P("section", "fsdp", None),
            P("section", "fsdp"),
            P("section", "fsdp"),
            P("section", "fsdp", None),
            P("section", "fsdp", None),
            P("section", "fsdp", None),
            P("section", "fsdp"),
            P("section", "fsdp"),
        ),
        check_vma=False,
    )
```
